128 devices in a mesh: ctx: 8 (over y, z_hi), shard: 16 (over x, z_lo, core).
Axes of the slice: x: 4, y: 4, z: 4 (z_hi: 2, z_lo: 2; z = z_hi * 2 + z_lo), core: 2. Of those that a mesh axis runs over, the one named last changes fastest.
Arguments:
- tokens: bfloat16 [16, 1024, 2048], P('shard', 'ctx'), may hold values from -6 to 6
- cotangent: bfloat16 [16, 1024, 2048], P('shard', 'ctx'), may hold values from -6 to 6
- lengths: int32 [16], P('shard'), may hold values from 512 to 1024, as said below
- routes: int32 [16, 1024, 4], P('shard', 'ctx'), may hold values from 0 to 5, all different within a row; in each aligned block of 128 rows (0 to 127, 128 to 255, ..., all dimensions but the last counted through in order) at most 112 rows name the same one
- block_order: int32 [16], replicated, may hold values from 0 to 15, as said below
- norm_gains: bfloat16 [2, 2048], P(None, 'shard'), may hold values from 0.5 to 1.5
- qkv_weight: bfloat16 [2048, 6144], P('shard'), may hold values from -0.125 to 0.125
- qkv_bias: bfloat16 [6144], P('shard'), may hold values from -3 to 3
- out_weight: bfloat16 [2048, 2048], P('shard'), may hold values from -0.5 to 0.5
- router: bfloat16 [2048, 6], P('shard'), may hold values from -0.0625 to 0.0625
- shared_gate: bfloat16 [2048], P('shard'), may hold values from -0.125 to 0.125
- ffn_in: bfloat16 [2048, 28160], P('shard'), may hold values from -0.125 to 0.125
- ffn_out: bfloat16 [2048, 14080], P('shard'), may hold values from -0.3125 to 0.3125
Outputs:
- output: bfloat16 [16, 1024, 2048], P('shard', 'ctx')
- input_grad: float32 [16, 1024, 2048], P('shard', 'ctx')
- grad_gains: float32 [2, 2048], P(None, 'shard')
- grad_qkv: float32 [2048, 6144], P('shard')
- grad_bias: float32 [6144], P('shard')
- grad_out: float32 [2048, 2048], P('shard')
- grad_router: float32 [2048, 6], P('shard')
- grad_shared_gate: float32 [2048], P('shard')
- grad_ffn_in: float32 [2048, 28160], P('shard')
- grad_ffn_out: float32 [2048, 14080], P('shard')
The draws below stay inside these ranges and needn't reach their ends.
Inputs may be any that keep to these rules, and one draw needn't show every extreme that they name: `lengths`: A row is valid when its position is below its sequence's length. `routes`: each token names 4 different experts; among the 128 rows held by one device (aligned blocks of rows) no expert is named by more than 112 tokens. `block_order`: A permutation of 0 to 15; entries 2c and 2c + 1 are some i and 15 - i in either order.
All inputs are finite; a program needn't handle non-finite values.
Results may differ from the reference program's by a relative error of at most 0.03.
Values may be sent and summed in bfloat16 or wider, within the bound.
A program may use at most 704 MiB of HBM per device.

```python
import math
import jax
import jax.numpy as jnp
import numpy as np
from jax import lax

D = 2048
HEADS = 16
HEAD = 128
HE = 1408
FS = 5632
TOPK = 4
EXPERTS = 6
SEQ_LEN = 1024
SEQS = 16
TOK_DEV = 128
BLOCK = 64
BLOCKS = 16
CAP = 112
FIN = 28160
FOUT = 14080


def draw_lengths(key, part):
    key = jax.random.fold_in(key, 5)
    first_key, second_key = jax.random.split(key)
    drawn = jax.random.randint(first_key, (SEQS,), SEQ_LEN // 2, SEQ_LEN + 1)
    order = jax.random.permutation(second_key, SEQS)
    drawn = drawn.at[order[0]].set(SEQ_LEN)
    drawn = drawn.at[order[1]].set(SEQ_LEN // 2)
    return drawn.astype(jnp.int32)


def draw_block_order(key, part):
    key = jax.random.fold_in(key, 9)
    first_key, second_key = jax.random.split(key)
    pairs = jax.random.permutation(first_key, BLOCKS // 2)
    flips = jax.random.randint(second_key, (BLOCKS // 2,), 0, 2)
    leading = jnp.where(flips == 1, BLOCKS - 1 - pairs, pairs)
    trailing = BLOCKS - 1 - leading
    return jnp.stack([leading, trailing], axis=1).reshape(BLOCKS).astype(jnp.int32)


def steps_of(key, extent, pieces, low, largest):
    level = 1.0
    for position, blocks in pieces:
        heights = jax.random.uniform(jax.random.fold_in(jax.random.fold_in(key, 6), position), (blocks,), jnp.float32, low / len(pieces), largest / len(pieces))
        level = level * jnp.repeat(jnp.exp(heights), extent[position] // blocks).reshape((-1,) + (1,) * (len(extent) - 1 - position))
    return level


def shared_out(stream_key, own, number, rows, amount, top, most, slope):
    ranking = jax.random.permutation(stream_key, amount)
    crowded, ordinary = shares(amount, rows * top, most, slope, True), shares(amount, rows * top, most, slope, False)
    places = jnp.arange(amount)

    def named(tallies, turn):
        used = int((tallies > 0).sum())
        fixed = max(1, used // 4)
        moved = fixed + (places - fixed + turn * (used - fixed)) % max(1, amount - fixed)
        return jnp.zeros((amount,), jnp.int32).at[ranking[jnp.where(places < fixed, places, moved)]].set(jnp.asarray(tallies, jnp.int32))

    tallies = jnp.where(number % 4 == 0, named(crowded, number // 4), named(ordinary, number - number // 4 - 1))
    mixed = jax.random.permutation(jax.random.fold_in(own, 3), amount)
    donor, sink = mixed[0:amount // 2 * 2:2], mixed[1:amount // 2 * 2:2]
    margin = jnp.minimum(tallies[donor] - 1, most - tallies[sink]) // 2
    margin = jnp.where((donor == ranking[0]) | (sink == ranking[0]) | (tallies[sink] == 0), 0, jnp.maximum(margin, 0))
    moved = jax.random.randint(jax.random.fold_in(own, 4), (amount // 2,), 0, 1 << 20) % (margin + 1)
    tallies = tallies.at[donor].add(-moved).at[sink].add(moved)
    labels = jnp.searchsorted(jnp.cumsum(tallies), jnp.arange(rows * top), side="right").astype(jnp.int32)
    grid = labels.reshape(top, rows).T
    grid = grid[jax.random.permutation(jax.random.fold_in(own, 1), rows)]
    turn = jax.random.randint(jax.random.fold_in(own, 2), (rows, 1), 0, top)
    return jnp.take_along_axis(grid, (jnp.arange(top)[None, :] + turn) % top, axis=1)


def shares(number_of, total, most, skew, full):
    portions = [(1 << 20) // math.isqrt(rank ** skew) + 1 for rank in range(1, number_of + 1)]
    largest = most if full else min(most, max(-(-total // number_of), total * portions[0] // sum(portions)))
    least = 1 if total - largest >= number_of - 1 else 0
    given, spare = [largest] + [least] * (number_of - 1), total - largest - least * (number_of - 1)
    while spare > 0:
        candidates = [i for i in range(1, number_of) if given[i] < largest] or [i for i in range(1, number_of) if given[i] < most]
        whole, left = sum([portions[i] for i in candidates]), spare
        for i in candidates:
            extra = min(most - given[i], max(1, left * portions[i] // whole), spare)
            given[i] = given[i] + extra
            spare = spare - extra
    return np.array(given)


def bell_draw(stream_key, dims, spread, reach, cuts=(), kind=jnp.bfloat16):
    entries = spread * jax.random.normal(stream_key, dims, jnp.float32)
    if cuts:
        entries = entries * steps_of(stream_key, dims, cuts, -0.22, 0.18)
    return jnp.clip(entries, -reach, reach).astype(kind)


def setup_inputs(seed: int = 0) -> dict:
    seeds = jax.random.split(jax.random.key(seed), 14)
    tokens = bell_draw(seeds[0], (SEQS, SEQ_LEN, D), 1.0, 6.0, ((0, 16), (1, 8)))
    cotangent = bell_draw(seeds[1], (SEQS, SEQ_LEN, D), 1.0, 6.0, ((0, 16), (1, 8)))
    lengths = draw_lengths(jax.random.fold_in(seeds[13], 71), 0)
    routes_keys = jax.random.split(jax.random.fold_in(seeds[3], 1), SEQS * SEQ_LEN // TOK_DEV)
    routes_turns = jax.random.permutation(jax.random.fold_in(seeds[3], 3), SEQS * SEQ_LEN // TOK_DEV)
    routes = jax.vmap(lambda own, number: shared_out(jax.random.fold_in(seeds[3], 2), own, number, TOK_DEV, EXPERTS, TOPK, CAP, 1))(routes_keys, routes_turns).reshape((SEQS, SEQ_LEN, TOPK))
    block_order = draw_block_order(jax.random.fold_in(seeds[13], 71), 0)
    norm_gains = jnp.clip(1.0 + 0.1 * jax.random.normal(seeds[5], (2, D), jnp.float32), 0.5, 1.5).astype(jnp.bfloat16)
    qkv_weight = bell_draw(seeds[6], (D, 3 * D), D ** -0.5, 0.125, ((0, 16),))
    qkv_bias = bell_draw(seeds[7], (3 * D,), 0.5, 3.0, ((0, 16),))
    out_weight = bell_draw(seeds[8], (D, D), (D // 16) ** -0.5, 0.5, ((0, 16),))
    router = bell_draw(seeds[9], (D, EXPERTS), (4 * D) ** -0.5, 0.0625, ((0, 16),))
    shared_gate = bell_draw(seeds[10], (D,), D ** -0.5, 0.125, ((0, 16),))
    ffn_in = bell_draw(seeds[11], (D, FIN), D ** -0.5, 0.125, ((0, 16),))
    ffn_out = bell_draw(seeds[12], (D, FOUT), (HE // 4) ** -0.5, 0.3125, ((0, 16),))
    return dict(tokens=tokens, cotangent=cotangent, lengths=lengths, routes=routes, block_order=block_order, norm_gains=norm_gains, qkv_weight=qkv_weight, qkv_bias=qkv_bias, out_weight=out_weight, router=router, shared_gate=shared_gate, ffn_in=ffn_in, ffn_out=ffn_out)


@jax.custom_vjp
def low(v):
    return lax.optimization_barrier(v.astype(jnp.bfloat16)).astype(jnp.float32)

@jax.custom_vjp
def low_back(v):
    return v

def low_keep(v):
    return (low(v), None)

def low_pass(kept, grad):
    return (grad,)

def back_keep(v):
    return (v, None)

def back_low(kept, grad):
    return (low(grad),)
low.defvjp(low_keep, low_pass)
low_back.defvjp(back_keep, back_low)
highest = lax.Precision.HIGHEST
epsilon = 1e-06
rope_base = 1000000.0

def product(left, right):
    return jnp.dot(left, right, precision=highest, preferred_element_type=jnp.float32)

def rope_tables(positions):
    half = HEAD // 2
    freqs = rope_base ** (-jnp.arange(half, dtype=jnp.float32) * 2.0 / HEAD)
    phase = positions.astype(jnp.float32)[:, None] * freqs[None, :]
    phase = jnp.concatenate([phase, phase], axis=1)
    return (jnp.cos(phase)[:, None, :], jnp.sin(phase)[:, None, :])

def rotate(values, cosines, sines):
    half = values.shape[-1] // 2
    turned = jnp.concatenate([-values[..., half:], values[..., :half]], axis=-1)
    return values * cosines + turned * sines

def normed(values, gain):
    return values * lax.rsqrt(lax.optimization_barrier(jnp.mean(values * values, axis=-1, keepdims=True)) + epsilon) * gain

def swiglu(hidden, weight_in, weight_out, width):
    gate_up = low_back(product(hidden, weight_in))
    active = low(jax.nn.silu(gate_up[:, :width]) * gate_up[:, width:])
    return low_back(product(active, weight_out.T))

def forward(inputs, norm_gains, qkv_weight, qkv_bias, out_weight, router, shared_gate, ffn_in, ffn_out, positions, valid, route_ids):
    length = inputs.shape[0]
    first = low(normed(inputs, norm_gains[0]))
    projected = low_back(product(first, qkv_weight) + qkv_bias)
    cosines, sines = rope_tables(positions)
    queries = low(rotate(projected[:, :D].reshape(length, HEADS, HEAD), cosines, sines))
    keyset = low(rotate(projected[:, D:2 * D].reshape(length, HEADS, HEAD), cosines, sines))
    valueset = low(projected[:, 2 * D:].reshape(length, HEADS, HEAD))
    scores = jnp.einsum('qhd,khd->hqk', queries, keyset, precision=highest) * HEAD ** (-0.5)
    scores = low_back(scores)
    allowed = (positions[None, :] <= positions[:, None]) & valid[None, :]
    scores = jnp.where(allowed[None], scores, -1e+30)
    probs = low(jax.nn.softmax(scores, axis=-1))
    mixed = jnp.einsum('hqk,khd->qhd', probs, valueset, precision=highest).reshape(length, D)
    mixed = low(low_back(mixed))
    attended = low_back(product(mixed, out_weight.T))
    residual = inputs + attended
    second = low(normed(residual, norm_gains[1]))
    logits = product(second, router)
    picked = (route_ids[:, :, None] == jnp.arange(EXPERTS, dtype=jnp.int32)[None, None, :]).astype(jnp.float32)
    chosen = lax.optimization_barrier(jnp.sum(logits[:, None, :] * picked, axis=-1))
    gates = jax.nn.softmax(chosen, axis=-1)
    weights = lax.optimization_barrier(jnp.sum(gates[:, :, None] * picked, axis=1))
    sigma = jax.nn.sigmoid(product(second, shared_gate))
    total = residual + sigma[:, None] * swiglu(second, ffn_in[:, :2 * FS], ffn_out[:, :FS], FS)
    for expert in range(EXPERTS):
        weight_in = ffn_in[:, 2 * FS + 2 * HE * expert:2 * FS + 2 * HE * (expert + 1)]
        weight_out = ffn_out[:, FS + HE * expert:FS + HE * (expert + 1)]
        total = total + weights[:, expert:expert + 1] * swiglu(second, weight_in, weight_out, HE)
    return total * valid[:, None].astype(jnp.float32)

def reference(tokens, cotangent, lengths, routes, block_order, norm_gains, qkv_weight, qkv_bias, out_weight, router, shared_gate, ffn_in, ffn_out):
    rows = jnp.arange(SEQ_LEN, dtype=jnp.int32)
    positions = (block_order[rows // BLOCK] * BLOCK + rows % BLOCK).astype(jnp.int32)
    params = tuple((p.astype(jnp.float32) for p in (norm_gains, qkv_weight, qkv_bias, out_weight, router, shared_gate, ffn_in, ffn_out)))

    def step(sums, item):
        inputs, grad_in, length, route_ids = item
        valid = positions < length

        def apply(values, *weights):
            return forward(values, *weights, positions, valid, route_ids)
        result, pullback = jax.vjp(apply, inputs.astype(jnp.float32), *params)
        grads = pullback(grad_in.astype(jnp.float32))
        sums = tuple((acc + grad for acc, grad in zip(sums, grads[1:])))
        return (sums, (result.astype(jnp.bfloat16), grads[0]))
    zeros = tuple((jnp.zeros(p.shape, jnp.float32) for p in params))
    sums, (output, input_grad) = lax.scan(step, zeros, (tokens, cotangent, lengths, routes))
    return (output, input_grad, sums[0], sums[1], sums[2], sums[3], sums[4], sums[5], sums[6], sums[7])
```

```python
import jax
import jax.numpy as jnp
import numpy as np
from jax import lax
from jax.sharding import PartitionSpec as P

D = 2048
HEAD = 128
HE = 1408
FS = 5632
EXPERTS = 6
FIN = 28160
FOUT = 14080
LANE = 128
SHARED_BLOCKS = FS // LANE
EXPERT_BLOCKS = HE // LANE
HIDDEN_BLOCKS = SHARED_BLOCKS + EXPERTS * EXPERT_BLOCKS

highest = lax.Precision.HIGHEST
epsilon = 1e-06
rope_base = 1000000.0


def contract_last(left, right):
    return lax.dot_general(
        left, right, (((1,), (1,)), ((), ())), preferred_element_type=jnp.float32
    )


def contract_first(left, right):
    return lax.dot_general(
        left, right, (((0,), (0,)), ((), ())), preferred_element_type=jnp.float32
    )


def dot(left, right):
    return jnp.dot(left, right, preferred_element_type=jnp.float32)


def rope_tables(positions):
    half = HEAD // 2
    freqs = rope_base ** (-jnp.arange(half, dtype=jnp.float32) * 2.0 / HEAD)
    phase = positions.astype(jnp.float32)[:, None] * freqs[None, :]
    phase = jnp.concatenate([phase, phase], axis=1)
    return (jnp.cos(phase)[:, None, :], jnp.sin(phase)[:, None, :])


def rotate(values, cosines, sines):
    half = values.shape[-1] // 2
    turned = jnp.concatenate([-values[..., half:], values[..., :half]], axis=-1)
    return values * cosines + turned * sines


def rotate_back(values, cosines, sines):
    half = values.shape[-1] // 2
    scaled = values * sines
    turned = jnp.concatenate([scaled[..., half:], -scaled[..., :half]], axis=-1)
    return values * cosines + turned


def normalize(values):
    factor = lax.rsqrt(jnp.mean(values * values, axis=-1, keepdims=True) + epsilon)
    return (values * factor, factor)


def norm_back(grad_normed, normalized, factor, gain):
    scaled = grad_normed * gain
    return factor * (scaled - normalized * jnp.mean(scaled * normalized, axis=-1, keepdims=True))


def gate_start(block):
    routed = block >= SHARED_BLOCKS
    expert = (block - SHARED_BLOCKS) // EXPERT_BLOCKS
    rest = (block - SHARED_BLOCKS) % EXPERT_BLOCKS
    start = jnp.where(routed, 2 * FS + 2 * HE * expert + LANE * rest, LANE * block)
    return start, jnp.where(routed, HE, FS)


def columns_at(array, starts):
    return jnp.concatenate(
        [lax.dynamic_slice_in_dim(array, start, LANE, axis=1) for start in starts], axis=1
    )


def ag_ctx(value):
    return lax.all_gather(value, "ctx", axis=0, tiled=True)


def rs_ctx(value):
    return lax.psum_scatter(value, "ctx", scatter_dimension=0, tiled=True)


def ag_shard(value):
    return lax.all_gather(value, "shard", axis=0, tiled=True)


def rs_shard(value):
    return lax.psum_scatter(value, "shard", scatter_dimension=0, tiled=True)


def local(
    tokens,
    cotangent,
    lengths,
    routes,
    block_order,
    norm_gains,
    qkv_weight,
    qkv_bias,
    out_weight,
    router,
    shared_gate,
    ffn_in,
    ffn_out,
):
    bf16, f32 = jnp.bfloat16, jnp.float32
    n_ctx = lax.axis_size("ctx")
    n_shard = lax.axis_size("shard")
    rows_dev = tokens.shape[1]
    seq_len = rows_dev * n_ctx
    n_blocks = block_order.shape[0]
    block = seq_len // n_blocks
    heads = D // HEAD // n_ctx
    width = heads * HEAD
    hidden_blocks = -(-HIDDEN_BLOCKS // n_ctx)
    hidden = hidden_blocks * LANE
    scale = HEAD ** (-0.5)
    place = lax.axis_index("ctx")
    owner = lax.axis_index("shard")

    every = jnp.arange(seq_len, dtype=jnp.int32)
    matches = (every // block)[:, None] == jnp.arange(n_blocks, dtype=jnp.int32)[None, :]
    pos = jnp.sum(jnp.where(matches, block_order[None, :], 0), axis=1) * block + every % block
    valid = pos < lengths[0]
    valid_rows = valid.astype(f32)[:, None]
    own_valid = lax.dynamic_slice_in_dim(valid_rows, place * rows_dev, rows_dev)

    inputs = tokens[0].astype(f32)
    picks = routes[0][:, :, None] == jnp.arange(EXPERTS, dtype=jnp.int32)[None, None, :]
    own_assigned = jnp.sum(picks.astype(f32), axis=1)
    x_all = ag_ctx(tokens[0])
    assigned = ag_ctx(own_assigned.astype(bf16)).astype(f32)

    small = jnp.concatenate(
        [
            norm_gains.reshape(-1),
            router.T.reshape(-1),
            shared_gate.reshape(-1),
            qkv_bias.reshape(-1),
        ]
    ).reshape(1, -1)
    small_all = ag_shard(small)
    gains = small_all[:, : 2 * LANE].reshape(n_shard, 2, LANE).transpose(1, 0, 2).reshape(2, D)
    first_gain, second_gain = gains[0].astype(f32), gains[1].astype(f32)
    logit_weights = (
        small_all[:, 2 * LANE : 9 * LANE]
        .reshape(n_shard, EXPERTS + 1, LANE)
        .transpose(0, 2, 1)
        .reshape(D, EXPERTS + 1)
    )
    bias = small_all[:, 9 * LANE :].reshape(3 * D)
    own_bias = jnp.concatenate(
        [lax.dynamic_slice_in_dim(bias, D * i + width * place, width) for i in range(3)]
    ).astype(f32)
    attn_weights = ag_shard(
        jnp.concatenate(
            [
                lax.dynamic_slice_in_dim(qkv_weight, D * i + width * place, width, axis=1)
                for i in range(3)
            ]
            + [lax.dynamic_slice_in_dim(out_weight, width * place, width, axis=1)],
            axis=1,
        )
    )
    w_qkv, w_out = attn_weights[:, : 3 * width], attn_weights[:, 3 * width :]
    blocks = [hidden_blocks * place + j for j in range(hidden_blocks)]
    safe = [jnp.minimum(b, HIDDEN_BLOCKS - 1) for b in blocks]
    starts = [gate_start(b) for b in safe]
    w_in = ag_shard(columns_at(ffn_in, [s for s, _ in starts] + [s + u for s, u in starts]))
    w_down = ag_shard(columns_at(ffn_out, [LANE * b for b in safe]))
    g_all = ag_ctx(cotangent[0])
    g_all = jnp.where(valid_rows > 0, g_all, 0).astype(bf16)

    first_normed_all, _ = normalize(x_all.astype(f32))
    first_all = (first_normed_all * first_gain).astype(bf16)
    projected = dot(first_all, w_qkv) + own_bias
    cosines, sines = rope_tables(pos)
    query = rotate(projected[:, :width].reshape(seq_len, heads, HEAD), cosines, sines).astype(bf16)
    key = rotate(
        projected[:, width : 2 * width].reshape(seq_len, heads, HEAD), cosines, sines
    ).astype(bf16)
    value = projected[:, 2 * width :].astype(bf16).reshape(seq_len, heads, HEAD)
    allowed = ((pos[None, :] <= pos[:, None]) & valid[None, :])[None]
    scores = jnp.einsum("qhd,khd->hqk", query, key, preferred_element_type=f32) * scale
    masked = jnp.where(allowed, scores, -1e30)
    peak = jnp.max(masked, axis=-1, keepdims=True)
    log_total = peak + jnp.log(jnp.sum(jnp.exp(masked - peak), axis=-1, keepdims=True))
    probs = jnp.exp(masked - log_total)
    probs_low = probs.astype(bf16)
    mixed = jnp.einsum("hqk,khd->qhd", probs_low, value, preferred_element_type=f32)
    mixed = mixed.reshape(seq_len, width).astype(bf16)
    attended = rs_ctx(contract_last(mixed, w_out).astype(bf16)).astype(f32)

    residual = inputs + attended
    second_normed, second_factor = normalize(residual)
    second = (second_normed * second_gain).astype(bf16)
    second_all = ag_ctx(second)

    logits = dot(second_all, logit_weights)
    chosen = jnp.where(assigned > 0, logits[:, :EXPERTS], -jnp.inf)
    raised = jnp.exp(chosen - jnp.max(chosen, axis=-1, keepdims=True))
    gates = raised / jnp.sum(raised, axis=-1, keepdims=True)
    sigma = jax.nn.sigmoid(logits[:, EXPERTS:])
    branch_weights = jnp.concatenate([gates, sigma], axis=1)
    block_ids = jnp.stack(blocks)
    branch_of = jnp.where(
        block_ids < SHARED_BLOCKS, EXPERTS, (block_ids - SHARED_BLOCKS) // EXPERT_BLOCKS
    )
    member = (
        (branch_of[None, :] == jnp.arange(EXPERTS + 1, dtype=jnp.int32)[:, None])
        & (block_ids < HIDDEN_BLOCKS)[None, :]
    ).astype(f32)
    block_weights = jnp.dot(branch_weights, member, precision=highest)
    spread = jnp.broadcast_to(block_weights[:, :, None], (seq_len, hidden_blocks, LANE))
    spread = spread.reshape(seq_len, hidden)

    gate = dot(second_all, w_in[:, :hidden])
    upward = dot(second_all, w_in[:, hidden:])
    squashed = jax.nn.sigmoid(gate)
    act = gate * squashed * upward
    act_low = (act * spread).astype(bf16)
    ffn = rs_ctx(contract_last(act_low, w_down).astype(bf16)).astype(f32)
    output = ((residual + ffn) * own_valid).astype(bf16)[None]
    grad_raw = dot(g_all, w_down)
    block_dots = jnp.sum((grad_raw * act).reshape(seq_len, hidden_blocks, LANE), axis=-1)
    branch_dots = rs_ctx(jnp.dot(block_dots, member.T, precision=highest))
    grad_act = grad_raw * spread
    grad_gate = grad_act * upward * squashed * (1.0 + gate * (1.0 - squashed))
    grad_up = grad_act * gate * squashed
    grad_gu = jnp.concatenate([grad_gate, grad_up], axis=1).astype(bf16)
    grad_second = rs_ctx(contract_last(grad_gu, w_in).astype(bf16)).astype(f32)

    own_weights = lax.dynamic_slice_in_dim(branch_weights, place * rows_dev, rows_dev)
    own_gates, own_sigma = own_weights[:, :EXPERTS], own_weights[:, EXPERTS:]
    dots = branch_dots[:, :EXPERTS]
    grad_logits = own_gates * (dots - jnp.sum(own_gates * dots, axis=-1, keepdims=True))
    grad_sigma = branch_dots[:, EXPERTS:] * own_sigma * (1.0 - own_sigma)
    grad_both = jnp.concatenate([grad_logits, grad_sigma], axis=1)
    grad_second = grad_second + lax.dot_general(
        grad_both,
        logit_weights.astype(f32),
        (((1,), (1,)), ((), ())),
        precision=highest,
        preferred_element_type=f32,
    )
    grad_second_gain = jnp.sum(grad_second * second_normed, axis=0)
    own_g = cotangent[0].astype(f32) * own_valid
    grad_residual = own_g + norm_back(grad_second, second_normed, second_factor, second_gain)
    grad_attended = ag_ctx(grad_residual.astype(bf16))

    ffn_share = jnp.concatenate(
        [
            contract_first(second_all, grad_gu).astype(bf16),
            contract_first(g_all, act_low).astype(bf16),
        ],
        axis=1,
    )
    ffn_grads = lax.all_gather(rs_shard(ffn_share), "ctx", axis=0)

    grad_mixed = dot(grad_attended, w_out).astype(bf16).reshape(seq_len, heads, HEAD)
    grad_probs = jnp.einsum("qhd,khd->hqk", grad_mixed, value, preferred_element_type=f32)
    centre = jnp.sum(probs * grad_probs, axis=-1, keepdims=True)
    grad_scores = (probs * (grad_probs - centre)).astype(bf16)
    grad_query = jnp.einsum("hqk,khd->qhd", grad_scores, key, preferred_element_type=f32) * scale
    grad_key = jnp.einsum("hqk,qhd->khd", grad_scores, query, preferred_element_type=f32) * scale
    grad_value = jnp.einsum("hqk,qhd->khd", probs_low, grad_mixed, preferred_element_type=f32)
    grad_projected = jnp.concatenate(
        [
            rotate_back(grad_query, cosines, sines).reshape(seq_len, width),
            rotate_back(grad_key, cosines, sines).reshape(seq_len, width),
            grad_value.reshape(seq_len, width),
        ],
        axis=1,
    ).astype(bf16)
    grad_first = rs_ctx(contract_last(grad_projected, w_qkv).astype(bf16)).astype(f32)
    first_normed, first_factor = normalize(inputs)
    grad_first_gain = jnp.sum(grad_first * first_normed, axis=0)
    input_grad = grad_residual + norm_back(grad_first, first_normed, first_factor, first_gain)
    attn_share = jnp.concatenate(
        [
            contract_first(first_all, grad_projected).astype(bf16),
            contract_first(grad_attended, mixed).astype(bf16),
        ],
        axis=1,
    )
    attn_grads = lax.all_gather(rs_shard(attn_share), "ctx", axis=0)

    grad_bias_own = jnp.sum(grad_projected.astype(f32), axis=0).reshape(3, width)
    grad_bias = lax.dynamic_update_slice(
        jnp.zeros((3, D), f32), grad_bias_own, (0, width * place)
    ).reshape(3 * D)
    second_full = second.astype(f32)
    grad_logit_weights = lax.dot_general(
        grad_both,
        second_full,
        (((0,), (0,)), ((), ())),
        precision=highest,
        preferred_element_type=f32,
    )
    small_grads = jnp.concatenate(
        [
            jnp.stack([grad_first_gain, grad_second_gain])
            .reshape(2, n_shard, LANE)
            .transpose(1, 0, 2)
            .reshape(n_shard, -1),
            grad_logit_weights.reshape(EXPERTS + 1, n_shard, LANE)
            .transpose(1, 0, 2)
            .reshape(n_shard, -1),
            grad_bias.reshape(n_shard, -1),
        ],
        axis=1,
    )
    small_sums = lax.psum(small_grads, ("ctx", "shard"))
    own_small = lax.dynamic_slice_in_dim(small_sums, owner, 1)[0]
    grad_gains = own_small[: 2 * LANE].reshape(2, LANE)
    grad_router = own_small[2 * LANE : 8 * LANE].reshape(EXPERTS, LANE).T
    grad_shared_gate = own_small[8 * LANE : 9 * LANE]
    grad_bias_out = own_small[9 * LANE :]

    grad_qkv = jnp.concatenate(
        [
            attn_grads[p, :, width * i : width * (i + 1)]
            for i in range(3)
            for p in range(n_ctx)
        ],
        axis=1,
    ).astype(f32)
    grad_out = jnp.concatenate(
        [attn_grads[p, :, 3 * width :] for p in range(n_ctx)], axis=1
    ).astype(f32)

    def piece(first, count, offset):
        parts = []
        while count:
            p, j = first // hidden_blocks, first % hidden_blocks
            take = min(count, hidden_blocks - j)
            start = offset + LANE * j
            parts.append(ffn_grads[p, :, start : start + LANE * take])
            first, count = first + take, count - take
        return parts

    spans = [(0, SHARED_BLOCKS)] + [
        (SHARED_BLOCKS + EXPERT_BLOCKS * e, EXPERT_BLOCKS) for e in range(EXPERTS)
    ]
    grad_ffn_in = jnp.concatenate(
        [part for f, n in spans for half in (0, hidden) for part in piece(f, n, half)], axis=1
    ).astype(f32)
    grad_ffn_out = jnp.concatenate(
        [part for f, n in spans for part in piece(f, n, 2 * hidden)], axis=1
    ).astype(f32)
    return (
        output,
        input_grad[None],
        grad_gains,
        grad_qkv,
        grad_bias_out,
        grad_out,
        grad_router,
        grad_shared_gate,
        grad_ffn_in,
        grad_ffn_out,
    )


def solution(mesh):
    placed = (
        P("shard", "ctx", None),
        P("shard", "ctx", None),
        P("shard"),
        P("shard", "ctx", None),
        P(),
        P(None, "shard"),
        P("shard", None),
        P("shard"),
        P("shard", None),
        P("shard", None),
        P("shard"),
        P("shard", None),
        P("shard", None),
    )
    return jax.shard_map(
        local,
        mesh=mesh,
        in_specs=placed,
        out_specs=(
            P("shard", "ctx", None),
            P("shard", "ctx", None),
            P(None, "shard"),
            P("shard", None),
            P("shard"),
            P("shard", None),
            P("shard", None),
            P("shard"),
            P("shard", None),
            P("shard", None),
        ),
        check_vma=False,
    )
```

```python
import jax
import jax.numpy as jnp
from jax import lax
from jax.experimental import pallas as pl
from jax.experimental.pallas import tpu as pltpu
from jax.sharding import PartitionSpec as P

D = 2048
HEAD = 128
HE = 1408
FS = 5632
EXPERTS = 6
FIN = 28160
FOUT = 14080
LANE = 128
SHARED_BLOCKS = FS // LANE
EXPERT_BLOCKS = HE // LANE
HIDDEN_BLOCKS = SHARED_BLOCKS + EXPERTS * EXPERT_BLOCKS

highest = lax.Precision.HIGHEST
epsilon = 1e-06
rope_base = 1000000.0


def contract_last(left, right):
    return lax.dot_general(
        left, right, (((1,), (1,)), ((), ())), preferred_element_type=jnp.float32
    )


def contract_first(left, right):
    return lax.dot_general(
        left, right, (((0,), (0,)), ((), ())), preferred_element_type=jnp.float32
    )


def dot(left, right):
    return jnp.dot(left, right, preferred_element_type=jnp.float32)


def rope_tables(positions):
    half = HEAD // 2
    freqs = rope_base ** (-jnp.arange(half, dtype=jnp.float32) * 2.0 / HEAD)
    phase = positions.astype(jnp.float32)[:, None] * freqs[None, :]
    phase = jnp.concatenate([phase, phase], axis=1)
    return (jnp.cos(phase)[:, None, :], jnp.sin(phase)[:, None, :])


def rotate(values, cosines, sines):
    half = values.shape[-1] // 2
    turned = jnp.concatenate([-values[..., half:], values[..., :half]], axis=-1)
    return values * cosines + turned * sines


def rotate_back(values, cosines, sines):
    half = values.shape[-1] // 2
    scaled = values * sines
    turned = jnp.concatenate([scaled[..., half:], -scaled[..., :half]], axis=-1)
    return values * cosines + turned


def normalize(values):
    factor = lax.rsqrt(jnp.mean(values * values, axis=-1, keepdims=True) + epsilon)
    return (values * factor, factor)


def norm_back(grad_normed, normalized, factor, gain):
    scaled = grad_normed * gain
    return factor * (scaled - normalized * jnp.mean(scaled * normalized, axis=-1, keepdims=True))


def gate_start(block):
    routed = block >= SHARED_BLOCKS
    expert = (block - SHARED_BLOCKS) // EXPERT_BLOCKS
    rest = (block - SHARED_BLOCKS) % EXPERT_BLOCKS
    start = jnp.where(routed, 2 * FS + 2 * HE * expert + LANE * rest, LANE * block)
    return start, jnp.where(routed, HE, FS)


def columns_at(array, starts):
    return jnp.concatenate(
        [lax.dynamic_slice_in_dim(array, start, LANE, axis=1) for start in starts], axis=1
    )


def ag_ctx(value):
    return lax.all_gather(value, "ctx", axis=0, tiled=True)


def ag_shard(value):
    return lax.all_gather(value, "shard", axis=0, tiled=True)


MESH = pl.DeviceIdType.MESH
ANY = pl.BlockSpec(memory_space=pl.ANY)
VMEM = pl.BlockSpec(memory_space=pltpu.VMEM)
N_CTX = 8
CHIPS = 8


def params(number, limit=None):
    return pltpu.CompilerParams(
        collective_id=number, has_side_effects=True, vmem_limit_bytes=limit
    )


def greet(peers):
    semaphore = pltpu.get_barrier_semaphore()
    for peer in peers:
        pl.semaphore_signal(semaphore, inc=1, device_id=peer, device_id_type=MESH)
    pl.semaphore_wait(semaphore, len(peers))


def remote(source, target, sends, arrivals, slot, peer):
    return pltpu.make_async_remote_copy(
        src_ref=source,
        dst_ref=target,
        send_sem=sends.at[slot],
        recv_sem=arrivals.at[slot],
        device_id=peer,
        device_id_type=MESH,
    )


def places_of(axis):
    me = lax.axis_index(axis)
    if axis == "ctx":
        peer = lambda place: {"ctx": place}
    else:
        core, me = lax.rem(me, 2), me // 2
        peer = lambda place: {"shard": 2 * place + core}
    other = me + 1 - 2 * lax.rem(me, 2)
    places = [[lax.rem(base + 2 * k, N_CTX) for k in (0, 1, 3, 2)] for base in (me, other)]
    return places, peer


def by_rows(rows, body):
    step = 16

    def run(i, carry):
        body(pl.ds(pl.multiple_of(i * step, step), step))
        return carry

    lax.fori_loop(0, rows // step, run, 0)


class Gather:
    SEMAPHORES = 9

    def __init__(self, own, out, sends, arrivals):
        self.own, self.out, self.sends, self.arrivals = own, out, sends, arrivals
        self.places, _ = places_of("ctx")
        (self.me, self.up, self.down, self.far), other = self.places
        self.other = other[0]
        self.half = out.shape[1] // 2
        self.started = []

    def _send(self, slot, source, target, place):
        def copy():
            return remote(source(), target(), self.sends, self.arrivals, slot, {"ctx": place})

        copy().start()
        self.started.append(copy)

    def _await(self, slot, ref):
        remote(ref, ref, self.sends, self.arrivals, slot, {"ctx": self.other}).wait_recv()

    def begin(self):
        for slot, place in ((0, self.other), (1, self.up), (2, self.down)):
            self._send(slot, lambda: self.own, lambda: self.out.at[self.me], place)

    def pass_other(self):
        def block():
            return self.out.at[self.other]

        self._await(0, block())
        self._send(3, block, block, self.up)
        self._send(4, block, block, self.down)

    def pass_ring(self, column):
        _, up, down, _ = self.places[column]
        first = 1 + 2 * column
        low, high = pl.ds(0, self.half), pl.ds(self.half, self.half)
        self._await(first, self.out.at[down])
        lower = lambda: self.out.at[down, low]
        self._send(5 + 2 * column, lower, lower, self.up)
        self._await(first + 1, self.out.at[up])
        upper = lambda: self.out.at[up, high]
        self._send(6 + 2 * column, upper, upper, self.down)

    def end(self):
        low, high = pl.ds(0, self.half), pl.ds(self.half, self.half)
        for column in range(2):
            far = self.places[column][3]
            self._await(5 + 2 * column, self.out.at[far, low])
            self._await(6 + 2 * column, self.out.at[far, high])
        for copy in self.started:
            copy().wait_send()


class Reduce:
    SEMAPHORES = 13

    @staticmethod
    def scratch(rows, width, across=2):
        return [
            pltpu.VMEM((4, rows // 2, width), jnp.bfloat16),
            pltpu.VMEM((4, rows, width), jnp.bfloat16),
            pltpu.VMEM((across, rows, width), jnp.bfloat16),
            pltpu.SemaphoreType.DMA((Reduce.SEMAPHORES,)),
            pltpu.SemaphoreType.DMA((Reduce.SEMAPHORES,)),
        ]

    def __init__(self, parts, held, passing, near, across, sends, arrivals, axis="ctx"):
        self.parts, self.held = parts, held
        self.passing, self.near, self.across = passing, near, across
        self.sends, self.arrivals = sends, arrivals
        self.places, self.peer = places_of(axis)
        _, self.up, self.down, _ = self.places[0]
        self.other = self.places[1][0]
        self.rows, self.width = near.shape[1], near.shape[2]
        self.half = self.rows // 2
        self.started = []

    def _send(self, slot, source, target, place):
        def copy():
            return remote(source(), target(), self.sends, self.arrivals, slot, self.peer(place))

        copy().start()
        self.started.append(copy)

    def _await(self, slot, ref):
        remote(ref, ref, self.sends, self.arrivals, slot, self.peer(self.other)).wait_recv()

    def begin(self):
        self.send_far()
        self.send_near(0)
        self.send_near(1)

    def send_far(self):
        for column in (1, 0):
            self._send_far(column)

    def _send_far(self, column):
        low, high = pl.ds(0, self.half), pl.ds(self.half, self.half)
        far = self.places[column][3]
        slot, a, b = 6 * column, 2 * column, 2 * column + 1
        parts, passing = self.parts, self.passing
        self._send(slot, lambda: parts.at[far, low], lambda: passing.at[a], self.up)
        self._send(slot + 1, lambda: parts.at[far, high], lambda: passing.at[b], self.down)

    def send_near(self, side):
        for column in (1, 0):
            self._send_near(column, side)

    def _send_near(self, column, side):
        half = pl.ds((1 - side) * self.half, self.half)
        toward, place = self.places[column][1 + side], (self.up, self.down)[side]
        index, parts, near = 2 * column + side, self.parts, self.near
        self._send(
            6 * column + 2 + side,
            lambda: parts.at[toward, half],
            lambda: near.at[index, half],
            place,
        )

    def pass_side(self, side):
        for column in (1, 0):
            self._pass_side(column, side)

    def _loop(self, rows, body):
        step = 16

        def run(i, carry):
            body(pl.multiple_of(i * step, step), step)
            return carry

        lax.fori_loop(0, rows // step, run, 0)

    def pass_on(self, column):
        self._pass_side(column, 0)
        self._pass_side(column, 1)

    def _pass_side(self, column, side):
        slot, index, start = 6 * column, 2 * column + side, side * self.half
        toward, place = self.places[column][1 + side], (self.up, self.down)[side]
        passing, near, held = self.passing, self.near, self.held
        self._await(slot + side, passing.at[index])

        def add(row, step):
            there = pl.ds(row, step)
            total = passing[index, there, :].astype(jnp.float32)
            total = total + held[toward, pl.ds(start + row, step), :].astype(jnp.float32)
            passing[index, there, :] = total.astype(jnp.bfloat16)

        self._loop(self.half, add)
        target = pl.ds(start, self.half)
        self._send(
            slot + 4 + side, lambda: passing.at[index], lambda: near.at[index, target], place
        )

    def _near(self, column):
        low, high = pl.ds(0, self.half), pl.ds(self.half, self.half)
        slot = 6 * column
        self._await(slot + 2, self.near.at[2 * column, high])
        self._await(slot + 3, self.near.at[2 * column + 1, low])
        self._await(slot + 4, self.near.at[2 * column, low])
        self._await(slot + 5, self.near.at[2 * column + 1, high])

    def _sum(self, column, there):
        place = self.places[column][0]
        total = self.held[place, there, :].astype(jnp.float32)
        total = total + self.near[2 * column, there, :].astype(jnp.float32)
        return total + self.near[2 * column + 1, there, :].astype(jnp.float32)

    def cross(self):
        self._near(1)
        place, held, across = self.places[1][0], self.held, self.across
        if across.shape[0] == 1:
            kept = lambda: held.at[place]
        else:
            kept = lambda: across.at[1]

        def add(row, step):
            there = pl.ds(row, step)
            kept()[there, :] = self._sum(1, there).astype(jnp.bfloat16)

        self._loop(self.rows, add)
        self._send(12, kept, lambda: across.at[0], self.other)

    def ready(self):
        self._near(0)
        self._await(12, self.across.at[0])

    def total(self, there):
        return self._sum(0, there) + self.across[0, there, :].astype(jnp.float32)

    def end(self):
        for copy in self.started:
            copy().wait_send()


class Spread:
    SEMAPHORES = 7 + 8

    def __init__(self, own, out, sends, arrivals):
        self.own, self.out, self.sends, self.arrivals = own, out, sends, arrivals
        self.me = lax.axis_index("shard")
        self.core, self.chip = lax.rem(self.me, 2), self.me // 2
        self.mate = {"shard": self.me + 1 - 2 * self.core}
        self.started = []

    def _send(self, slot, source, target, peer):
        copy = remote(source, target, self.sends, self.arrivals, slot, peer)
        copy.start()
        self.started.append(copy)

    def _await(self, slot, ref):
        remote(ref, ref, self.sends, self.arrivals, slot, self.mate).wait_recv()

    def _from(self, k, core):
        return self.out.at[2 * lax.rem(self.chip + CHIPS - k, CHIPS) + core]

    def peers(self):
        return [self.mate] + [
            {"shard": 2 * lax.rem(self.chip + k, CHIPS) + self.core} for k in range(1, CHIPS)
        ]

    def begin(self):
        target = self.out.at[self.me]
        for k in range(1, CHIPS):
            peer = {"shard": 2 * lax.rem(self.chip + k, CHIPS) + self.core}
            self._send(k - 1, self.own, target, peer)
        self._send(7, self.own, target, self.mate)

    def hand_on(self):
        for k in range(1, CHIPS):
            block = self._from(k, self.core)
            self._await(k - 1, block)
            self._send(7 + k, block, block, self.mate)

    def end(self):
        for k in range(CHIPS):
            self._await(7 + k, self._from(k, 1 - self.core))
        for copy in self.started:
            copy.wait_send()


def front(block, qkv_weight, out_weight, small):
    rows, width = qkv_weight.shape[0], out_weight.shape[1] // N_CTX
    n_shard = out_weight.shape[1] // rows

    def kernel(
        block, qkv_weight, out_weight, small, x_all, weights, small_all, staged, loads, local, *scratch
    ):
        gather = Gather(block, x_all, *scratch[0:2])
        spread = Spread(staged, weights, *scratch[2:4])
        spread_small = Spread(small, small_all, *scratch[4:6])
        place = gather.me
        loaded = [
            pltpu.make_async_copy(
                qkv_weight.at[:, pl.ds(pl.multiple_of(width * N_CTX * i + width * place, width), width)],
                staged.at[:, width * i : width * (i + 1)],
                loads.at[i],
            )
            for i in range(3)
        ] + [
            pltpu.make_async_copy(
                out_weight.at[:, pl.ds(pl.multiple_of(width * place, width), width)],
                staged.at[:, 3 * width :],
                loads.at[3],
            )
        ]
        for copy in loaded:
            copy.start()
        greet([{"ctx": p} for p in (gather.other, gather.up, gather.down)] + spread.peers())
        gather.begin()
        spread_small.begin()
        for copy in loaded:
            copy.wait()
        spread.begin()
        kept = [
            pltpu.make_async_copy(source, target, local.at[k])
            for k, (source, target) in enumerate(
                (
                    (block, x_all.at[place]),
                    (staged, weights.at[spread.me]),
                    (small, small_all.at[spread.me]),
                )
            )
        ]
        for copy in kept:
            copy.start()
        gather.pass_other()
        spread_small.hand_on()
        gather.pass_ring(0)
        spread.hand_on()
        gather.pass_ring(1)
        for copy in kept:
            copy.wait()
        spread_small.end()
        spread.end()
        gather.end()

    bf16 = jnp.bfloat16
    return pl.pallas_call(
        kernel,
        out_shape=(
            jax.ShapeDtypeStruct((N_CTX,) + block.shape, bf16),
            jax.ShapeDtypeStruct((n_shard, rows, 4 * width), bf16),
            jax.ShapeDtypeStruct((n_shard,) + small.shape, bf16),
        ),
        in_specs=[ANY] * 4,
        out_specs=(ANY, ANY, ANY),
        scratch_shapes=[
            pltpu.VMEM((rows, 4 * width), bf16),
            pltpu.SemaphoreType.DMA((4,)),
            pltpu.SemaphoreType.DMA((3,)),
        ]
        + [pltpu.SemaphoreType.DMA((Gather.SEMAPHORES,))] * 2
        + [pltpu.SemaphoreType.DMA((Spread.SEMAPHORES,))] * 4,
        compiler_params=params(0),
        name="front",
    )(block, qkv_weight, out_weight, small)


def middle(parts, inputs, gain):
    _, rows, width = parts.shape

    def kernel(parts, inputs, gain, residual, out, own, local, *scratch):
        reduce_scratch, gather_scratch = scratch[:5], scratch[5:]
        reduce = Reduce(parts, parts, *reduce_scratch)
        gather = Gather(own, out, *gather_scratch)
        greet([{"ctx": p} for p in (gather.other, gather.up, gather.down)])
        reduce.begin()
        reduce.pass_on(1)
        reduce.pass_on(0)
        reduce.cross()
        reduce.ready()

        def norm(there):
            total = inputs[there, :].astype(jnp.float32) + reduce.total(there)
            residual[there, :] = total
            normed, _ = normalize(total)
            own[there, :] = (normed * gain[...]).astype(jnp.bfloat16)

        by_rows(rows, norm)
        gather.begin()
        copy = pltpu.make_async_copy(own, out.at[gather.me], local)
        copy.start()
        gather.pass_other()
        gather.pass_ring(0)
        gather.pass_ring(1)
        reduce.end()
        copy.wait()
        gather.end()

    return pl.pallas_call(
        kernel,
        out_shape=(
            jax.ShapeDtypeStruct((rows, width), jnp.float32),
            jax.ShapeDtypeStruct((N_CTX, rows, width), jnp.bfloat16),
        ),
        in_specs=[VMEM, VMEM, VMEM],
        out_specs=(VMEM, ANY),
        scratch_shapes=[pltpu.VMEM((rows, width), jnp.bfloat16), pltpu.SemaphoreType.DMA]
        + Reduce.scratch(rows, width)
        + [pltpu.SemaphoreType.DMA((Gather.SEMAPHORES,))] * 2,
        compiler_params=params(1, 40 << 20),
        name="middle",
    )(parts, inputs, gain)


def feed_forward(second, grad_out, assigned, w_in, w_down, logit_weights, logit_rows, member, residual, own_grad, own_valid, gain):
    _, rows, width = second.shape
    seq = rows * N_CTX
    hidden = w_down.shape[1]
    lanes = logit_weights.shape[1]
    pair = 2 * rows
    tile = 256
    f32, bf16 = jnp.float32, jnp.bfloat16

    def kernel(
        second, grad_out, assigned, w_in, w_down, logit_weights, logit_rows, member,
        residual, own_grad, own_valid, gain,
        grad_residual, output, grad_gain, grad_logits, act_out, grad_gu_out,
        second_held, grad_held, in_held, down_held, act, grad_gu, weights, dots, dots_in, gain_sum,
        back_parts, ffn_parts, dot_sends, dot_arrivals, loads, weight_loads, stores, *scratch,
    ):
        back = Reduce(back_parts, back_parts, *scratch[:5])
        ahead = Reduce(ffn_parts, ffn_parts, *scratch[5:])
        own, other = back.places
        me = own[0]
        peers = [lax.rem(me + k, N_CTX) for k in range(1, N_CTX)]
        copies = [
            pltpu.make_async_copy(source, target, loads.at[k])
            for k, (source, target) in enumerate(((second, second_held), (grad_out, grad_held)))
        ]
        for copy in copies:
            copy.start()

        def weight_copies(t):
            columns = [
                pl.ds(pl.multiple_of(start + tile * t, tile), tile) for start in (0, hidden, 0)
            ]
            return [
                pltpu.make_async_copy(
                    source.at[:, there], target.at[:, there], weight_loads.at[3 * t + k]
                )
                for k, (source, target, there) in enumerate(
                    zip((w_in, w_in, w_down), (in_held, in_held, down_held), columns)
                )
            ]

        def start_weights(t, carry):
            for copy in weight_copies(t):
                copy.start()
            return carry

        lax.fori_loop(0, hidden // tile, start_weights, 0)
        greet([{"ctx": p} for p in peers])
        for copy in copies:
            copy.wait()

        def stored(slot, start):
            there = pl.ds(start, pair)
            return [
                pltpu.make_async_copy(act.at[slot], act_out.at[there, :], stores.at[slot, 0]),
                pltpu.make_async_copy(grad_gu.at[slot], grad_gu_out.at[there, :], stores.at[slot, 1]),
            ]

        def dot_copy(slot, place):
            return remote(
                dots.at[place], dots_in.at[slot], dot_sends, dot_arrivals, slot, {"ctx": place}
            )

        def start_of(b):
            ahead = 2 - b + 3 * (b // 2) - 2 * (b // 3)
            return pl.multiple_of(lax.rem(me // 2 + ahead, N_CTX // 2) * pair, pair)

        def block(b, carry):
            start = start_of(b)
            slot = lax.rem(b, 2)
            first = pl.multiple_of(start // rows, 2)

            @pl.when(b >= 2)
            def _():
                for copy in stored(slot, start_of(b - 2)):
                    copy.wait()

            def rows_of(ref):
                return ref[pl.ds(first, 2)].reshape(pair, width)

            logits = jnp.dot(
                rows_of(second_held), logit_weights[...], preferred_element_type=f32
            )
            lane = lax.broadcasted_iota(jnp.int32, logits.shape, 1)
            named = assigned[pl.ds(start, pair), :] > 0
            raised = jnp.where(named, logits, -1e30)
            raised = jnp.exp(raised - jnp.max(raised, axis=-1, keepdims=True))
            raised = jnp.where(named, raised, 0.0)
            gates = raised / jnp.sum(raised, axis=-1, keepdims=True)
            gates = jnp.where(lane == EXPERTS, jax.nn.sigmoid(logits), gates)
            weights[pl.ds(start, pair), :] = gates
            dots[pl.ds(first, 2)] = jnp.zeros((2, rows, lanes), f32)

            def hidden_tile(t, carry):
                @pl.when(b == 0)
                def _():
                    for copy in weight_copies(t):
                        copy.wait()

                low = pl.ds(pl.multiple_of(tile * t, tile), tile)
                high = pl.ds(pl.multiple_of(hidden + tile * t, tile), tile)
                rows_in = rows_of(second_held)
                gate = jnp.dot(rows_in, in_held[:, low], preferred_element_type=f32)
                upward = jnp.dot(rows_in, in_held[:, high], preferred_element_type=f32)
                raw = jnp.dot(rows_of(grad_held), down_held[:, low], preferred_element_type=f32)
                held = jnp.dot(
                    weights[pl.ds(start, pair), :],
                    member[:, low],
                    precision=highest,
                    preferred_element_type=f32,
                )
                squashed = jax.nn.sigmoid(gate)
                swished = gate * squashed
                value = swished * upward
                act[slot, :, low] = (value * held).astype(bf16)
                part = lax.dot_general(
                    raw * value,
                    member[:, low],
                    (((1,), (1,)), ((), ())),
                    precision=highest,
                    preferred_element_type=f32,
                )
                dots[pl.ds(first, 2)] += part.reshape(2, rows, lanes)
                grad = raw * held
                grad_gu[slot, :, low] = (
                    grad * upward * squashed * (1.0 + gate * (1.0 - squashed))
                ).astype(bf16)
                grad_gu[slot, :, high] = (grad * swished).astype(bf16)
                return carry

            lax.fori_loop(0, hidden // tile, hidden_tile, 0)
            for copy in stored(slot, start):
                copy.start()

            def out_tile(t, carry):
                there = pl.ds(pl.multiple_of(512 * t, 512), 512)
                for parts, left, right in (
                    (back_parts, grad_gu, in_held),
                    (ffn_parts, act, down_held),
                ):
                    made = contract_last(left[slot], right[there, :])
                    parts[pl.ds(first, 2), :, there] = made.astype(bf16).reshape(2, rows, 512)
                return carry

            lax.fori_loop(0, width // 512, out_tile, 0)

            def far():
                back.send_far()
                ahead.send_far()
                dot_copy(0, own[3]).start()
                dot_copy(1, other[3]).start()

            def near(side):
                back.send_near(side)
                back.pass_side(side)
                ahead.send_near(side)
                ahead.pass_side(side)
                dot_copy(2 + 2 * side, own[1 + side]).start()
                dot_copy(3 + 2 * side, other[1 + side]).start()

            pl.when(b == 0)(far)
            pl.when(b == 1)(lambda: near(0))
            pl.when(b == 2)(lambda: near(1))
            return carry

        lax.fori_loop(0, 4, block, 0)
        dot_copy(6, other[0]).start()
        back.cross()
        ahead.cross()
        back.ready()
        for k in range(7):
            ref = dots_in.at[k]
            remote(ref, ref, dot_sends, dot_arrivals, k, {"ctx": other[0]}).wait_recv()
        total_dots = dots[me]
        for k in range(7):
            total_dots = total_dots + dots_in[k]
        held = weights[pl.ds(pl.multiple_of(me * rows, rows), rows), :]
        lane = lax.broadcasted_iota(jnp.int32, held.shape, 1)
        routed = lane < EXPERTS
        centre = jnp.sum(jnp.where(routed, held * total_dots, 0.0), axis=-1, keepdims=True)
        both = jnp.where(
            routed,
            held * (total_dots - centre),
            jnp.where(lane == EXPERTS, total_dots * held * (1.0 - held), 0.0),
        )
        grad_logits[...] = both
        grad_residual[...] = jnp.dot(
            both, logit_rows[...], precision=highest, preferred_element_type=f32
        )
        gain_sum[...] = jnp.zeros_like(gain_sum)

        def norm(there):
            normed, factor = normalize(residual[there, :])
            grad = back.total(there) + grad_residual[there, :]
            gain_sum[...] += grad * normed
            grad_residual[there, :] = own_grad[there, :].astype(f32) + norm_back(
                grad, normed, factor, gain[...]
            )

        by_rows(rows, norm)
        grad_gain[...] = jnp.sum(gain_sum[...], axis=0, keepdims=True)
        ahead.ready()

        def finish(there):
            total = residual[there, :] + ahead.total(there)
            output[there, :] = (total * own_valid[there, :]).astype(bf16)

        by_rows(rows, finish)
        for b in (2, 3):
            for copy in stored(b % 2, start_of(b)):
                copy.wait()
        back.end()
        ahead.end()
        for slot, place in enumerate((own[3], other[3], own[1], other[1], own[2], other[2], other[0])):
            dot_copy(slot, place).wait_send()

    return pl.pallas_call(
        kernel,
        out_shape=(
            jax.ShapeDtypeStruct((rows, width), f32),
            jax.ShapeDtypeStruct((rows, width), bf16),
            jax.ShapeDtypeStruct((1, width), f32),
            jax.ShapeDtypeStruct((rows, lanes), f32),
            jax.ShapeDtypeStruct((seq, hidden), bf16),
            jax.ShapeDtypeStruct((seq, 2 * hidden), bf16),
        ),
        in_specs=[ANY, ANY, VMEM, ANY, ANY] + [VMEM] * 7,
        out_specs=(VMEM, VMEM, VMEM, VMEM, ANY, ANY),
        scratch_shapes=[
            pltpu.VMEM(second.shape, bf16),
            pltpu.VMEM(grad_out.shape, bf16),
            pltpu.VMEM(w_in.shape, bf16),
            pltpu.VMEM(w_down.shape, bf16),
            pltpu.VMEM((2, pair, hidden), bf16),
            pltpu.VMEM((2, pair, 2 * hidden), bf16),
            pltpu.VMEM((seq, lanes), f32),
            pltpu.VMEM((N_CTX, rows, lanes), f32),
            pltpu.VMEM((N_CTX - 1, rows, lanes), f32),
            pltpu.VMEM((16, width), f32),
            pltpu.VMEM(second.shape, bf16),
            pltpu.VMEM(second.shape, bf16),
            pltpu.SemaphoreType.DMA((N_CTX - 1,)),
            pltpu.SemaphoreType.DMA((N_CTX - 1,)),
            pltpu.SemaphoreType.DMA((2,)),
            pltpu.SemaphoreType.DMA((3 * hidden // tile,)),
            pltpu.SemaphoreType.DMA((2, 2)),
        ]
        + Reduce.scratch(rows, width, 1) * 2,
        compiler_params=params(2, 64 << 20),
        name="feed_forward",
    )(second, grad_out, assigned, w_in, w_down, logit_weights, logit_rows, member, residual, own_grad, own_valid, gain)


class Exchange:
    @staticmethod
    def scratch():
        return [pltpu.SemaphoreType.DMA((CHIPS,)), pltpu.SemaphoreType.DMA((CHIPS,))]

    def __init__(self, parts, staged, sends, arrivals):
        self.parts, self.staged = parts, staged
        self.sems = (sends, arrivals)
        self.width = parts.shape[2]
        me = lax.axis_index("shard")
        self.core, self.chip = lax.rem(me, 2), me // 2
        self.mate = {"shard": me + 1 - 2 * self.core}

    def chip_at(self, step):
        base = self.chip + (1 - lax.rem(step, 2)) * (1 - 2 * lax.rem(self.chip, 2))
        b = step // 2
        ahead = 2 - b + 3 * (b // 2) - 2 * (b // 3)
        return 2 * lax.rem(base // 2 + ahead, 4) + lax.rem(base, 2)

    def _pair(self, step):
        return remote(
            self.staged.at[lax.rem(step, 2), 1 - self.core, :, pl.ds(0, self.width)],
            self.parts.at[self.chip_at(step)],
            *self.sems,
            step,
            self.mate,
        )

    def finish(self, step):
        chip, slot, width = self.chip_at(step), lax.rem(step, 2), self.width
        ref = self.parts.at[chip]
        remote(ref, ref, *self.sems, step, self.mate).wait_recv()

        def add(there):
            total = self.parts[chip, there, :].astype(jnp.float32)
            total = total + self.staged[slot, self.core, there, 0:width].astype(jnp.float32)
            self.parts[chip, there, :] = total.astype(jnp.bfloat16)

        by_rows(128, add)

    def run(self, left, right, turned, between):
        width = self.width
        tile = 896 if width % 896 == 0 else width

        def step_of(step, carry):
            @pl.when(step >= 2)
            def _():
                self._pair(step - 2).wait_send()

            slot = lax.rem(step, 2)
            columns = pl.ds(pl.multiple_of(self.chip_at(step) * 256, 256), 256)
            turned[...] = left[:, :, columns].reshape(turned.shape[1], 256).T
            for start in range(0, width, tile):
                made = jnp.dot(
                    turned[...], right(start, tile), preferred_element_type=jnp.float32
                ).astype(jnp.bfloat16)
                self.staged[slot, 0, :, start : start + tile] = made[:128]
                self.staged[slot, 1, :, start : start + tile] = made[128:]
            self._pair(step).start()

            @pl.when(step >= 1)
            def _():
                self.finish(step - 1)

            for at, events in between.items():

                @pl.when(step == at)
                def _(events=events):
                    for event in events:
                        event()

            return carry

        lax.fori_loop(0, CHIPS, step_of, 0)
        self.finish(CHIPS - 1)
        for step in (CHIPS - 2, CHIPS - 1):
            self._pair(step).wait_send()


class Share:
    @staticmethod
    def scratch(width):
        return (
            [pltpu.VMEM((CHIPS, 128, width), jnp.bfloat16), pltpu.VMEM((128, width), jnp.bfloat16)]
            + Exchange.scratch()
            + Reduce.scratch(128, width, 1)
            + [pltpu.SemaphoreType.DMA((Gather.SEMAPHORES,))] * 2
            + [pltpu.SemaphoreType.DMA]
        )

    COUNT = 2 + 2 + 5 + 2 + 1

    def __init__(self, staged, out, scratch):
        parts, self.owned = scratch[0:2]
        self.exchange = Exchange(parts, staged, *scratch[2:4])
        self.reduce = Reduce(parts, parts, *scratch[4:9], axis="shard")
        self.gather = Gather(self.owned, out, *scratch[9:11])
        self.local = scratch[11]

    def near(self, side):
        return lambda: self.reduce.send_near(side)

    def side(self, side):
        return lambda: self.reduce.pass_side(side)

    def ring(self, column):
        return lambda: self.gather.pass_ring(column)

    def own(self):
        self.reduce.ready()

        def keep(there):
            self.owned[there, :] = self.reduce.total(there).astype(jnp.bfloat16)

        by_rows(128, keep)
        self.gather.begin()
        self._kept().start()

    def _kept(self):
        return pltpu.make_async_copy(
            self.owned, self.gather.out.at[self.gather.me], self.local
        )

    def end(self):
        self._kept().wait()
        self.gather.end()
        self.reduce.end()


def backward(own, second, grad_out, grad_gu, act, qkv, mixed, weights, first, cosines, sines, key_pos, query_pos, inputs, grad_residual, gain, second_gain_grad, grad_logits):
    rows, width = own.shape
    seq = rows * N_CTX
    hidden = act.shape[1]
    heads_width = mixed.shape[1]
    heads = heads_width // HEAD
    lanes = grad_logits.shape[1]
    n_shard = width // 128
    f32, bf16 = jnp.float32, jnp.bfloat16
    scale = HEAD ** (-0.5)
    tile = 256
    half = width // 2

    def kernel(
        own, second, grad_out, grad_gu, act, qkv, mixed, weights, first, cosines, sines, key_pos,
        query_pos, inputs, grad_residual, gain, second_gain_grad, grad_logits,
        input_grad, small_out, grad_attended, out_share, gate_share, up_share, mixed_share, qkv_share,
        second_held, g_held, gu_held, act_held, turned, staged, key_sum, value_sum, gain_sum,
        small, small_in, small_kept, small_across,
        loads, local, small_sends, small_arrivals, across_sends, across_arrivals, *scratch,
    ):
        gather = Gather(own, grad_attended, *scratch[0:2])
        reduce = Reduce(g_held, g_held, *scratch[2:7])
        shares = []
        for k, out in enumerate((out_share, gate_share, up_share, mixed_share, qkv_share)):
            start = 7 + Share.COUNT * k
            shares.append(Share(staged, out, scratch[start : start + Share.COUNT]))
        a, b, c, d, e = shares
        me = gather.me
        shard = lax.axis_index("shard")
        owners = [lax.rem(shard + k, n_shard) for k in range(1, n_shard)]
        places = [lax.rem(me + k, N_CTX) for k in range(1, N_CTX)]

        def load(k, source, target):
            return pltpu.make_async_copy(source, target, loads.at[k])

        early = [
            load(0, grad_out, g_held),
            load(1, act, act_held),
            load(2, second, second_held),
            load(3, grad_gu, gu_held),
        ]
        for copy in early:
            copy.start()
        greet([{"ctx": p} for p in places] + [{"shard": s} for s in owners])
        gather.begin()
        kept = pltpu.make_async_copy(own, grad_attended.at[me], local)
        kept.start()
        early[0].wait()
        early[1].wait()
        a.exchange.run(
            g_held,
            lambda start, count: act_held[:, start : start + count],
            turned,
            {
                2: [a.reduce.send_far],
                4: [a.near(0)],
                6: [a.near(1), gather.pass_other],
                7: [a.side(0)],
            },
        )
        early[2].wait()
        early[3].wait()
        b.exchange.run(
            second_held,
            lambda start, count: gu_held[:, start : start + count],
            turned,
            {
                0: [a.side(1)],
                2: [b.reduce.send_far],
                3: [lambda: gather.pass_ring(0)],
                4: [b.near(0)],
                5: [a.reduce.cross],
                6: [b.near(1), lambda: gather.pass_ring(1)],
                7: [b.side(0)],
            },
        )
        c.exchange.run(
            second_held,
            lambda start, count: gu_held[:, hidden + start : hidden + start + count],
            turned,
            {
                0: [b.side(1)],
                2: [c.reduce.send_far],
                3: [a.own],
                4: [c.near(0)],
                5: [b.reduce.cross],
                6: [c.near(1)],
                7: [c.side(0)],
            },
        )
        logits_grad = lax.dot_general(
            grad_logits[...],
            second_held[me].astype(f32),
            (((0,), (0,)), ((), ())),
            precision=highest,
            preferred_element_type=f32,
        )
        small[...] = jnp.zeros_like(small)
        for s in range(n_shard):
            there = slice(128 * s, 128 * (s + 1))
            small[s, 1:2, :] = second_gain_grad[:, there]
            small[s, 2 : 3 + EXPERTS, :] = logits_grad[: EXPERTS + 1, there]
        kept.wait()
        gather.end()
        late = [
            load(0, grad_attended, g_held),
            load(1, weights.at[pl.ds(0, half), :], gu_held.at[:, 0:half]),
            load(2, weights.at[pl.ds(half, half), :], gu_held.at[:, half : 2 * half]),
            load(3, qkv, gu_held.at[:, 2 * half : 2 * half + 3 * heads_width]),
            load(
                4,
                mixed,
                gu_held.at[:, 2 * half + 3 * heads_width : 2 * half + 4 * heads_width],
            ),
            load(5, first, second_held),
        ]
        for copy in late:
            copy.start()
        c.side(1)()
        for copy in late:
            copy.wait()
        columns_qkv = 2 * half
        columns_mixed = columns_qkv + 3 * heads_width
        columns_grad = columns_mixed + heads_width
        w_out = [3 * heads_width, half + 3 * heads_width]

        def grad_mixed(i, carry):
            first_block = 2 * i
            there = pl.ds(pl.multiple_of(i * tile, tile), tile)
            left = g_held[pl.ds(first_block, 2)].reshape(tile, width)
            made = jnp.dot(
                left[:, :half],
                gu_held[:, w_out[0] : w_out[0] + heads_width],
                preferred_element_type=f32,
            ) + jnp.dot(
                left[:, half:],
                gu_held[:, w_out[1] : w_out[1] + heads_width],
                preferred_element_type=f32,
            )
            gu_held[there, columns_grad : columns_grad + heads_width] = made.astype(bf16)
            return carry

        lax.fori_loop(0, seq // tile, grad_mixed, 0)
        a.gather.pass_other()
        d.exchange.run(
            g_held,
            lambda start, count: gu_held[:, columns_mixed + start : columns_mixed + start + count],
            turned,
            {
                2: [d.reduce.send_far],
                4: [d.near(0), a.ring(0)],
                6: [d.near(1)],
                7: [d.side(0), b.own],
            },
        )
        events = {
            0: [c.reduce.cross, a.ring(1), d.side(1)],
            1: [b.gather.pass_other],
            2: [d.reduce.cross, b.ring(0)],
            3: [c.own],
            4: [b.ring(1), d.own],
            5: [c.gather.pass_other],
            6: [d.gather.pass_other],
            7: [c.ring(0), d.ring(0)],
        }

        def attend(n, carry):
            head, i = n // (seq // tile), lax.rem(n, seq // tile)
            there = pl.ds(pl.multiple_of(i * tile, tile), tile)

            def lanes_of(start):
                return pl.ds(pl.multiple_of(start + HEAD * head, HEAD), HEAD)

            query = gu_held[there, lanes_of(columns_qkv)]
            key = gu_held[:, lanes_of(columns_qkv + heads_width)]
            value = gu_held[:, lanes_of(columns_qkv + 2 * heads_width)]
            grad = gu_held[there, lanes_of(columns_grad)]
            scores = contract_last(key, query) * scale
            scores = jnp.where(key_pos[...] <= query_pos[:, there], scores, -1e30)
            raised = jnp.exp(scores - jnp.max(scores, axis=0, keepdims=True))
            probs = raised * (1.0 / jnp.sum(raised, axis=0, keepdims=True))
            grad_probs = contract_last(value, grad)
            centre = jnp.sum(probs * grad_probs, axis=0, keepdims=True)
            grad_scores = (probs * (grad_probs - centre)).astype(bf16)

            @pl.when(i == 0)
            def _():
                key_sum[...] = jnp.zeros_like(key_sum)
                value_sum[...] = jnp.zeros_like(value_sum)

            key_sum[...] += jnp.dot(grad_scores, query, preferred_element_type=f32)
            value_sum[...] += jnp.dot(probs.astype(bf16), grad, preferred_element_type=f32)
            grad_query = contract_first(grad_scores, key) * scale

            def turn_back(values, cosines, sines):
                return (values * cosines + pltpu.roll(values, HEAD // 2, 1) * sines).astype(bf16)

            act_held[there, lanes_of(0)] = turn_back(
                grad_query, cosines[there, :], sines[there, :]
            )

            @pl.when(i == seq // tile - 1)
            def _():
                act_held[:, lanes_of(heads_width)] = turn_back(
                    key_sum[...] * scale, cosines[...], sines[...]
                )
                act_held[:, lanes_of(2 * heads_width)] = value_sum[...].astype(bf16)

            for at, todo in events.items():

                @pl.when(n == at)
                def _(todo=todo):
                    for event in todo:
                        event()

            return carry

        lax.fori_loop(0, heads * (seq // tile), attend, 0)

        def start_of(k):
            ahead = 2 - k + 3 * (k // 2) - 2 * (k // 3)
            return lax.rem(me // 2 + ahead, N_CTX // 2) * 2

        def grad_first(k, carry):
            block = start_of(k)
            left = act_held[pl.ds(pl.multiple_of(block * rows, tile), tile), 0 : 3 * heads_width]
            for t in range(4):
                low = 512 * (t % 2)
                start = half * (t // 2)
                made = contract_last(left, gu_held[low : low + 512, start : start + 3 * heads_width])
                g_held[pl.ds(block, 2), :, 512 * t : 512 * (t + 1)] = made.astype(bf16).reshape(
                    2, rows, 512
                )
            pl.when(k == 0)(reduce.send_far)
            pl.when(k == 1)(lambda: reduce.send_near(0))
            pl.when(k == 2)(lambda: reduce.send_near(1))
            return carry

        lax.fori_loop(0, 4, grad_first, 0)
        e.exchange.run(
            second_held,
            lambda start, count: act_held[:, start : start + count],
            turned,
            {
                1: [lambda: reduce.pass_side(0)],
                2: [e.reduce.send_far, lambda: reduce.pass_side(1)],
                4: [e.near(0), c.ring(1)],
                6: [e.near(1), d.ring(1)],
                7: [e.side(0), reduce.cross],
            },
        )
        e.side(1)()
        bias = jnp.sum(act_held[:, 0 : 3 * heads_width].astype(f32), axis=0, keepdims=True)
        per = heads_width // 128
        for i in range(3):
            for j in range(per):
                block = n_shard * i + per * me + j
                there = slice(heads_width * i + 128 * j, heads_width * i + 128 * (j + 1))
                small[block // 3, pl.ds(3 + EXPERTS + lax.rem(block, 3), 1), :] = bias[:, there]
        e.reduce.cross()
        reduce.ready()
        gain_sum[...] = jnp.zeros_like(gain_sum)

        def norm(there):
            normed, factor = normalize(inputs[there, :].astype(f32))
            grad = reduce.total(there)
            gain_sum[...] += grad * normed
            input_grad[there, :] = grad_residual[there, :] + norm_back(
                grad, normed, factor, gain[...]
            )

        by_rows(rows, norm)
        first_gain_grad = jnp.sum(gain_sum[...], axis=0, keepdims=True)
        for s in range(n_shard):
            small[s, 0:1, :] = first_gain_grad[:, 128 * s : 128 * (s + 1)]
        to_owners = [
            remote(small.at[s], small_in.at[k], small_sends, small_arrivals, k, {"shard": s})
            for k, s in enumerate(owners)
        ]
        for copy in to_owners:
            copy.start()
        e.own()
        total = small[shard]
        for k, copy in enumerate(to_owners):
            copy.wait_recv()
            total = total + small_in[k]
        small_kept[...] = total
        to_places = [
            remote(small_kept, small_across.at[k], across_sends, across_arrivals, k, {"ctx": p})
            for k, p in enumerate(places)
        ]
        for copy in to_places:
            copy.start()
        e.gather.pass_other()
        e.ring(0)()
        e.ring(1)()
        for k, copy in enumerate(to_places):
            copy.wait_recv()
            total = total + small_across[k]
        small_out[...] = total
        for copy in to_owners + to_places:
            copy.wait_send()
        reduce.end()
        for share in shares:
            share.end()

    def shared(count):
        return jax.ShapeDtypeStruct((N_CTX, 128, count), bf16)

    return pl.pallas_call(
        kernel,
        out_shape=(
            jax.ShapeDtypeStruct((rows, width), f32),
            jax.ShapeDtypeStruct((16, 128), f32),
            jax.ShapeDtypeStruct((N_CTX, rows, width), bf16),
            shared(hidden),
            shared(hidden),
            shared(hidden),
            shared(heads_width),
            shared(3 * heads_width),
        ),
        in_specs=[VMEM] + [ANY] * 8 + [VMEM] * 9,
        out_specs=(VMEM, VMEM) + (ANY,) * 6,
        scratch_shapes=[
            pltpu.VMEM(second.shape, bf16),
            pltpu.VMEM(grad_out.shape, bf16),
            pltpu.VMEM(grad_gu.shape, bf16),
            pltpu.VMEM(act.shape, bf16),
            pltpu.VMEM((256, seq), bf16),
            pltpu.VMEM((2, 2, 128, hidden), bf16),
            pltpu.VMEM((seq, HEAD), f32),
            pltpu.VMEM((seq, HEAD), f32),
            pltpu.VMEM((16, width), f32),
            pltpu.VMEM((n_shard, 16, 128), f32),
            pltpu.VMEM((n_shard - 1, 16, 128), f32),
            pltpu.VMEM((16, 128), f32),
            pltpu.VMEM((N_CTX - 1, 16, 128), f32),
            pltpu.SemaphoreType.DMA((6,)),
            pltpu.SemaphoreType.DMA,
            pltpu.SemaphoreType.DMA((n_shard - 1,)),
            pltpu.SemaphoreType.DMA((n_shard - 1,)),
            pltpu.SemaphoreType.DMA((N_CTX - 1,)),
            pltpu.SemaphoreType.DMA((N_CTX - 1,)),
        ]
        + [pltpu.SemaphoreType.DMA((Gather.SEMAPHORES,))] * 2
        + Reduce.scratch(rows, width, 1)
        + Share.scratch(hidden) * 3
        + Share.scratch(heads_width)
        + Share.scratch(3 * heads_width),
        compiler_params=params(3, 64 << 20),
        name="backward",
    )(own, second, grad_out, grad_gu, act, qkv, mixed, weights, first, cosines, sines, key_pos, query_pos, inputs, grad_residual, gain, second_gain_grad, grad_logits)


def local(
    tokens,
    cotangent,
    lengths,
    routes,
    block_order,
    norm_gains,
    qkv_weight,
    qkv_bias,
    out_weight,
    router,
    shared_gate,
    ffn_in,
    ffn_out,
):
    bf16, f32 = jnp.bfloat16, jnp.float32
    n_ctx = lax.axis_size("ctx")
    n_shard = lax.axis_size("shard")
    rows_dev = tokens.shape[1]
    seq_len = rows_dev * n_ctx
    n_blocks = block_order.shape[0]
    block = seq_len // n_blocks
    heads = D // HEAD // n_ctx
    width = heads * HEAD
    hidden_blocks = -(-HIDDEN_BLOCKS // n_ctx)
    hidden = hidden_blocks * LANE
    scale = HEAD ** (-0.5)
    place = lax.axis_index("ctx")

    every = jnp.arange(seq_len, dtype=jnp.int32)
    matches = (every // block)[:, None] == jnp.arange(n_blocks, dtype=jnp.int32)[None, :]
    pos = jnp.sum(jnp.where(matches, block_order[None, :], 0), axis=1) * block + every % block
    valid = pos < lengths[0]
    valid_rows = valid.astype(f32)[:, None]

    blocked = (n_ctx, rows_dev, D)
    own_valid = lax.dynamic_slice_in_dim(valid_rows, place * rows_dev, rows_dev)
    own_grad = jnp.where(own_valid > 0, cotangent[0], 0).astype(bf16)
    g_all = ag_ctx(own_grad)
    blocks = [hidden_blocks * place + j for j in range(hidden_blocks)]
    safe = [jnp.minimum(b, HIDDEN_BLOCKS - 1) for b in blocks]
    starts = [gate_start(b) for b in safe]
    w_in = ag_shard(columns_at(ffn_in, [s for s, _ in starts] + [s + u for s, u in starts]))
    w_down = ag_shard(columns_at(ffn_out, [LANE * b for b in safe]))
    picks = routes[0][:, :, None] == jnp.arange(LANE, dtype=jnp.int32)[None, None, :]
    own_assigned = jnp.sum(picks.astype(f32), axis=1).astype(bf16)
    small = jnp.concatenate(
        [
            norm_gains.reshape(-1),
            router.T.reshape(-1),
            shared_gate.reshape(-1),
            qkv_bias.reshape(-1),
        ]
    ).reshape(-1, LANE)
    small = jnp.pad(small, ((0, 4), (0, 0)))
    x_all, attn_weights, small_all = front(
        jnp.concatenate([tokens[0], own_assigned], axis=1), qkv_weight, out_weight, small
    )
    x_all = x_all.reshape(seq_len, D + LANE)
    x_all, assigned = x_all[:, :D], x_all[:, D:]
    attn_weights = attn_weights.reshape(D, 4 * width)
    small_all = small_all.reshape(n_shard, -1)
    gains = small_all[:, : 2 * LANE].reshape(n_shard, 2, LANE).transpose(1, 0, 2).reshape(2, D)
    first_gain, second_gain = gains[0].astype(f32), gains[1].astype(f32)
    logit_weights = (
        small_all[:, 2 * LANE : 9 * LANE]
        .reshape(n_shard, EXPERTS + 1, LANE)
        .transpose(0, 2, 1)
        .reshape(D, EXPERTS + 1)
    )
    bias = small_all[:, 9 * LANE : 12 * LANE].reshape(3 * D)
    own_bias = jnp.concatenate(
        [lax.dynamic_slice_in_dim(bias, D * i + width * place, width) for i in range(3)]
    ).astype(f32)
    w_qkv, w_out = attn_weights[:, : 3 * width], attn_weights[:, 3 * width :]

    first_normed_all, _ = normalize(x_all.astype(f32))
    first_all = (first_normed_all * first_gain).astype(bf16)
    projected = dot(first_all, w_qkv) + own_bias
    cosines, sines = rope_tables(pos)
    query = rotate(projected[:, :width].reshape(seq_len, heads, HEAD), cosines, sines).astype(bf16)
    key = rotate(
        projected[:, width : 2 * width].reshape(seq_len, heads, HEAD), cosines, sines
    ).astype(bf16)
    value = projected[:, 2 * width :].astype(bf16).reshape(seq_len, heads, HEAD)
    allowed = ((pos[None, :] <= pos[:, None]) & valid[None, :])[None]
    scores = jnp.einsum("qhd,khd->hqk", query, key, preferred_element_type=f32) * scale
    masked = jnp.where(allowed, scores, -1e30)
    peak = jnp.max(masked, axis=-1, keepdims=True)
    log_total = peak + jnp.log(jnp.sum(jnp.exp(masked - peak), axis=-1, keepdims=True))
    probs = jnp.exp(masked - log_total)
    probs_low = probs.astype(bf16)
    mixed = jnp.einsum("hqk,khd->qhd", probs_low, value, preferred_element_type=f32)
    mixed = mixed.reshape(seq_len, width).astype(bf16)
    residual, second_all = middle(
        contract_last(mixed, w_out).astype(bf16).reshape(n_ctx, rows_dev, D),
        tokens[0],
        second_gain[None],
    )

    block_ids = jnp.stack(blocks)
    branch_of = jnp.where(
        block_ids < SHARED_BLOCKS, EXPERTS, (block_ids - SHARED_BLOCKS) // EXPERT_BLOCKS
    )
    member = (
        (branch_of[None, :] == jnp.arange(LANE, dtype=jnp.int32)[:, None])
        & (block_ids < HIDDEN_BLOCKS)[None, :]
    ).astype(f32)
    member = jnp.repeat(member, LANE, axis=1)
    logit_weights = jnp.pad(logit_weights, ((0, 0), (0, LANE - EXPERTS - 1)))
    grad_residual, output, grad_second_gain, grad_both, act_low, grad_gu = feed_forward(
        second_all,
        g_all.reshape(blocked),
        assigned,
        w_in,
        w_down,
        logit_weights,
        logit_weights.T.astype(f32),
        member,
        residual,
        own_grad,
        own_valid,
        second_gain[None],
    )
    lane = jnp.arange(HEAD, dtype=jnp.int32)
    turned_sines = jnp.where(lane < HEAD // 2, sines[:, 0, :], -sines[:, 0, :])
    qkv_low = jnp.concatenate(
        [part.reshape(seq_len, width) for part in (query, key, value)], axis=1
    )
    input_grad, own_small, _, out_share, gate_share, up_share, mixed_share, qkv_share = backward(
        grad_residual.astype(bf16),
        second_all,
        g_all.reshape(blocked),
        grad_gu,
        act_low,
        qkv_low,
        mixed,
        attn_weights,
        first_all.reshape(blocked),
        cosines[:, 0, :],
        turned_sines,
        jnp.where(valid, pos, 2 * seq_len)[:, None],
        pos[None],
        tokens[0],
        grad_residual,
        first_gain[None],
        grad_second_gain,
        grad_both,
    )
    own_small = own_small.reshape(-1)
    grad_gains = own_small[: 2 * LANE].reshape(2, LANE)
    grad_router = own_small[2 * LANE : 8 * LANE].reshape(EXPERTS, LANE).T
    grad_shared_gate = own_small[8 * LANE : 9 * LANE]
    grad_bias_out = own_small[9 * LANE : 12 * LANE]

    grad_qkv = jnp.concatenate(
        [
            qkv_share[p, :, width * i : width * (i + 1)]
            for i in range(3)
            for p in range(n_ctx)
        ],
        axis=1,
    ).astype(f32)
    grad_out = jnp.concatenate(
        [mixed_share[p] for p in range(n_ctx)], axis=1
    ).astype(f32)

    def piece(share, first, count):
        parts = []
        while count:
            p, j = first // hidden_blocks, first % hidden_blocks
            take = min(count, hidden_blocks - j)
            parts.append(share[p, :, LANE * j : LANE * (j + take)])
            first, count = first + take, count - take
        return parts

    spans = [(0, SHARED_BLOCKS)] + [
        (SHARED_BLOCKS + EXPERT_BLOCKS * e, EXPERT_BLOCKS) for e in range(EXPERTS)
    ]
    grad_ffn_in = jnp.concatenate(
        [part for f, n in spans for share in (gate_share, up_share) for part in piece(share, f, n)],
        axis=1,
    ).astype(f32)
    grad_ffn_out = jnp.concatenate(
        [part for f, n in spans for part in piece(out_share, f, n)], axis=1
    ).astype(f32)
    return (
        output[None],
        input_grad[None],
        grad_gains,
        grad_qkv,
        grad_bias_out,
        grad_out,
        grad_router,
        grad_shared_gate,
        grad_ffn_in,
        grad_ffn_out,
    )


def solution(mesh):
    placed = (
        P("shard", "ctx", None),
        P("shard", "ctx", None),
        P("shard"),
        P("shard", "ctx", None),
        P(),
        P(None, "shard"),
        P("shard", None),
        P("shard"),
        P("shard", None),
        P("shard", None),
        P("shard"),
        P("shard", None),
        P("shard", None),
    )
    return jax.shard_map(
        local,
        mesh=mesh,
        in_specs=placed,
        out_specs=(
            P("shard", "ctx", None),
            P("shard", "ctx", None),
            P(None, "shard"),
            P("shard", None),
            P("shard"),
            P("shard", None),
            P("shard", None),
            P("shard"),
            P("shard", None),
            P("shard", None),
        ),
        check_vma=False,
    )
```

```python
import jax
import jax.numpy as jnp
from jax import lax
from jax.experimental import pallas as pl
from jax.experimental.pallas import tpu as pltpu
from jax.sharding import PartitionSpec as P

D = 2048
HEAD = 128
HE = 1408
FS = 5632
EXPERTS = 6
FIN = 28160
FOUT = 14080
LANE = 128
SHARED_BLOCKS = FS // LANE
EXPERT_BLOCKS = HE // LANE
HIDDEN_BLOCKS = SHARED_BLOCKS + EXPERTS * EXPERT_BLOCKS

highest = lax.Precision.HIGHEST
epsilon = 1e-06
rope_base = 1000000.0


def contract_last(left, right):
    return lax.dot_general(
        left, right, (((1,), (1,)), ((), ())), preferred_element_type=jnp.float32
    )


def contract_first(left, right):
    return lax.dot_general(
        left, right, (((0,), (0,)), ((), ())), preferred_element_type=jnp.float32
    )


def dot(left, right):
    return jnp.dot(left, right, preferred_element_type=jnp.float32)


def rope_tables(positions):
    half = HEAD // 2
    freqs = rope_base ** (-jnp.arange(half, dtype=jnp.float32) * 2.0 / HEAD)
    phase = positions.astype(jnp.float32)[:, None] * freqs[None, :]
    cosines, sines = jnp.cos(phase), jnp.sin(phase)
    return (
        jnp.concatenate([cosines, cosines], axis=1),
        jnp.concatenate([-sines, sines], axis=1),
    )


def normalize(values):
    factor = lax.rsqrt(jnp.mean(values * values, axis=-1, keepdims=True) + epsilon)
    return (values * factor, factor)


def norm_back(grad_normed, normalized, factor, gain):
    scaled = grad_normed * gain
    return factor * (scaled - normalized * jnp.mean(scaled * normalized, axis=-1, keepdims=True))


MESH = pl.DeviceIdType.MESH
ANY = pl.BlockSpec(memory_space=pl.ANY)
VMEM = pl.BlockSpec(memory_space=pltpu.VMEM)
N_CTX = 8
CHIPS = 8


def params(number, limit=None):
    return pltpu.CompilerParams(
        collective_id=number, has_side_effects=True, vmem_limit_bytes=limit
    )


def greet(peers):
    semaphore = pltpu.get_barrier_semaphore()
    for peer in peers:
        pl.semaphore_signal(semaphore, inc=1, device_id=peer, device_id_type=MESH)
    pl.semaphore_wait(semaphore, len(peers))


def remote(source, target, sends, arrivals, slot, peer):
    return pltpu.make_async_remote_copy(
        src_ref=source,
        dst_ref=target,
        send_sem=sends.at[slot],
        recv_sem=arrivals.at[slot],
        device_id=peer,
        device_id_type=MESH,
    )


def places_of(axis):
    me = lax.axis_index(axis)
    if axis == "ctx":
        peer = lambda place: {"ctx": place}
    else:
        core, me = lax.rem(me, 2), me // 2
        peer = lambda place: {"shard": 2 * place + core}
    other = me + 1 - 2 * lax.rem(me, 2)
    places = [[lax.rem(base + 2 * k, N_CTX) for k in (0, 1, 3, 2)] for base in (me, other)]
    return places, peer


def by_rows(rows, body):
    step = 16

    def run(i, carry):
        body(pl.ds(pl.multiple_of(i * step, step), step))
        return carry

    lax.fori_loop(0, rows // step, run, 0)


class Gather:
    SEMAPHORES = 9
    PAIRED = 9 + CHIPS

    def __init__(self, own, out, sends, arrivals, axis="ctx"):
        self.own, self.out, self.sends, self.arrivals = own, out, sends, arrivals
        self.places, self.peer = places_of(axis)
        (self.me, self.up, self.down, self.far), other = self.places
        self.other = other[0]
        self.half = out.shape[-2] // 2
        self.paired = axis == "shard"
        if self.paired:
            shard = lax.axis_index("shard")
            self.core = lax.rem(shard, 2)
            self.mate = {"shard": shard + 1 - 2 * self.core}
        self.started = []

    def at(self, place, *half):
        if self.paired:
            return self.out.at[(place, self.core) + half]
        return self.out.at[(place,) + half]

    def _send(self, slot, source, target, peer):
        def copy():
            return remote(source(), target(), self.sends, self.arrivals, slot, peer())

        copy().start()
        self.started.append(copy)

    def _await(self, slot, ref):
        remote(ref, ref, self.sends, self.arrivals, slot, self.peer(self.other)).wait_recv()

    def _hand(self, number, place, source=None):
        if self.paired:
            block = lambda: self.at(place)
            self._send(9 + number, source or block, block, lambda: self.mate)

    def begin(self):
        for slot, place in ((0, self.other), (1, self.up), (2, self.down)):
            self._send(slot, lambda: self.own, lambda: self.at(self.me), lambda place=place: self.peer(place))
        self._hand(0, self.me, lambda: self.own)

    def pass_other(self):
        block = lambda: self.at(self.other)
        self._await(0, block())
        self._send(3, block, block, lambda: self.peer(self.up))
        self._send(4, block, block, lambda: self.peer(self.down))
        self._hand(1, self.other)

    def pass_ring(self, column):
        _, up, down, _ = self.places[column]
        first = 1 + 2 * column
        low, high = pl.ds(0, self.half), pl.ds(self.half, self.half)
        self._await(first, self.at(down))
        lower = lambda: self.at(down, low)
        self._send(5 + 2 * column, lower, lower, lambda: self.peer(self.up))
        self._await(first + 1, self.at(up))
        upper = lambda: self.at(up, high)
        self._send(6 + 2 * column, upper, upper, lambda: self.peer(self.down))
        self._hand(2 + 2 * column, down)
        self._hand(3 + 2 * column, up)

    def end(self):
        low, high = pl.ds(0, self.half), pl.ds(self.half, self.half)
        for column in range(2):
            far = self.places[column][3]
            self._await(5 + 2 * column, self.at(far, low))
            self._await(6 + 2 * column, self.at(far, high))
            self._hand(6 + column, far)
        if self.paired:
            (me, up, down, far), (other, other_up, other_down, other_far) = self.places
            for number, place in enumerate(
                (me, other, down, up, other_down, other_up, far, other_far)
            ):
                self._await(9 + number, self.out.at[place, 1 - self.core])
        for copy in self.started:
            copy().wait_send()


class Reduce:
    SEMAPHORES = 13

    @staticmethod
    def scratch(rows, width, across=2):
        return [
            pltpu.VMEM((4, rows // 2, width), jnp.bfloat16),
            pltpu.VMEM((4, rows, width), jnp.bfloat16),
            pltpu.VMEM((across, rows, width), jnp.bfloat16),
            pltpu.SemaphoreType.DMA((Reduce.SEMAPHORES,)),
            pltpu.SemaphoreType.DMA((Reduce.SEMAPHORES,)),
        ]

    def __init__(self, parts, held, passing, near, across, sends, arrivals, axis="ctx"):
        self.parts, self.held = parts, held
        self.passing, self.near, self.across = passing, near, across
        self.sends, self.arrivals = sends, arrivals
        self.places, self.peer = places_of(axis)
        _, self.up, self.down, _ = self.places[0]
        self.other = self.places[1][0]
        self.rows, self.width = near.shape[1], near.shape[2]
        self.half = self.rows // 2
        self.started = []

    def _send(self, slot, source, target, place):
        def copy():
            return remote(source(), target(), self.sends, self.arrivals, slot, self.peer(place))

        copy().start()
        self.started.append(copy)

    def _await(self, slot, ref):
        remote(ref, ref, self.sends, self.arrivals, slot, self.peer(self.other)).wait_recv()

    def begin(self):
        self.send_far()
        self.send_near(0)
        self.send_near(1)

    def send_far(self):
        for column in (1, 0):
            self._send_far(column)

    def _send_far(self, column):
        low, high = pl.ds(0, self.half), pl.ds(self.half, self.half)
        far = self.places[column][3]
        slot, a, b = 6 * column, 2 * column, 2 * column + 1
        parts, passing = self.parts, self.passing
        self._send(slot, lambda: parts.at[far, low], lambda: passing.at[a], self.up)
        self._send(slot + 1, lambda: parts.at[far, high], lambda: passing.at[b], self.down)

    def send_near(self, side):
        for column in (1, 0):
            self._send_near(column, side)

    def _send_near(self, column, side):
        half = pl.ds((1 - side) * self.half, self.half)
        toward, place = self.places[column][1 + side], (self.up, self.down)[side]
        index, parts, near = 2 * column + side, self.parts, self.near
        self._send(
            6 * column + 2 + side,
            lambda: parts.at[toward, half],
            lambda: near.at[index, half],
            place,
        )

    def pass_side(self, side):
        for column in (1, 0):
            self._pass_side(column, side)

    def _loop(self, rows, body):
        step = 16

        def run(i, carry):
            body(pl.multiple_of(i * step, step), step)
            return carry

        lax.fori_loop(0, rows // step, run, 0)

    def pass_on(self, column):
        self._pass_side(column, 0)
        self._pass_side(column, 1)

    def _pass_side(self, column, side):
        slot, index, start = 6 * column, 2 * column + side, side * self.half
        toward, place = self.places[column][1 + side], (self.up, self.down)[side]
        passing, near, held = self.passing, self.near, self.held
        self._await(slot + side, passing.at[index])

        def add(row, step):
            there = pl.ds(row, step)
            total = passing[index, there, :].astype(jnp.float32)
            total = total + held[toward, pl.ds(start + row, step), :].astype(jnp.float32)
            passing[index, there, :] = total.astype(jnp.bfloat16)

        self._loop(self.half, add)
        target = pl.ds(start, self.half)
        self._send(
            slot + 4 + side, lambda: passing.at[index], lambda: near.at[index, target], place
        )

    def _near(self, column):
        low, high = pl.ds(0, self.half), pl.ds(self.half, self.half)
        slot = 6 * column
        self._await(slot + 2, self.near.at[2 * column, high])
        self._await(slot + 3, self.near.at[2 * column + 1, low])
        self._await(slot + 4, self.near.at[2 * column, low])
        self._await(slot + 5, self.near.at[2 * column + 1, high])

    def _sum(self, column, there):
        place = self.places[column][0]
        total = self.held[place, there, :].astype(jnp.float32)
        total = total + self.near[2 * column, there, :].astype(jnp.float32)
        return total + self.near[2 * column + 1, there, :].astype(jnp.float32)

    def cross(self):
        self._near(1)
        place, held, across = self.places[1][0], self.held, self.across
        if across.shape[0] == 1:
            kept = lambda: held.at[place]
        else:
            kept = lambda: across.at[1]

        def add(row, step):
            there = pl.ds(row, step)
            kept()[there, :] = self._sum(1, there).astype(jnp.bfloat16)

        self._loop(self.rows, add)
        self._send(12, kept, lambda: across.at[0], self.other)

    def ready(self):
        self._near(0)
        self._await(12, self.across.at[0])

    def total(self, there):
        return self._sum(0, there) + self.across[0, there, :].astype(jnp.float32)

    def end(self):
        for copy in self.started:
            copy().wait_send()


class Spread:
    SEMAPHORES = 7 + 8

    def __init__(self, own, out, sends, arrivals):
        self.own, self.out, self.sends, self.arrivals = own, out, sends, arrivals
        self.me = lax.axis_index("shard")
        self.core, self.chip = lax.rem(self.me, 2), self.me // 2
        self.mate = {"shard": self.me + 1 - 2 * self.core}
        self.started = []

    def _send(self, slot, source, target, peer):
        copy = remote(source, target, self.sends, self.arrivals, slot, peer)
        copy.start()
        self.started.append(copy)

    def _await(self, slot, ref):
        remote(ref, ref, self.sends, self.arrivals, slot, self.mate).wait_recv()

    def _from(self, k, core):
        return self.out.at[2 * lax.rem(self.chip + CHIPS - k, CHIPS) + core]

    def peers(self):
        return [self.mate] + [
            {"shard": 2 * lax.rem(self.chip + k, CHIPS) + self.core} for k in range(1, CHIPS)
        ]

    def begin(self):
        target = self.out.at[self.me]
        for k in range(1, CHIPS):
            peer = {"shard": 2 * lax.rem(self.chip + k, CHIPS) + self.core}
            self._send(k - 1, self.own, target, peer)
        self._send(7, self.own, target, self.mate)

    def hand_on(self):
        for k in range(1, CHIPS):
            block = self._from(k, self.core)
            self._await(k - 1, block)
            self._send(7 + k, block, block, self.mate)

    def end(self):
        for k in range(CHIPS):
            self._await(7 + k, self._from(k, 1 - self.core))
        for copy in self.started:
            copy.wait_send()


def pick_copies(ffn_in, ffn_out, picked, sems):
    count = -(-HIDDEN_BLOCKS // N_CTX)
    place = lax.axis_index("ctx")
    copies = []
    for j in range(count):
        block = place * count + j
        block = block - (block // HIDDEN_BLOCKS) * (block - HIDDEN_BLOCKS + 1)
        routed = (block // SHARED_BLOCKS + 1) // 2
        rest = block - SHARED_BLOCKS
        expert = (rest + SHARED_BLOCKS * (1 - routed)) // EXPERT_BLOCKS * routed
        gate = block * (1 - routed) + (2 * SHARED_BLOCKS + EXPERT_BLOCKS * expert + rest) * routed
        up = gate + SHARED_BLOCKS * (1 - routed) + EXPERT_BLOCKS * routed
        for k, (source, at) in enumerate(((ffn_in, gate), (ffn_in, up), (ffn_out, block))):
            copies.append(
                pltpu.make_async_copy(
                    source.at[:, pl.ds(pl.multiple_of(at * LANE, LANE), LANE)],
                    picked.at[:, LANE * (count * k + j) : LANE * (count * k + j + 1)],
                    sems.at[3 * j + k],
                )
            )
    return copies


def assemble(out_share, gate_share, up_share, mixed_share, qkv_share):
    rows, hidden = out_share.shape[1:]
    width = mixed_share.shape[2]
    count = hidden // LANE
    spans = [(0, SHARED_BLOCKS)] + [
        (SHARED_BLOCKS + EXPERT_BLOCKS * e, EXPERT_BLOCKS) for e in range(EXPERTS)
    ]

    def moves(place, kind):
        result = []
        for index, (first, size) in enumerate(spans):
            low, high = max(first, count * place), min(first + size, count * (place + 1))
            if low >= high:
                continue
            there = low if kind == 0 else first + low + (kind - 1) * size
            result.append(((low - count * place) * LANE, there * LANE, (high - low) * LANE))
        return result

    jobs = []
    for place in range(N_CTX):
        for kind in range(3):
            jobs.append((kind, place, hidden, min(kind, 1), moves(place, kind)))
        jobs.append((3, place, width, 2, [(0, width * place, width)]))
        jobs.append(
            (4, place, 3 * width, 3, [(width * i, D * i + width * place, width) for i in range(3)])
        )
    depth = 4
    most = max(len(job[4]) for job in jobs)

    def kernel(*refs):
        shares, outs = refs[0:5], refs[5:9]
        low, full, loads, stores = refs[9:]

        def load(n):
            kind, place, size, _, _ = jobs[n]
            return pltpu.make_async_copy(
                shares[kind].at[place], low.at[n % depth, :, 0:size], loads.at[n % depth]
            )

        def store(n):
            _, _, _, to, spans_of = jobs[n]
            return [
                pltpu.make_async_copy(
                    full.at[n % depth, :, start : start + size],
                    outs[to].at[:, there : there + size],
                    stores.at[n % depth, k],
                )
                for k, (start, there, size) in enumerate(spans_of)
            ]

        for n in range(depth - 1):
            load(n).start()
        for n in range(len(jobs)):
            if n + depth - 1 < len(jobs):
                load(n + depth - 1).start()
            load(n).wait()
            if n >= depth:
                for copy in store(n - depth):
                    copy.wait()
            slot, size = n % depth, jobs[n][2]

            def widen(there, slot=slot, size=size):
                full[slot, there, 0:size] = low[slot, there, 0:size].astype(jnp.float32)

            by_rows(rows, widen)
            for copy in store(n):
                copy.start()
        for n in range(len(jobs) - depth, len(jobs)):
            for copy in store(n):
                copy.wait()

    f32 = jnp.float32
    return pl.pallas_call(
        kernel,
        out_shape=(
            jax.ShapeDtypeStruct((rows, FOUT), f32),
            jax.ShapeDtypeStruct((rows, FIN), f32),
            jax.ShapeDtypeStruct((rows, D), f32),
            jax.ShapeDtypeStruct((rows, 3 * D), f32),
        ),
        in_specs=[ANY] * 5,
        out_specs=(ANY,) * 4,
        scratch_shapes=[
            pltpu.VMEM((depth, rows, hidden), jnp.bfloat16),
            pltpu.VMEM((depth, rows, hidden), f32),
            pltpu.SemaphoreType.DMA((depth,)),
            pltpu.SemaphoreType.DMA((depth, most)),
        ],
        compiler_params=pltpu.CompilerParams(vmem_limit_bytes=60 << 20),
        name="assemble",
    )(out_share, gate_share, up_share, mixed_share, qkv_share)


def front(block, own_grad, qkv_weight, out_weight, ffn_in, ffn_out, small, cosines, sines, key_pos, query_pos):
    rows, width = qkv_weight.shape[0], out_weight.shape[1]
    n_shard = width // rows
    heads_width = width // N_CTX
    heads = heads_width // HEAD
    seq = rows * N_CTX
    extra = block.shape[1] - width
    tile = 256
    scale = HEAD ** (-0.5)
    hidden = -(-HIDDEN_BLOCKS // N_CTX) * LANE
    f32, bf16 = jnp.float32, jnp.bfloat16

    def kernel(
        block, own_grad, qkv_weight, out_weight, ffn_in, ffn_out, small, cosines, sines, key_pos,
        query_pos,
        residual, second_all, g_all, weights_out, small_all, first_out, ffn_weights, qkv, mixed, assigned,
        x_all, weights, first, staged, picked, params_all, parts, own, loads, picks, local, *scratch,
    ):
        gather = Gather(block, x_all, *scratch[0:2])
        spread = Spread(staged, weights, *scratch[2:4])
        spread_small = Spread(small, small_all, *scratch[4:6])
        gather_grad = Gather(own_grad, g_all, *scratch[6:8])
        gather_second = Gather(own, second_all, *scratch[8:10])
        gather_ffn = Gather(picked, ffn_weights, *scratch[10:12], axis="shard")
        reduce = Reduce(parts, parts, *scratch[12:17])
        me = gather.me
        loaded = [
            pltpu.make_async_copy(
                source.at[:, pl.ds(pl.multiple_of(start + heads_width * me, heads_width), heads_width)],
                staged.at[:, heads_width * i : heads_width * (i + 1)],
                loads.at[i],
            )
            for i, (source, start) in enumerate(
                ((qkv_weight, 0), (qkv_weight, width), (qkv_weight, 2 * width), (out_weight, 0))
            )
        ]
        for copy in loaded:
            copy.start()
        picking = pick_copies(ffn_in, ffn_out, picked, picks)
        for copy in picking:
            copy.start()
        greet([{"ctx": p} for p in (gather.other, gather.up, gather.down)] + spread.peers())
        gather.begin()
        spread_small.begin()
        for copy in loaded:
            copy.wait()
        spread.begin()
        for copy in picking:
            copy.wait()
        gather_ffn.begin()
        kept = [
            pltpu.make_async_copy(source, target, local.at[k])
            for k, (source, target) in enumerate(
                (
                    (block, x_all.at[me]),
                    (staged, weights.at[spread.me]),
                    (small, small_all.at[spread.me]),
                    (own_grad, g_all.at[me]),
                    (picked, ffn_weights.at[spread.chip, spread.core]),
                )
            )
        ]
        for copy in kept:
            copy.start()
        gather.pass_other()
        spread_small.hand_on()
        gather.pass_ring(0)
        spread.hand_on()
        gather.pass_ring(1)
        gather_grad.begin()
        spread_small.end()
        spread.end()
        gather.end()
        for copy in kept:
            copy.wait()
        gather_ffn.pass_other()
        weights_kept = pltpu.make_async_copy(weights, weights_out, local.at[0])
        weights_kept.start()
        assigned[...] = x_all[:, :, width:].reshape(seq, extra)
        params_all[...] = small_all[...].astype(f32)
        gains = [
            jnp.concatenate([params_all[s, k : k + 1, :] for s in range(n_shard)], axis=1)
            for k in range(2)
        ]
        per = heads_width // 128

        def bias_of(i):
            parts_of = []
            for j in range(per):
                at = n_shard * i + per * me + j
                parts_of.append(params_all[at // 3, pl.ds(3 + EXPERTS + lax.rem(at, 3), 1), :])
            return jnp.concatenate(parts_of, axis=1)

        biases = [bias_of(i) for i in range(3)]

        def project(n, carry):
            there = pl.ds(pl.multiple_of(n * tile, tile), tile)

            def norm(k, inner):
                inner_rows = pl.ds(pl.multiple_of(lax.rem(k, rows // 16) * 16, 16), 16)
                at = 2 * n + k // (rows // 16)
                normed, _ = normalize(x_all[at, inner_rows, 0:width].astype(f32))
                first[at, inner_rows, :] = (normed * gains[0]).astype(bf16)
                return inner

            lax.fori_loop(0, tile // 16, norm, 0)
            left = first[pl.ds(2 * n, 2)].reshape(tile, width)
            for i in range(3):
                columns = slice(heads_width * i, heads_width * (i + 1))
                made = biases[i] + jnp.dot(
                    left,
                    weights[:, :, columns].reshape(width, heads_width),
                    preferred_element_type=f32,
                )
                if i == 2:
                    qkv[there, columns] = made.astype(bf16)
                    continue
                for h in range(heads):
                    part = made[:, HEAD * h : HEAD * (h + 1)]
                    turned = part * cosines[there, :] + pltpu.roll(part, HEAD // 2, 1) * sines[there, :]
                    start = heads_width * i + HEAD * h
                    qkv[there, start : start + HEAD] = turned.astype(bf16)

            @pl.when(n == 1)
            def _():
                gather_grad.pass_other()

            return carry

        lax.fori_loop(0, seq // tile, project, 0)
        first_kept = pltpu.make_async_copy(first, first_out, local.at[1])
        first_kept.start()
        events = {
            0: lambda: gather_grad.pass_ring(0),
            1: lambda: gather_ffn.pass_ring(0),
            3: lambda: gather_grad.pass_ring(1),
            7: lambda: gather_ffn.pass_ring(1),
        }

        def attend(n, carry):
            head, i = n // (seq // tile), lax.rem(n, seq // tile)
            there = pl.ds(pl.multiple_of(i * tile, tile), tile)

            def lanes_of(start):
                return pl.ds(pl.multiple_of(start + HEAD * head, HEAD), HEAD)

            scores = scale * contract_last(qkv[:, lanes_of(heads_width)], qkv[there, lanes_of(0)])
            scores = jnp.where(key_pos[...] <= query_pos[:, there], scores, -1e30)
            raised = jnp.exp(scores - jnp.max(scores, axis=0, keepdims=True))
            probs = (raised * (1.0 / jnp.sum(raised, axis=0, keepdims=True))).astype(bf16)
            mixed[there, lanes_of(0)] = contract_first(
                probs, qkv[:, lanes_of(2 * heads_width)]
            ).astype(bf16)
            for at, event in events.items():
                pl.when(n == at)(event)
            return carry

        lax.fori_loop(0, heads * (seq // tile), attend, 0)

        def attended(k, carry):
            ahead = 2 - k + 3 * (k // 2) - 2 * (k // 3)
            at = lax.rem(me // 2 + ahead, N_CTX // 2) * 2
            left = mixed[pl.ds(pl.multiple_of(at * rows, tile), tile), :]
            blocks = 512 // rows
            for t in range(width // 512):
                right = weights[blocks * t : blocks * (t + 1), :, 3 * heads_width :]
                made = contract_last(left, right.reshape(512, heads_width)).astype(bf16)
                parts[pl.ds(at, 2), :, 512 * t : 512 * (t + 1)] = made.reshape(2, rows, 512)
            pl.when(k == 0)(reduce.send_far)
            pl.when(k == 1)(lambda: reduce.send_near(0))
            pl.when(k == 2)(lambda: reduce.send_near(1))
            return carry

        lax.fori_loop(0, 4, attended, 0)
        reduce.pass_side(0)
        reduce.pass_side(1)
        reduce.cross()
        reduce.ready()

        def norm_second(there):
            total = x_all[me, there, 0:width].astype(f32) + reduce.total(there)
            residual[there, :] = total
            normed, _ = normalize(total)
            own[there, :] = (normed * gains[1]).astype(bf16)

        by_rows(rows, norm_second)
        gather_second.begin()
        second_kept = pltpu.make_async_copy(own, second_all.at[me], local.at[2])
        second_kept.start()
        gather_second.pass_other()
        gather_second.pass_ring(0)
        gather_second.pass_ring(1)
        gather_grad.end()
        gather_ffn.end()
        reduce.end()
        for copy in (weights_kept, first_kept, second_kept):
            copy.wait()
        gather_second.end()

    def shape(*dims, kind=bf16):
        return jax.ShapeDtypeStruct(dims, kind)

    pair = [pltpu.SemaphoreType.DMA((Gather.SEMAPHORES,))] * 2
    spread_pair = [pltpu.SemaphoreType.DMA((Spread.SEMAPHORES,))] * 2
    return pl.pallas_call(
        kernel,
        out_shape=(
            shape(rows, width, kind=f32),
            shape(N_CTX, rows, width),
            shape(N_CTX, rows, width),
            shape(n_shard, rows, 4 * heads_width),
            shape(n_shard, 16, 128),
            shape(N_CTX, rows, width),
            shape(CHIPS, 2, rows, 3 * hidden),
            shape(seq, 3 * heads_width),
            shape(seq, heads_width),
            shape(seq, extra),
        ),
        in_specs=[ANY, VMEM] + [ANY] * 5 + [VMEM] * 4,
        out_specs=(VMEM, ANY, ANY, ANY, VMEM, ANY, ANY, VMEM, VMEM, VMEM),
        scratch_shapes=[
            pltpu.VMEM((N_CTX,) + block.shape, bf16),
            pltpu.VMEM((n_shard, rows, 4 * heads_width), bf16),
            pltpu.VMEM((N_CTX, rows, width), bf16),
            pltpu.VMEM((rows, 4 * heads_width), bf16),
            pltpu.VMEM((rows, 3 * hidden), bf16),
            pltpu.VMEM((n_shard, 16, 128), f32),
            pltpu.VMEM((N_CTX, rows, width), bf16),
            pltpu.VMEM((rows, width), bf16),
            pltpu.SemaphoreType.DMA((4,)),
            pltpu.SemaphoreType.DMA((3 * hidden // LANE,)),
            pltpu.SemaphoreType.DMA((5,)),
        ]
        + pair
        + spread_pair * 2
        + pair * 2
        + [pltpu.SemaphoreType.DMA((Gather.PAIRED,))] * 2
        + Reduce.scratch(rows, width, 1),
        compiler_params=params(0, 56 << 20),
        name="front",
    )(block, own_grad, qkv_weight, out_weight, ffn_in, ffn_out, small, cosines, sines, key_pos, query_pos)


def feed_forward(second, grad_out, assigned, ffn_weights, small, member, residual, own_grad, own_valid):
    _, rows, width = second.shape
    seq = rows * N_CTX
    hidden = ffn_weights.shape[1] // 3
    lanes = 128
    n_shard = small.shape[0]
    pair = 2 * rows
    tile = 256
    f32, bf16 = jnp.float32, jnp.bfloat16

    def kernel(
        second, grad_out, assigned, ffn_weights, small, member, residual, own_grad, own_valid,
        grad_residual, grad_low, output, grad_gain, grad_logits, act_out, grad_gu_out,
        second_held, grad_held, in_held, down_held, act, grad_gu, weights, dots, dots_in, gain_sum,
        logit_rows, logit_low,
        back_parts, ffn_parts, dot_sends, dot_arrivals, loads, weight_loads, stores, *scratch,
    ):
        back = Reduce(back_parts, back_parts, *scratch[:5])
        ahead = Reduce(ffn_parts, ffn_parts, *scratch[5:])
        own, other = back.places
        me = own[0]
        peers = [lax.rem(me + k, N_CTX) for k in range(1, N_CTX)]
        copies = [
            pltpu.make_async_copy(source, target, loads.at[k])
            for k, (source, target) in enumerate(((second, second_held), (grad_out, grad_held)))
        ]
        for copy in copies:
            copy.start()

        def weight_copies(t):
            copies = []
            for k, (target, there, here) in enumerate(
                ((in_held, 0, 0), (in_held, hidden, hidden), (down_held, 2 * hidden, 0))
            ):
                source = ffn_weights.at[:, pl.ds(pl.multiple_of(there + tile * t, tile), tile)]
                target = target.at[:, pl.ds(pl.multiple_of(here + tile * t, tile), tile)]
                copies.append(pltpu.make_async_copy(source, target, weight_loads.at[3 * t + k]))
            return copies

        def start_weights(t, carry):
            for copy in weight_copies(t):
                copy.start()
            return carry

        lax.fori_loop(0, hidden // tile, start_weights, 0)
        greet([{"ctx": p} for p in peers])
        logit_rows[...] = jnp.zeros_like(logit_rows)
        gains = []
        for s in range(n_shard):
            held = small[s].astype(f32)
            gains.append(held[1:2])
            logit_rows[0 : EXPERTS + 1, 128 * s : 128 * (s + 1)] = held[2 : 3 + EXPERTS]
        gain = jnp.concatenate(gains, axis=1)
        logit_low[...] = logit_rows[...].astype(bf16)
        for copy in copies:
            copy.wait()

        def stored(slot, start):
            there = pl.ds(start, pair)
            return [
                pltpu.make_async_copy(act.at[slot], act_out.at[there, :], stores.at[slot, 0]),
                pltpu.make_async_copy(grad_gu.at[slot], grad_gu_out.at[there, :], stores.at[slot, 1]),
            ]

        def dot_copy(slot, place):
            return remote(
                dots.at[place], dots_in.at[slot], dot_sends, dot_arrivals, slot, {"ctx": place}
            )

        def start_of(b):
            ahead = 2 - b + 3 * (b // 2) - 2 * (b // 3)
            return pl.multiple_of(lax.rem(me // 2 + ahead, N_CTX // 2) * pair, pair)

        def block(b, carry):
            start = start_of(b)
            slot = lax.rem(b, 2)
            first = pl.multiple_of(start // rows, 2)

            @pl.when(b >= 2)
            def _():
                for copy in stored(slot, start_of(b - 2)):
                    copy.wait()

            def rows_of(ref):
                return ref[pl.ds(first, 2)].reshape(pair, width)

            logits = contract_last(rows_of(second_held), logit_low[...])
            lane = lax.broadcasted_iota(jnp.int32, logits.shape, 1)
            named = assigned[pl.ds(start, pair), :] > 0
            raised = jnp.where(named, logits, -1e30)
            raised = jnp.exp(raised - jnp.max(raised, axis=-1, keepdims=True))
            raised = jnp.where(named, raised, 0.0)
            gates = raised / jnp.sum(raised, axis=-1, keepdims=True)
            gates = jnp.where(lane == EXPERTS, jax.nn.sigmoid(logits), gates)
            weights[pl.ds(start, pair), :] = gates
            dots[pl.ds(first, 2)] = jnp.zeros((2, rows, lanes), f32)

            def hidden_tile(t, carry):
                @pl.when(b == 0)
                def _():
                    for copy in weight_copies(t):
                        copy.wait()

                low = pl.ds(pl.multiple_of(tile * t, tile), tile)
                high = pl.ds(pl.multiple_of(hidden + tile * t, tile), tile)
                rows_in = rows_of(second_held)
                gate = jnp.dot(rows_in, in_held[:, low], preferred_element_type=f32)
                upward = jnp.dot(rows_in, in_held[:, high], preferred_element_type=f32)
                raw = jnp.dot(rows_of(grad_held), down_held[:, low], preferred_element_type=f32)
                held = jnp.dot(
                    weights[pl.ds(start, pair), :],
                    member[:, low],
                    precision=highest,
                    preferred_element_type=f32,
                )
                squashed = jax.nn.sigmoid(gate)
                swished = gate * squashed
                value = swished * upward
                act[slot, :, low] = (value * held).astype(bf16)
                part = lax.dot_general(
                    raw * value,
                    member[:, low],
                    (((1,), (1,)), ((), ())),
                    precision=highest,
                    preferred_element_type=f32,
                )
                dots[pl.ds(first, 2)] += part.reshape(2, rows, lanes)
                grad = raw * held
                grad_gu[slot, :, low] = (
                    grad * upward * squashed * (1.0 + gate * (1.0 - squashed))
                ).astype(bf16)
                grad_gu[slot, :, high] = (grad * swished).astype(bf16)
                return carry

            lax.fori_loop(0, hidden // tile, hidden_tile, 0)
            for copy in stored(slot, start):
                copy.start()

            def out_tile(t, carry):
                there = pl.ds(pl.multiple_of(512 * t, 512), 512)
                for parts, left, right in (
                    (back_parts, grad_gu, in_held),
                    (ffn_parts, act, down_held),
                ):
                    made = contract_last(left[slot], right[there, :])
                    parts[pl.ds(first, 2), :, there] = made.astype(bf16).reshape(2, rows, 512)
                return carry

            lax.fori_loop(0, width // 512, out_tile, 0)

            def far():
                back.send_far()
                ahead.send_far()
                dot_copy(0, own[3]).start()
                dot_copy(1, other[3]).start()

            def near(side):
                back.send_near(side)
                back.pass_side(side)
                ahead.send_near(side)
                ahead.pass_side(side)
                dot_copy(2 + 2 * side, own[1 + side]).start()
                dot_copy(3 + 2 * side, other[1 + side]).start()

            pl.when(b == 0)(far)
            pl.when(b == 1)(lambda: near(0))
            pl.when(b == 2)(lambda: near(1))
            return carry

        lax.fori_loop(0, 4, block, 0)
        dot_copy(6, other[0]).start()
        back.cross()
        ahead.cross()
        back.ready()
        for k in range(7):
            ref = dots_in.at[k]
            remote(ref, ref, dot_sends, dot_arrivals, k, {"ctx": other[0]}).wait_recv()
        total_dots = dots[me]
        for k in range(7):
            total_dots = total_dots + dots_in[k]
        held = weights[pl.ds(pl.multiple_of(me * rows, rows), rows), :]
        lane = lax.broadcasted_iota(jnp.int32, held.shape, 1)
        routed = lane < EXPERTS
        centre = jnp.sum(jnp.where(routed, held * total_dots, 0.0), axis=-1, keepdims=True)
        both = jnp.where(
            routed,
            held * (total_dots - centre),
            jnp.where(lane == EXPERTS, total_dots * held * (1.0 - held), 0.0),
        )
        grad_logits[...] = both
        grad_residual[...] = jnp.dot(
            both, logit_rows[...], precision=highest, preferred_element_type=f32
        )
        gain_sum[...] = jnp.zeros_like(gain_sum)

        def norm(there):
            normed, factor = normalize(residual[there, :])
            grad = back.total(there) + grad_residual[there, :]
            gain_sum[...] += grad * normed
            grad = own_grad[there, :].astype(f32) + norm_back(grad, normed, factor, gain)
            grad_residual[there, :] = grad
            grad_low[there, :] = grad.astype(bf16)

        by_rows(rows, norm)
        grad_gain[...] = jnp.sum(gain_sum[...], axis=0, keepdims=True)
        ahead.ready()

        def finish(there):
            total = residual[there, :] + ahead.total(there)
            output[there, :] = (total * own_valid[there, :]).astype(bf16)

        by_rows(rows, finish)
        for b in (2, 3):
            for copy in stored(b % 2, start_of(b)):
                copy.wait()
        back.end()
        ahead.end()
        for slot, place in enumerate((own[3], other[3], own[1], other[1], own[2], other[2], other[0])):
            dot_copy(slot, place).wait_send()

    return pl.pallas_call(
        kernel,
        out_shape=(
            jax.ShapeDtypeStruct((rows, width), f32),
            jax.ShapeDtypeStruct((rows, width), bf16),
            jax.ShapeDtypeStruct((rows, width), bf16),
            jax.ShapeDtypeStruct((1, width), f32),
            jax.ShapeDtypeStruct((rows, lanes), f32),
            jax.ShapeDtypeStruct((seq, hidden), bf16),
            jax.ShapeDtypeStruct((seq, 2 * hidden), bf16),
        ),
        in_specs=[ANY, ANY, VMEM, ANY] + [VMEM] * 5,
        out_specs=(VMEM,) * 5 + (ANY, ANY),
        scratch_shapes=[
            pltpu.VMEM(second.shape, bf16),
            pltpu.VMEM(grad_out.shape, bf16),
            pltpu.VMEM((width, 2 * hidden), bf16),
            pltpu.VMEM((width, hidden), bf16),
            pltpu.VMEM((2, pair, hidden), bf16),
            pltpu.VMEM((2, pair, 2 * hidden), bf16),
            pltpu.VMEM((seq, lanes), f32),
            pltpu.VMEM((N_CTX, rows, lanes), f32),
            pltpu.VMEM((N_CTX - 1, rows, lanes), f32),
            pltpu.VMEM((16, width), f32),
            pltpu.VMEM((lanes, width), f32),
            pltpu.VMEM((lanes, width), bf16),
            pltpu.VMEM(second.shape, bf16),
            pltpu.VMEM(second.shape, bf16),
            pltpu.SemaphoreType.DMA((N_CTX - 1,)),
            pltpu.SemaphoreType.DMA((N_CTX - 1,)),
            pltpu.SemaphoreType.DMA((2,)),
            pltpu.SemaphoreType.DMA((3 * hidden // tile,)),
            pltpu.SemaphoreType.DMA((2, 2)),
        ]
        + Reduce.scratch(rows, width, 1) * 2,
        compiler_params=params(2, 64 << 20),
        name="feed_forward",
    )(second, grad_out, assigned, ffn_weights, small, member, residual, own_grad, own_valid)


class Exchange:
    @staticmethod
    def scratch():
        return [pltpu.SemaphoreType.DMA((CHIPS,)), pltpu.SemaphoreType.DMA((CHIPS,))]

    def __init__(self, parts, staged, sends, arrivals):
        self.parts, self.staged = parts, staged
        self.sems = (sends, arrivals)
        self.width = parts.shape[2]
        me = lax.axis_index("shard")
        self.core, self.chip = lax.rem(me, 2), me // 2
        self.mate = {"shard": me + 1 - 2 * self.core}

    def chip_at(self, step):
        base = self.chip + (1 - lax.rem(step, 2)) * (1 - 2 * lax.rem(self.chip, 2))
        b = step // 2
        ahead = 2 - b + 3 * (b // 2) - 2 * (b // 3)
        return 2 * lax.rem(base // 2 + ahead, 4) + lax.rem(base, 2)

    def _pair(self, step):
        return remote(
            self.staged.at[lax.rem(step, 2), 1 - self.core, :, pl.ds(0, self.width)],
            self.parts.at[self.chip_at(step)],
            *self.sems,
            step,
            self.mate,
        )

    def finish(self, step):
        chip, slot, width = self.chip_at(step), lax.rem(step, 2), self.width
        ref = self.parts.at[chip]
        remote(ref, ref, *self.sems, step, self.mate).wait_recv()

        def add(there):
            total = self.parts[chip, there, :].astype(jnp.float32)
            total = total + self.staged[slot, self.core, there, 0:width].astype(jnp.float32)
            self.parts[chip, there, :] = total.astype(jnp.bfloat16)

        by_rows(128, add)

    def run(self, left, right, turned, between):
        width = self.width
        tile = 896 if width % 896 == 0 else width

        def step_of(step, carry):
            @pl.when(step >= 2)
            def _():
                self._pair(step - 2).wait_send()

            slot = lax.rem(step, 2)
            columns = pl.ds(pl.multiple_of(self.chip_at(step) * 256, 256), 256)
            turned[...] = left[:, :, columns].reshape(turned.shape[1], 256).T
            for start in range(0, width, tile):
                made = jnp.dot(
                    turned[...], right(start, tile), preferred_element_type=jnp.float32
                ).astype(jnp.bfloat16)
                self.staged[slot, 0, :, start : start + tile] = made[:128]
                self.staged[slot, 1, :, start : start + tile] = made[128:]
            self._pair(step).start()

            @pl.when(step >= 1)
            def _():
                self.finish(step - 1)

            for at, events in between.items():

                @pl.when(step == at)
                def _(events=events):
                    for event in events:
                        event()

            return carry

        lax.fori_loop(0, CHIPS, step_of, 0)
        self.finish(CHIPS - 1)
        for step in (CHIPS - 2, CHIPS - 1):
            self._pair(step).wait_send()


class Share:
    @staticmethod
    def scratch(width):
        return (
            [pltpu.VMEM((CHIPS, 128, width), jnp.bfloat16), pltpu.VMEM((128, width), jnp.bfloat16)]
            + Exchange.scratch()
            + Reduce.scratch(128, width, 1)
            + [pltpu.SemaphoreType.DMA((Gather.SEMAPHORES,))] * 2
            + [pltpu.SemaphoreType.DMA]
        )

    COUNT = 2 + 2 + 5 + 2 + 1

    def __init__(self, staged, out, scratch):
        parts, self.owned = scratch[0:2]
        self.exchange = Exchange(parts, staged, *scratch[2:4])
        self.reduce = Reduce(parts, parts, *scratch[4:9], axis="shard")
        self.gather = Gather(self.owned, out, *scratch[9:11])
        self.local = scratch[11]

    def near(self, side):
        return lambda: self.reduce.send_near(side)

    def side(self, side):
        return lambda: self.reduce.pass_side(side)

    def ring(self, column):
        return lambda: self.gather.pass_ring(column)

    def own(self):
        self.reduce.ready()

        def keep(there):
            self.owned[there, :] = self.reduce.total(there).astype(jnp.bfloat16)

        by_rows(128, keep)
        self.gather.begin()
        self._kept().start()

    def _kept(self):
        return pltpu.make_async_copy(
            self.owned, self.gather.out.at[self.gather.me], self.local
        )

    def end(self):
        self._kept().wait()
        self.gather.end()
        self.reduce.end()


def backward(own, second, grad_out, grad_gu, act, qkv, mixed, weights, first, cosines, sines, key_pos, query_pos, inputs, grad_residual, gain, second_gain_grad, grad_logits):
    rows, width = own.shape
    seq = rows * N_CTX
    hidden = act.shape[1]
    heads_width = mixed.shape[1]
    heads = heads_width // HEAD
    lanes = grad_logits.shape[1]
    n_shard = width // 128
    f32, bf16 = jnp.float32, jnp.bfloat16
    scale = HEAD ** (-0.5)
    tile = 256
    half = width // 2

    def kernel(
        own, second, grad_out, grad_gu, act, qkv, mixed, weights, first, cosines, sines, key_pos,
        query_pos, inputs, grad_residual, gain, second_gain_grad, grad_logits,
        input_grad, small_out, grad_attended, out_share, gate_share, up_share, mixed_share, qkv_share,
        second_held, g_held, gu_held, act_held, turned, staged, key_sum, value_sum, gain_sum,
        small, small_in, small_kept, small_across,
        loads, local, small_sends, small_arrivals, across_sends, across_arrivals, *scratch,
    ):
        gather = Gather(own, grad_attended, *scratch[0:2])
        reduce = Reduce(g_held, g_held, *scratch[2:7])
        shares = []
        for k, out in enumerate((out_share, gate_share, up_share, mixed_share, qkv_share)):
            start = 7 + Share.COUNT * k
            shares.append(Share(staged, out, scratch[start : start + Share.COUNT]))
        a, b, c, d, e = shares
        me = gather.me
        shard = lax.axis_index("shard")
        owners = [lax.rem(shard + k, n_shard) for k in range(1, n_shard)]
        places = [lax.rem(me + k, N_CTX) for k in range(1, N_CTX)]

        def load(k, source, target):
            return pltpu.make_async_copy(source, target, loads.at[k])

        early = [
            load(0, grad_out, g_held),
            load(1, act, act_held),
            load(2, second, second_held),
            load(3, grad_gu, gu_held),
        ]
        for copy in early:
            copy.start()
        greet([{"ctx": p} for p in places] + [{"shard": s} for s in owners])
        gather.begin()
        kept = pltpu.make_async_copy(own, grad_attended.at[me], local)
        kept.start()
        early[0].wait()
        early[1].wait()
        a.exchange.run(
            g_held,
            lambda start, count: act_held[:, start : start + count],
            turned,
            {
                2: [a.reduce.send_far],
                4: [a.near(0)],
                6: [a.near(1), gather.pass_other],
            },
        )
        early[2].wait()
        early[3].wait()
        b.exchange.run(
            second_held,
            lambda start, count: gu_held[:, start : start + count],
            turned,
            {
                0: [a.side(0)],
                1: [a.side(1)],
                2: [b.reduce.send_far],
                3: [lambda: gather.pass_ring(0)],
                4: [b.near(0)],
                6: [b.near(1), lambda: gather.pass_ring(1)],
            },
        )
        c.exchange.run(
            second_held,
            lambda start, count: gu_held[:, hidden + start : hidden + start + count],
            turned,
            {
                2: [c.reduce.send_far],
                4: [c.near(0)],
                5: [a.reduce.cross],
                6: [c.near(1)],
                7: [b.side(0)],
            },
        )
        logits_grad = lax.dot_general(
            grad_logits[...],
            second_held[me].astype(f32),
            (((0,), (0,)), ((), ())),
            precision=highest,
            preferred_element_type=f32,
        )
        small[...] = jnp.zeros_like(small)
        for s in range(n_shard):
            there = slice(128 * s, 128 * (s + 1))
            small[s, 1:2, :] = second_gain_grad[:, there]
            small[s, 2 : 3 + EXPERTS, :] = logits_grad[: EXPERTS + 1, there]
        kept.wait()
        gather.end()
        late = [
            load(0, grad_attended, g_held),
            load(1, weights.at[pl.ds(0, half), :], gu_held.at[:, 0:half]),
            load(2, weights.at[pl.ds(half, half), :], gu_held.at[:, half : 2 * half]),
            load(3, qkv, gu_held.at[:, 2 * half : 2 * half + 3 * heads_width]),
            load(
                4,
                mixed,
                gu_held.at[:, 2 * half + 3 * heads_width : 2 * half + 4 * heads_width],
            ),
            load(5, first, second_held),
        ]
        for copy in late:
            copy.start()
        b.side(1)()
        a.own()
        for copy in late:
            copy.wait()
        columns_qkv = 2 * half
        columns_mixed = columns_qkv + 3 * heads_width
        columns_grad = columns_mixed + heads_width
        w_out = [3 * heads_width, half + 3 * heads_width]

        def grad_mixed(i, carry):
            first_block = 2 * i
            there = pl.ds(pl.multiple_of(i * tile, tile), tile)
            left = g_held[pl.ds(first_block, 2)].reshape(tile, width)
            made = jnp.dot(
                left[:, :half],
                gu_held[:, w_out[0] : w_out[0] + heads_width],
                preferred_element_type=f32,
            ) + jnp.dot(
                left[:, half:],
                gu_held[:, w_out[1] : w_out[1] + heads_width],
                preferred_element_type=f32,
            )
            gu_held[there, columns_grad : columns_grad + heads_width] = made.astype(bf16)
            return carry

        lax.fori_loop(0, seq // tile, grad_mixed, 0)
        d.exchange.run(
            g_held,
            lambda start, count: gu_held[:, columns_mixed + start : columns_mixed + start + count],
            turned,
            {
                2: [d.reduce.send_far],
                4: [d.near(0)],
                6: [d.near(1)],
            },
        )
        events = {
            0: [a.gather.pass_other],
            1: [b.reduce.cross],
            2: [a.ring(0)],
            3: [d.side(0), d.side(1)],
            4: [b.own],
            5: [a.ring(1), c.side(0)],
            6: [c.side(1)],
            7: [d.reduce.cross],
        }

        def attend(n, carry):
            head, i = n // (seq // tile), lax.rem(n, seq // tile)
            there = pl.ds(pl.multiple_of(i * tile, tile), tile)

            def lanes_of(start):
                return pl.ds(pl.multiple_of(start + HEAD * head, HEAD), HEAD)

            query = gu_held[there, lanes_of(columns_qkv)]
            key = gu_held[:, lanes_of(columns_qkv + heads_width)]
            value = gu_held[:, lanes_of(columns_qkv + 2 * heads_width)]
            grad = gu_held[there, lanes_of(columns_grad)]
            scores = contract_last(key, query) * scale
            scores = jnp.where(key_pos[...] <= query_pos[:, there], scores, -1e30)
            raised = jnp.exp(scores - jnp.max(scores, axis=0, keepdims=True))
            probs = raised * (1.0 / jnp.sum(raised, axis=0, keepdims=True))
            grad_probs = contract_last(value, grad)
            centre = jnp.sum(probs * grad_probs, axis=0, keepdims=True)
            grad_scores = (probs * (grad_probs - centre)).astype(bf16)

            @pl.when(i == 0)
            def _():
                key_sum[...] = jnp.zeros_like(key_sum)
                value_sum[...] = jnp.zeros_like(value_sum)

            key_sum[...] += jnp.dot(grad_scores, query, preferred_element_type=f32)
            value_sum[...] += jnp.dot(probs.astype(bf16), grad, preferred_element_type=f32)
            grad_query = contract_first(grad_scores, key) * scale

            def turn_back(values, cosines, sines):
                return (values * cosines - pltpu.roll(values, HEAD // 2, 1) * sines).astype(bf16)

            act_held[there, lanes_of(0)] = turn_back(
                grad_query, cosines[there, :], sines[there, :]
            )

            @pl.when(i == seq // tile - 1)
            def _():
                act_held[:, lanes_of(heads_width)] = turn_back(
                    key_sum[...] * scale, cosines[...], sines[...]
                )
                act_held[:, lanes_of(2 * heads_width)] = value_sum[...].astype(bf16)

            for at, todo in events.items():

                @pl.when(n == at)
                def _(todo=todo):
                    for event in todo:
                        event()

            return carry

        lax.fori_loop(0, heads * (seq // tile), attend, 0)

        def start_of(k):
            ahead = 2 - k + 3 * (k // 2) - 2 * (k // 3)
            return lax.rem(me // 2 + ahead, N_CTX // 2) * 2

        def grad_first(k, carry):
            block = start_of(k)
            left = act_held[pl.ds(pl.multiple_of(block * rows, tile), tile), 0 : 3 * heads_width]
            for t in range(4):
                low = 512 * (t % 2)
                start = half * (t // 2)
                made = contract_last(left, gu_held[low : low + 512, start : start + 3 * heads_width])
                g_held[pl.ds(block, 2), :, 512 * t : 512 * (t + 1)] = made.astype(bf16).reshape(
                    2, rows, 512
                )
            pl.when(k == 0)(reduce.send_far)
            pl.when(k == 1)(lambda: reduce.send_near(0))
            pl.when(k == 2)(lambda: reduce.send_near(1))
            return carry

        lax.fori_loop(0, 4, grad_first, 0)
        b.gather.pass_other()
        e.exchange.run(
            second_held,
            lambda start, count: act_held[:, start : start + count],
            turned,
            {
                1: [lambda: reduce.pass_side(0)],
                2: [e.reduce.send_far, lambda: reduce.pass_side(1)],
                3: [b.ring(0)],
                4: [e.near(0), c.reduce.cross],
                6: [e.near(1), c.own],
                7: [b.ring(1), reduce.cross],
            },
        )
        e.side(0)()
        e.side(1)()
        d.own()
        bias = jnp.sum(act_held[:, 0 : 3 * heads_width].astype(f32), axis=0, keepdims=True)
        per = heads_width // 128
        for i in range(3):
            for j in range(per):
                block = n_shard * i + per * me + j
                there = slice(heads_width * i + 128 * j, heads_width * i + 128 * (j + 1))
                small[block // 3, pl.ds(3 + EXPERTS + lax.rem(block, 3), 1), :] = bias[:, there]
        e.reduce.cross()
        c.gather.pass_other()
        d.gather.pass_other()
        reduce.ready()
        gain_sum[...] = jnp.zeros_like(gain_sum)

        def norm(there):
            normed, factor = normalize(inputs[there, :].astype(f32))
            grad = reduce.total(there)
            gain_sum[...] += grad * normed
            input_grad[there, :] = grad_residual[there, :] + norm_back(
                grad, normed, factor, gain[...]
            )

        by_rows(rows, norm)
        first_gain_grad = jnp.sum(gain_sum[...], axis=0, keepdims=True)
        for s in range(n_shard):
            small[s, 0:1, :] = first_gain_grad[:, 128 * s : 128 * (s + 1)]
        to_owners = [
            remote(small.at[s], small_in.at[k], small_sends, small_arrivals, k, {"shard": s})
            for k, s in enumerate(owners)
        ]
        for copy in to_owners:
            copy.start()
        e.own()
        c.ring(0)()
        d.ring(0)()
        total = small[shard]
        for k, copy in enumerate(to_owners):
            copy.wait_recv()
            total = total + small_in[k]
        small_kept[...] = total
        to_places = [
            remote(small_kept, small_across.at[k], across_sends, across_arrivals, k, {"ctx": p})
            for k, p in enumerate(places)
        ]
        for copy in to_places:
            copy.start()
        e.gather.pass_other()
        c.ring(1)()
        d.ring(1)()
        e.ring(0)()
        e.ring(1)()
        for k, copy in enumerate(to_places):
            copy.wait_recv()
            total = total + small_across[k]
        small_out[...] = total
        for copy in to_owners + to_places:
            copy.wait_send()
        reduce.end()
        for share in shares:
            share.end()

    def shared(count):
        return jax.ShapeDtypeStruct((N_CTX, 128, count), bf16)

    return pl.pallas_call(
        kernel,
        out_shape=(
            jax.ShapeDtypeStruct((rows, width), f32),
            jax.ShapeDtypeStruct((16, 128), f32),
            jax.ShapeDtypeStruct((N_CTX, rows, width), bf16),
            shared(hidden),
            shared(hidden),
            shared(hidden),
            shared(heads_width),
            shared(3 * heads_width),
        ),
        in_specs=[VMEM] + [ANY] * 8 + [VMEM] * 9,
        out_specs=(VMEM, VMEM) + (ANY,) * 6,
        scratch_shapes=[
            pltpu.VMEM(second.shape, bf16),
            pltpu.VMEM(grad_out.shape, bf16),
            pltpu.VMEM(grad_gu.shape, bf16),
            pltpu.VMEM(act.shape, bf16),
            pltpu.VMEM((256, seq), bf16),
            pltpu.VMEM((2, 2, 128, hidden), bf16),
            pltpu.VMEM((seq, HEAD), f32),
            pltpu.VMEM((seq, HEAD), f32),
            pltpu.VMEM((16, width), f32),
            pltpu.VMEM((n_shard, 16, 128), f32),
            pltpu.VMEM((n_shard - 1, 16, 128), f32),
            pltpu.VMEM((16, 128), f32),
            pltpu.VMEM((N_CTX - 1, 16, 128), f32),
            pltpu.SemaphoreType.DMA((6,)),
            pltpu.SemaphoreType.DMA,
            pltpu.SemaphoreType.DMA((n_shard - 1,)),
            pltpu.SemaphoreType.DMA((n_shard - 1,)),
            pltpu.SemaphoreType.DMA((N_CTX - 1,)),
            pltpu.SemaphoreType.DMA((N_CTX - 1,)),
        ]
        + [pltpu.SemaphoreType.DMA((Gather.SEMAPHORES,))] * 2
        + Reduce.scratch(rows, width, 1)
        + Share.scratch(hidden) * 3
        + Share.scratch(heads_width)
        + Share.scratch(3 * heads_width),
        compiler_params=params(3, 64 << 20),
        name="backward",
    )(own, second, grad_out, grad_gu, act, qkv, mixed, weights, first, cosines, sines, key_pos, query_pos, inputs, grad_residual, gain, second_gain_grad, grad_logits)


def local(
    tokens,
    cotangent,
    lengths,
    routes,
    block_order,
    norm_gains,
    qkv_weight,
    qkv_bias,
    out_weight,
    router,
    shared_gate,
    ffn_in,
    ffn_out,
):
    bf16, f32 = jnp.bfloat16, jnp.float32
    n_ctx = lax.axis_size("ctx")
    n_shard = lax.axis_size("shard")
    rows_dev = tokens.shape[1]
    seq_len = rows_dev * n_ctx
    n_blocks = block_order.shape[0]
    block = seq_len // n_blocks
    hidden_blocks = -(-HIDDEN_BLOCKS // n_ctx)
    place = lax.axis_index("ctx")

    every = jnp.arange(seq_len, dtype=jnp.int32)
    matches = (every // block)[:, None] == jnp.arange(n_blocks, dtype=jnp.int32)[None, :]
    pos = jnp.sum(jnp.where(matches, block_order[None, :], 0), axis=1) * block + every % block
    valid = pos < lengths[0]
    valid_rows = valid.astype(f32)[:, None]

    own_valid = lax.dynamic_slice_in_dim(valid_rows, place * rows_dev, rows_dev)
    own_grad = jnp.where(own_valid > 0, cotangent[0], 0).astype(bf16)
    picks = routes[0][:, :, None] == jnp.arange(LANE, dtype=jnp.int32)[None, None, :]
    own_assigned = jnp.sum(picks.astype(f32), axis=1).astype(bf16)
    small = jnp.concatenate(
        [
            norm_gains,
            router.T,
            shared_gate.reshape(1, LANE),
            qkv_bias.reshape(3, LANE),
            jnp.zeros((4, LANE), bf16),
        ]
    )
    cosines, sines = rope_tables(pos)
    key_pos = jnp.where(valid, pos, 2 * seq_len)[:, None]
    (
        residual,
        second_all,
        g_all,
        attn_weights,
        small_all,
        first_all,
        ffn_weights,
        qkv,
        mixed,
        assigned,
    ) = front(
        jnp.concatenate([tokens[0], own_assigned], axis=1),
        own_grad,
        qkv_weight,
        out_weight,
        ffn_in,
        ffn_out,
        small,
        cosines,
        sines,
        key_pos,
        pos[None],
    )

    block_ids = hidden_blocks * place + jnp.arange(hidden_blocks, dtype=jnp.int32)
    branch_of = jnp.where(
        block_ids < SHARED_BLOCKS, EXPERTS, (block_ids - SHARED_BLOCKS) // EXPERT_BLOCKS
    )
    member = (
        (branch_of[None, :] == jnp.arange(LANE, dtype=jnp.int32)[:, None])
        & (block_ids < HIDDEN_BLOCKS)[None, :]
    ).astype(f32)
    member = jnp.repeat(member, LANE, axis=1)
    grad_residual, grad_low, output, grad_second_gain, grad_both, act_low, grad_gu = feed_forward(
        second_all,
        g_all,
        assigned,
        ffn_weights.reshape(D, -1),
        small_all,
        member,
        residual,
        own_grad,
        own_valid,
    )
    first_gain = small_all[:, 0, :].reshape(1, D).astype(f32)
    input_grad, own_small, _, out_share, gate_share, up_share, mixed_share, qkv_share = backward(
        grad_low,
        second_all,
        g_all,
        grad_gu,
        act_low,
        qkv,
        mixed,
        attn_weights.reshape(D, -1),
        first_all,
        cosines,
        sines,
        key_pos,
        pos[None],
        tokens[0],
        grad_residual,
        first_gain,
        grad_second_gain,
        grad_both,
    )
    own_small = own_small.reshape(-1)
    grad_gains = own_small[: 2 * LANE].reshape(2, LANE)
    grad_router = own_small[2 * LANE : 8 * LANE].reshape(EXPERTS, LANE).T
    grad_shared_gate = own_small[8 * LANE : 9 * LANE]
    grad_bias_out = own_small[9 * LANE : 12 * LANE]

    grad_ffn_out, grad_ffn_in, grad_out, grad_qkv = assemble(
        out_share, gate_share, up_share, mixed_share, qkv_share
    )
    return (
        output[None],
        input_grad[None],
        grad_gains,
        grad_qkv,
        grad_bias_out,
        grad_out,
        grad_router,
        grad_shared_gate,
        grad_ffn_in,
        grad_ffn_out,
    )


def solution(mesh):
    placed = (
        P("shard", "ctx", None),
        P("shard", "ctx", None),
        P("shard"),
        P("shard", "ctx", None),
        P(),
        P(None, "shard"),
        P("shard", None),
        P("shard"),
        P("shard", None),
        P("shard", None),
        P("shard"),
        P("shard", None),
        P("shard", None),
    )
    return jax.shard_map(
        local,
        mesh=mesh,
        in_specs=placed,
        out_specs=(
            P("shard", "ctx", None),
            P("shard", "ctx", None),
            P(None, "shard"),
            P("shard", None),
            P("shard"),
            P("shard", None),
            P("shard", None),
            P("shard"),
            P("shard", None),
            P("shard", None),
        ),
        check_vma=False,
    )
```

```python
import jax
import jax.numpy as jnp
from jax import lax
from jax.experimental import pallas as pl
from jax.experimental.pallas import tpu as pltpu
from jax.sharding import PartitionSpec as P

D = 2048
HEAD = 128
HE = 1408
FS = 5632
EXPERTS = 6
FIN = 28160
FOUT = 14080
LANE = 128
SHARED_BLOCKS = FS // LANE
EXPERT_BLOCKS = HE // LANE
HIDDEN_BLOCKS = SHARED_BLOCKS + EXPERTS * EXPERT_BLOCKS

highest = lax.Precision.HIGHEST
epsilon = 1e-06
rope_base = 1000000.0


def contract_last(left, right):
    return lax.dot_general(
        left, right, (((1,), (1,)), ((), ())), preferred_element_type=jnp.float32
    )


def contract_first(left, right):
    return lax.dot_general(
        left, right, (((0,), (0,)), ((), ())), preferred_element_type=jnp.float32
    )


def dot(left, right):
    return jnp.dot(left, right, preferred_element_type=jnp.float32)


def rope_tables(positions):
    half = HEAD // 2
    freqs = rope_base ** (-jnp.arange(half, dtype=jnp.float32) * 2.0 / HEAD)
    phase = positions.astype(jnp.float32)[:, None] * freqs[None, :]
    cosines, sines = jnp.cos(phase), jnp.sin(phase)
    return (
        jnp.concatenate([cosines, cosines], axis=1),
        jnp.concatenate([-sines, sines], axis=1),
    )


def normalize(values):
    factor = lax.rsqrt(jnp.mean(values * values, axis=-1, keepdims=True) + epsilon)
    return (values * factor, factor)


def norm_back(grad_normed, normalized, factor, gain):
    scaled = grad_normed * gain
    return factor * (scaled - normalized * jnp.mean(scaled * normalized, axis=-1, keepdims=True))


MESH = pl.DeviceIdType.MESH
ANY = pl.BlockSpec(memory_space=pl.ANY)
VMEM = pl.BlockSpec(memory_space=pltpu.VMEM)
N_CTX = 8
CHIPS = 8
AFTER = 512


def params(number, limit=None):
    return pltpu.CompilerParams(
        collective_id=number, has_side_effects=True, vmem_limit_bytes=limit
    )


def greet(peers):
    semaphore = pltpu.get_barrier_semaphore()
    for peer in peers:
        pl.semaphore_signal(semaphore, inc=1, device_id=peer, device_id_type=MESH)
    pl.semaphore_wait(semaphore, len(peers))


def remote(source, target, sends, arrivals, slot, peer):
    return pltpu.make_async_remote_copy(
        src_ref=source,
        dst_ref=target,
        send_sem=sends.at[slot],
        recv_sem=arrivals.at[slot],
        device_id=peer,
        device_id_type=MESH,
    )


def places_of(axis):
    me = lax.axis_index(axis)
    if axis == "ctx":
        peer = lambda place: {"ctx": place}
    else:
        core, me = lax.rem(me, 2), me // 2
        peer = lambda place: {"shard": 2 * place + core}
    other = me + 1 - 2 * lax.rem(me, 2)
    places = [[lax.rem(base + 2 * k, N_CTX) for k in (0, 1, 3, 2)] for base in (me, other)]
    return places, peer


def by_rows(rows, body):
    step = 16

    def run(i, carry):
        body(pl.ds(pl.multiple_of(i * step, step), step))
        return carry

    lax.fori_loop(0, rows // step, run, 0)


class Gather:
    SEMAPHORES = 9
    PAIRED = 9 + CHIPS

    def __init__(self, own, out, sends, arrivals, axis="ctx", columns=None, offset=0):
        self.block, self.out, self.sends, self.arrivals = own, out, sends, arrivals
        self.columns, self.offset = columns, offset
        self.places, self.peer = places_of(axis)
        (self.me, self.up, self.down, self.far), other = self.places
        self.other = other[0]
        self.half = out.shape[-2] // 2
        self.paired = axis == "shard"
        if self.paired:
            shard = lax.axis_index("shard")
            self.core = lax.rem(shard, 2)
            self.mate = {"shard": shard + 1 - 2 * self.core}
        self.started = []

    def at(self, place, *half):
        if self.paired:
            return self.out.at[(place, self.core) + half]
        if self.columns is None:
            return self.out.at[(place,) + half]
        rows = half[0] if half else pl.ds(0, self.out.shape[1])
        return self.out.at[place, rows, pl.ds(*self.columns)]

    def own(self):
        if self.columns is None:
            return self.block
        return self.block.at[:, pl.ds(*self.columns)]

    def _send(self, slot, source, target, peer):
        def copy():
            return remote(
                source(), target(), self.sends, self.arrivals, slot + self.offset, peer()
            )

        copy().start()
        self.started.append(copy)

    def _await(self, slot, ref):
        peer = self.peer(self.other)
        remote(ref, ref, self.sends, self.arrivals, slot + self.offset, peer).wait_recv()

    def _hand(self, number, place, source=None):
        if self.paired:
            block = lambda: self.at(place)
            self._send(9 + number, source or block, block, lambda: self.mate)

    def _begin(self, slot, place):
        self._send(slot, self.own, lambda: self.at(self.me), lambda: self.peer(place))

    def begin_other(self):
        self._begin(0, self.other)
        self._hand(0, self.me, self.own)

    def begin_ring(self):
        self._begin(1, self.up)
        self._begin(2, self.down)

    def begin(self):
        self.begin_other()
        self.begin_ring()

    def pass_other(self):
        block = lambda: self.at(self.other)
        self._await(0, block())
        self._send(3, block, block, lambda: self.peer(self.up))
        self._send(4, block, block, lambda: self.peer(self.down))
        self._hand(1, self.other)

    def pass_ring(self, column):
        _, up, down, _ = self.places[column]
        first = 1 + 2 * column
        low, high = pl.ds(0, self.half), pl.ds(self.half, self.half)
        self._await(first, self.at(down))
        lower = lambda: self.at(down, low)
        self._send(5 + 2 * column, lower, lower, lambda: self.peer(self.up))
        self._await(first + 1, self.at(up))
        upper = lambda: self.at(up, high)
        self._send(6 + 2 * column, upper, upper, lambda: self.peer(self.down))
        self._hand(2 + 2 * column, down)
        self._hand(3 + 2 * column, up)

    def end(self):
        low, high = pl.ds(0, self.half), pl.ds(self.half, self.half)
        for column in range(2):
            far = self.places[column][3]
            self._await(5 + 2 * column, self.at(far, low))
            self._await(6 + 2 * column, self.at(far, high))
            self._hand(6 + column, far)
        if self.paired:
            (me, up, down, far), (other, other_up, other_down, other_far) = self.places
            for number, place in enumerate(
                (me, other, down, up, other_down, other_up, far, other_far)
            ):
                self._await(9 + number, self.out.at[place, 1 - self.core])
        for copy in self.started:
            copy().wait_send()


class RingFirst(Gather):
    def _across(self, slot, block):
        self._send(slot, block, block, lambda: self.peer(self.other))

    def pass_other(self):
        pass

    def pass_ring(self, column):
        _, up, down, far = self.places[0]
        low, high = pl.ds(0, self.half), pl.ds(self.half, self.half)
        if column:
            for slot, half in ((5, low), (6, high)):
                self._await(slot, self.at(far, half))
                self._across(slot + 2, lambda half=half: self.at(far, half))
            return
        for slot, place, half, toward in ((1, down, low, self.up), (2, up, high, self.down)):
            self._await(slot, self.at(place))
            self._on(slot + 4, place, half, toward)
            self._across(slot + 2, lambda place=place: self.at(place))

    def _on(self, slot, place, half, toward):
        block = lambda: self.at(place, half)
        self._send(slot, block, block, lambda: self.peer(toward))

    def end(self):
        low, high = pl.ds(0, self.half), pl.ds(self.half, self.half)
        other, up, down, far = self.places[1]
        for slot, block in (
            (0, self.at(other)),
            (3, self.at(down)),
            (4, self.at(up)),
            (7, self.at(far, low)),
            (8, self.at(far, high)),
        ):
            self._await(slot, block)
        for copy in self.started:
            copy().wait_send()


class Both:
    SEMAPHORES = 2 * Gather.SEMAPHORES

    def __init__(self, own, out, sends, arrivals, after):
        width = out.shape[-1]
        first = Gather(own, out, sends, arrivals, columns=(0, width - after))
        last = RingFirst(
            own, out, sends, arrivals, columns=(width - after, after), offset=Gather.SEMAPHORES
        )
        self.parts, self.out = (first, last), out
        self.me, self.up, self.down, self.other = first.me, first.up, first.down, first.other

    def begin(self):
        for part in self.parts:
            part.begin()

    def pass_other(self):
        for part in self.parts:
            part.pass_other()

    def pass_ring(self, column):
        for part in self.parts:
            part.pass_ring(column)

    def end(self):
        for part in self.parts:
            part.end()


class Reduce:
    SEMAPHORES = 13

    @staticmethod
    def scratch(rows, width, across=2):
        return [
            pltpu.VMEM((4, rows // 2, width), jnp.bfloat16),
            pltpu.VMEM((4, rows, width), jnp.bfloat16),
            pltpu.VMEM((across, rows, width), jnp.bfloat16),
            pltpu.SemaphoreType.DMA((Reduce.SEMAPHORES,)),
            pltpu.SemaphoreType.DMA((Reduce.SEMAPHORES,)),
        ]

    def __init__(self, parts, held, passing, near, across, sends, arrivals, axis="ctx"):
        self.parts, self.held = parts, held
        self.passing, self.near, self.across = passing, near, across
        self.sends, self.arrivals = sends, arrivals
        self.places, self.peer = places_of(axis)
        _, self.up, self.down, _ = self.places[0]
        self.other = self.places[1][0]
        self.rows, self.width = near.shape[1], near.shape[2]
        self.half = self.rows // 2
        self.started = []

    def _send(self, slot, source, target, place):
        def copy():
            return remote(source(), target(), self.sends, self.arrivals, slot, self.peer(place))

        copy().start()
        self.started.append(copy)

    def _await(self, slot, ref):
        remote(ref, ref, self.sends, self.arrivals, slot, self.peer(self.other)).wait_recv()

    def begin(self):
        self.send_far()
        self.send_near(0)
        self.send_near(1)

    def send_far(self):
        for column in (1, 0):
            self._send_far(column)

    def _send_far(self, column):
        low, high = pl.ds(0, self.half), pl.ds(self.half, self.half)
        far = self.places[column][3]
        slot, a, b = 6 * column, 2 * column, 2 * column + 1
        parts, passing = self.parts, self.passing
        self._send(slot, lambda: parts.at[far, low], lambda: passing.at[a], self.up)
        self._send(slot + 1, lambda: parts.at[far, high], lambda: passing.at[b], self.down)

    def send_near(self, side):
        for column in (1, 0):
            self._send_near(column, side)

    def _send_near(self, column, side):
        half = pl.ds((1 - side) * self.half, self.half)
        toward, place = self.places[column][1 + side], (self.up, self.down)[side]
        index, parts, near = 2 * column + side, self.parts, self.near
        self._send(
            6 * column + 2 + side,
            lambda: parts.at[toward, half],
            lambda: near.at[index, half],
            place,
        )

    def pass_side(self, side):
        for column in (1, 0):
            self._pass_side(column, side)

    def _loop(self, rows, body):
        step = 16

        def run(i, carry):
            body(pl.multiple_of(i * step, step), step)
            return carry

        lax.fori_loop(0, rows // step, run, 0)

    def pass_on(self, column):
        self._pass_side(column, 0)
        self._pass_side(column, 1)

    def _pass_side(self, column, side):
        slot, index, start = 6 * column, 2 * column + side, side * self.half
        toward, place = self.places[column][1 + side], (self.up, self.down)[side]
        passing, near, held = self.passing, self.near, self.held
        self._await(slot + side, passing.at[index])

        def add(row, step):
            there = pl.ds(row, step)
            total = passing[index, there, :].astype(jnp.float32)
            total = total + held[toward, pl.ds(start + row, step), :].astype(jnp.float32)
            passing[index, there, :] = total.astype(jnp.bfloat16)

        self._loop(self.half, add)
        target = pl.ds(start, self.half)
        self._send(
            slot + 4 + side, lambda: passing.at[index], lambda: near.at[index, target], place
        )

    def _near(self, column):
        low, high = pl.ds(0, self.half), pl.ds(self.half, self.half)
        slot = 6 * column
        self._await(slot + 2, self.near.at[2 * column, high])
        self._await(slot + 3, self.near.at[2 * column + 1, low])
        self._await(slot + 4, self.near.at[2 * column, low])
        self._await(slot + 5, self.near.at[2 * column + 1, high])

    def _sum(self, column, there):
        place = self.places[column][0]
        total = self.held[place, there, :].astype(jnp.float32)
        total = total + self.near[2 * column, there, :].astype(jnp.float32)
        return total + self.near[2 * column + 1, there, :].astype(jnp.float32)

    def cross(self):
        self._near(1)
        place, held, across = self.places[1][0], self.held, self.across
        if across.shape[0] == 1:
            kept = lambda: held.at[place]
        else:
            kept = lambda: across.at[1]

        def add(row, step):
            there = pl.ds(row, step)
            kept()[there, :] = self._sum(1, there).astype(jnp.bfloat16)

        self._loop(self.rows, add)
        self._send(12, kept, lambda: across.at[0], self.other)

    def ready(self):
        self._near(0)
        self._await(12, self.across.at[0])

    def total(self, there):
        return self._sum(0, there) + self.across[0, there, :].astype(jnp.float32)

    def end(self):
        for copy in self.started:
            copy().wait_send()


class Spread:
    SEMAPHORES = 7 + 8

    def __init__(self, own, out, sends, arrivals):
        self.own, self.out, self.sends, self.arrivals = own, out, sends, arrivals
        self.me = lax.axis_index("shard")
        self.core, self.chip = lax.rem(self.me, 2), self.me // 2
        self.mate = {"shard": self.me + 1 - 2 * self.core}
        self.started = []

    def _send(self, slot, source, target, peer):
        copy = remote(source, target, self.sends, self.arrivals, slot, peer)
        copy.start()
        self.started.append(copy)

    def _await(self, slot, ref):
        remote(ref, ref, self.sends, self.arrivals, slot, self.mate).wait_recv()

    def _from(self, k, core):
        return self.out.at[2 * lax.rem(self.chip + CHIPS - k, CHIPS) + core]

    def peers(self):
        return [self.mate] + [
            {"shard": 2 * lax.rem(self.chip + k, CHIPS) + self.core} for k in range(1, CHIPS)
        ]

    def begin(self):
        target = self.out.at[self.me]
        for k in range(1, CHIPS):
            peer = {"shard": 2 * lax.rem(self.chip + k, CHIPS) + self.core}
            self._send(k - 1, self.own, target, peer)
        self._send(7, self.own, target, self.mate)

    def hand_on(self):
        for k in range(1, CHIPS):
            block = self._from(k, self.core)
            self._await(k - 1, block)
            self._send(7 + k, block, block, self.mate)

    def end(self):
        for k in range(CHIPS):
            self._await(7 + k, self._from(k, 1 - self.core))
        for copy in self.started:
            copy.wait_send()


def pick_copies(ffn_in, ffn_out, picked, sems):
    count = -(-HIDDEN_BLOCKS // N_CTX)
    place = lax.axis_index("ctx")
    copies = []
    for j in range(count):
        block = place * count + j
        block = block - (block // HIDDEN_BLOCKS) * (block - HIDDEN_BLOCKS + 1)
        routed = (block // SHARED_BLOCKS + 1) // 2
        rest = block - SHARED_BLOCKS
        expert = (rest + SHARED_BLOCKS * (1 - routed)) // EXPERT_BLOCKS * routed
        gate = block * (1 - routed) + (2 * SHARED_BLOCKS + EXPERT_BLOCKS * expert + rest) * routed
        up = gate + SHARED_BLOCKS * (1 - routed) + EXPERT_BLOCKS * routed
        for k, (source, at) in enumerate(((ffn_in, gate), (ffn_in, up), (ffn_out, block))):
            copies.append(
                pltpu.make_async_copy(
                    source.at[:, pl.ds(pl.multiple_of(at * LANE, LANE), LANE)],
                    picked.at[:, LANE * (count * k + j) : LANE * (count * k + j + 1)],
                    sems.at[3 * j + k],
                )
            )
    return copies


def assemble(out_share, gate_share, up_share, mixed_share, qkv_share):
    rows, hidden = out_share.shape[1:]
    width = mixed_share.shape[2]
    count = hidden // LANE
    spans = [(0, SHARED_BLOCKS)] + [
        (SHARED_BLOCKS + EXPERT_BLOCKS * e, EXPERT_BLOCKS) for e in range(EXPERTS)
    ]

    def moves(place, kind):
        result = []
        for index, (first, size) in enumerate(spans):
            low, high = max(first, count * place), min(first + size, count * (place + 1))
            if low >= high:
                continue
            there = low if kind == 0 else first + low + (kind - 1) * size
            result.append(((low - count * place) * LANE, there * LANE, (high - low) * LANE))
        return result

    jobs = []
    for place in range(N_CTX):
        for kind in range(3):
            jobs.append((kind, place, hidden, min(kind, 1), moves(place, kind)))
        jobs.append((3, place, width, 2, [(0, width * place, width)]))
        jobs.append(
            (4, place, 3 * width, 3, [(width * i, D * i + width * place, width) for i in range(3)])
        )
    depth = 4
    most = max(len(job[4]) for job in jobs)

    def kernel(*refs):
        shares, outs = refs[0:5], refs[5:9]
        low, full, loads, stores = refs[9:]

        def load(n):
            kind, place, size, _, _ = jobs[n]
            return pltpu.make_async_copy(
                shares[kind].at[place], low.at[n % depth, :, 0:size], loads.at[n % depth]
            )

        def store(n):
            _, _, _, to, spans_of = jobs[n]
            return [
                pltpu.make_async_copy(
                    full.at[n % depth, :, start : start + size],
                    outs[to].at[:, there : there + size],
                    stores.at[n % depth, k],
                )
                for k, (start, there, size) in enumerate(spans_of)
            ]

        for n in range(depth - 1):
            load(n).start()
        for n in range(len(jobs)):
            if n + depth - 1 < len(jobs):
                load(n + depth - 1).start()
            load(n).wait()
            if n >= depth:
                for copy in store(n - depth):
                    copy.wait()
            slot, size = n % depth, jobs[n][2]

            def widen(there, slot=slot, size=size):
                full[slot, there, 0:size] = low[slot, there, 0:size].astype(jnp.float32)

            by_rows(rows, widen)
            for copy in store(n):
                copy.start()
        for n in range(len(jobs) - depth, len(jobs)):
            for copy in store(n):
                copy.wait()

    f32 = jnp.float32
    return pl.pallas_call(
        kernel,
        out_shape=(
            jax.ShapeDtypeStruct((rows, FOUT), f32),
            jax.ShapeDtypeStruct((rows, FIN), f32),
            jax.ShapeDtypeStruct((rows, D), f32),
            jax.ShapeDtypeStruct((rows, 3 * D), f32),
        ),
        in_specs=[ANY] * 5,
        out_specs=(ANY,) * 4,
        scratch_shapes=[
            pltpu.VMEM((depth, rows, hidden), jnp.bfloat16),
            pltpu.VMEM((depth, rows, hidden), f32),
            pltpu.SemaphoreType.DMA((depth,)),
            pltpu.SemaphoreType.DMA((depth, most)),
        ],
        compiler_params=pltpu.CompilerParams(vmem_limit_bytes=60 << 20),
        name="assemble",
    )(out_share, gate_share, up_share, mixed_share, qkv_share)


def front(block, own_grad, qkv_weight, out_weight, ffn_in, ffn_out, small, cosines, sines, key_pos, query_pos):
    rows, width = qkv_weight.shape[0], out_weight.shape[1]
    n_shard = width // rows
    heads_width = width // N_CTX
    heads = heads_width // HEAD
    seq = rows * N_CTX
    extra = block.shape[1] - width
    tile = 256
    scale = HEAD ** (-0.5)
    hidden = -(-HIDDEN_BLOCKS // N_CTX) * LANE
    f32, bf16 = jnp.float32, jnp.bfloat16

    def kernel(
        block, own_grad, qkv_weight, out_weight, ffn_in, ffn_out, small, cosines, sines, key_pos,
        query_pos,
        residual, second_all, g_all, weights_out, small_all, first_out, w_gate, w_up, w_down, qkv,
        mixed_own, assigned,
        x_all, weights, first, staged, picked, params_all, mixed, own, parts, loads, picks, local,
        mixed_sends, mixed_arrivals, *scratch,
    ):
        gather = Gather(block, x_all, *scratch[0:2])
        gather_qkv = Gather(staged, weights, *scratch[2:4], axis="shard")
        spread_small = Spread(small, small_all, *scratch[4:6])
        gather_grad = Both(own_grad, g_all, *scratch[6:8], AFTER)
        gather_second = Both(own, second_all, *scratch[8:10], AFTER)
        w_outs = (w_gate, w_up, w_down)
        ffn = [
            Gather(
                picked.at[:, pl.ds(hidden * k, hidden)], out, *scratch[10 + 2 * k : 12 + 2 * k], axis="shard"
            )
            for k, out in enumerate(w_outs)
        ]
        reduce = Reduce(parts, parts, *scratch[16:21])
        me = gather.me
        loaded = [
            pltpu.make_async_copy(
                source.at[:, pl.ds(pl.multiple_of(start + heads_width * me, heads_width), heads_width)],
                staged.at[:, heads_width * i : heads_width * (i + 1)],
                loads.at[i],
            )
            for i, (source, start) in enumerate(
                ((qkv_weight, 0), (qkv_weight, width), (qkv_weight, 2 * width), (out_weight, 0))
            )
        ]
        for copy in loaded:
            copy.start()
        picking = pick_copies(ffn_in, ffn_out, picked, picks)
        for copy in picking:
            copy.start()
        places = [lax.rem(me + k, N_CTX) for k in range(1, N_CTX)]
        greet([{"ctx": p} for p in places] + spread_small.peers())
        gather.begin()
        spread_small.begin()
        for copy in loaded:
            copy.wait()
        gather_qkv.begin()
        for copy in picking:
            copy.wait()
        ffn[0].begin()
        kept = [
            pltpu.make_async_copy(source, target, local.at[k])
            for k, (source, target) in enumerate(
                (
                    (block, x_all.at[me]),
                    (staged, weights.at[spread_small.chip, spread_small.core]),
                    (small, small_all.at[spread_small.me]),
                    (own_grad, g_all.at[me]),
                )
            )
        ] + [
            pltpu.make_async_copy(gather_w.block, gather_w.at(gather_w.me), local.at[4 + k])
            for k, gather_w in enumerate(ffn)
        ]
        for copy in kept:
            copy.start()
        gather.pass_other()
        gather_qkv.pass_other()
        gather_qkv.pass_ring(0)
        spread_small.hand_on()
        gather.pass_ring(0)
        gather_qkv.pass_ring(1)
        ffn[0].pass_other()
        gather.pass_ring(1)
        spread_small.end()
        gather_qkv.end()
        gather.end()
        gather_grad.begin()
        ffn[1].begin()
        for copy in kept:
            copy.wait()
        weights_kept = pltpu.make_async_copy(weights, weights_out, local.at[0])
        weights_kept.start()
        assigned[...] = x_all[:, :, width:].reshape(seq, extra)
        params_all[...] = small_all[...].astype(f32)
        gains = [
            jnp.concatenate([params_all[s, k : k + 1, :] for s in range(n_shard)], axis=1)
            for k in range(2)
        ]
        per = heads_width // 128

        def bias_of(i):
            parts_of = []
            for j in range(per):
                at = n_shard * i + per * me + j
                parts_of.append(params_all[at // 3, pl.ds(3 + EXPERTS + lax.rem(at, 3), 1), :])
            return jnp.concatenate(parts_of, axis=1)

        biases = [bias_of(i) for i in range(3)]

        def project(n, carry):
            there = pl.ds(pl.multiple_of(n * tile, tile), tile)

            def norm(k, inner):
                inner_rows = pl.ds(pl.multiple_of(lax.rem(k, rows // 16) * 16, 16), 16)
                at = 2 * n + k // (rows // 16)
                normed, _ = normalize(x_all[at, inner_rows, 0:width].astype(f32))
                first[at, inner_rows, :] = (normed * gains[0]).astype(bf16)
                return inner

            lax.fori_loop(0, tile // 16, norm, 0)
            left = first[pl.ds(2 * n, 2)].reshape(tile, width)
            for i in range(3):
                columns = slice(heads_width * i, heads_width * (i + 1))
                made = biases[i] + jnp.dot(
                    left,
                    weights[:, :, :, columns].reshape(width, heads_width),
                    preferred_element_type=f32,
                )
                if i == 2:
                    qkv[there, columns] = made.astype(bf16)
                    continue
                for h in range(heads):
                    part = made[:, HEAD * h : HEAD * (h + 1)]
                    turned = part * cosines[there, :] + pltpu.roll(part, HEAD // 2, 1) * sines[there, :]
                    start = heads_width * i + HEAD * h
                    qkv[there, start : start + HEAD] = turned.astype(bf16)

            @pl.when(n == 0)
            def _():
                ffn[0].pass_ring(0)

            @pl.when(n == 1)
            def _():
                ffn[0].pass_ring(1)

            @pl.when(n == 2)
            def _():
                gather_grad.pass_other()
                ffn[1].pass_other()

            return carry

        lax.fori_loop(0, seq // tile, project, 0)
        first_kept = pltpu.make_async_copy(first, first_out, local.at[1])
        first_kept.start()
        events = {
            0: [lambda: gather_grad.pass_ring(0)],
            2: [lambda: ffn[1].pass_ring(0)],
            3: [lambda: gather_grad.pass_ring(1)],
            5: [lambda: ffn[1].pass_ring(1)],
        }

        def attend(n, carry):
            head, i = n // (seq // tile), lax.rem(n, seq // tile)
            there = pl.ds(pl.multiple_of(i * tile, tile), tile)

            def lanes_of(start):
                return pl.ds(pl.multiple_of(start + HEAD * head, HEAD), HEAD)

            scores = scale * contract_last(qkv[:, lanes_of(heads_width)], qkv[there, lanes_of(0)])
            scores = jnp.where(key_pos[...] <= query_pos[:, there], scores, -1e30)
            raised = jnp.exp(scores - jnp.max(scores, axis=0, keepdims=True))
            probs = (raised * (1.0 / jnp.sum(raised, axis=0, keepdims=True))).astype(bf16)
            mixed[there, lanes_of(0)] = contract_first(
                probs, qkv[:, lanes_of(2 * heads_width)]
            ).astype(bf16)
            for at, todo in events.items():

                @pl.when(n == at)
                def _(todo=todo):
                    for event in todo:
                        event()

            return carry

        lax.fori_loop(0, heads * (seq // tile), attend, 0)

        def columns_of(place):
            return pl.ds(pl.multiple_of(heads_width * place, heads_width), heads_width)

        def rows_of(place):
            return pl.ds(pl.multiple_of(rows * place, rows), rows)

        to_rows = [
            remote(
                mixed.at[rows_of(p), :],
                mixed_own.at[:, columns_of(me)],
                mixed_sends,
                mixed_arrivals,
                k,
                {"ctx": p},
            )
            for k, p in enumerate(places)
        ]

        def attended(k, carry):
            ahead = 2 - k + 3 * (k // 2) - 2 * (k // 3)
            at = lax.rem(me // 2 + ahead, N_CTX // 2) * 2
            left = mixed[pl.ds(pl.multiple_of(at * rows, tile), tile), :]
            for t in range(width // 512):
                right = weights[2 * t : 2 * (t + 1), :, :, 3 * heads_width :]
                made = contract_last(left, right.reshape(512, heads_width)).astype(bf16)
                parts[pl.ds(at, 2), :, 512 * t : 512 * (t + 1)] = made.reshape(2, rows, 512)
            pl.when(k == 0)(reduce.send_far)
            pl.when(k == 1)(lambda: reduce.send_near(0))
            pl.when(k == 2)(lambda: reduce.send_near(1))
            return carry

        lax.fori_loop(0, 4, attended, 0)
        for copy in to_rows:
            copy.start()
        ffn[2].begin()
        mixed_own[:, columns_of(me)] = mixed[rows_of(me), :]
        reduce.pass_side(0)
        reduce.pass_side(1)
        reduce.cross()
        ffn[2].pass_other()
        ffn[0].end()
        reduce.ready()

        def norm_second(there):
            total = x_all[me, there, 0:width].astype(f32) + reduce.total(there)
            residual[there, :] = total
            normed, _ = normalize(total)
            own[there, :] = (normed * gains[1]).astype(bf16)

        by_rows(rows, norm_second)
        gather_second.begin()
        second_kept = pltpu.make_async_copy(own, second_all.at[me], local.at[2])
        second_kept.start()
        gather_second.pass_other()
        ffn[2].pass_ring(0)
        gather_second.pass_ring(0)
        ffn[2].pass_ring(1)
        ffn[1].end()
        gather_second.pass_ring(1)
        gather_grad.end()
        for k, p in enumerate(places):
            ref = mixed_own.at[:, columns_of(lax.rem(me + N_CTX - 1 - k, N_CTX))]
            remote(ref, ref, mixed_sends, mixed_arrivals, k, {"ctx": p}).wait_recv()
        for copy in to_rows:
            copy.wait_send()
        reduce.end()
        for copy in (weights_kept, first_kept, second_kept):
            copy.wait()
        gather_second.end()
        ffn[2].end()

    def shape(*dims, kind=bf16):
        return jax.ShapeDtypeStruct(dims, kind)

    pair = [pltpu.SemaphoreType.DMA((Both.SEMAPHORES,))] * 2
    paired = [pltpu.SemaphoreType.DMA((Gather.PAIRED,))] * 2
    return pl.pallas_call(
        kernel,
        out_shape=(
            shape(rows, width, kind=f32),
            shape(N_CTX, rows, width),
            shape(N_CTX, rows, width),
            shape(CHIPS, 2, rows, 4 * heads_width),
            shape(n_shard, 16, 128),
            shape(N_CTX, rows, width),
            shape(CHIPS, 2, rows, hidden),
            shape(CHIPS, 2, rows, hidden),
            shape(CHIPS, 2, rows, hidden),
            shape(seq, 3 * heads_width),
            shape(rows, width),
            shape(seq, extra),
        ),
        in_specs=[ANY, VMEM] + [ANY] * 5 + [VMEM] * 4,
        out_specs=(VMEM, ANY, ANY, ANY, VMEM, ANY, ANY, ANY, ANY, VMEM, VMEM, VMEM),
        scratch_shapes=[
            pltpu.VMEM((N_CTX,) + block.shape, bf16),
            pltpu.VMEM((CHIPS, 2, rows, 4 * heads_width), bf16),
            pltpu.VMEM((N_CTX, rows, width), bf16),
            pltpu.VMEM((rows, 4 * heads_width), bf16),
            pltpu.VMEM((rows, 3 * hidden), bf16),
            pltpu.VMEM((n_shard, 16, 128), f32),
            pltpu.VMEM((seq, heads_width), bf16),
            pltpu.VMEM((rows, width), bf16),
            pltpu.VMEM((N_CTX, rows, width), bf16),
            pltpu.SemaphoreType.DMA((4,)),
            pltpu.SemaphoreType.DMA((3 * hidden // LANE,)),
            pltpu.SemaphoreType.DMA((7,)),
            pltpu.SemaphoreType.DMA((N_CTX - 1,)),
            pltpu.SemaphoreType.DMA((N_CTX - 1,)),
        ]
        + pair
        + paired
        + [pltpu.SemaphoreType.DMA((Spread.SEMAPHORES,))] * 2
        + pair * 2
        + paired * 3
        + Reduce.scratch(rows, width, 1),
        compiler_params=params(0, 56 << 20),
        name="front",
    )(block, own_grad, qkv_weight, out_weight, ffn_in, ffn_out, small, cosines, sines, key_pos, query_pos)


class Exchange:
    @staticmethod
    def scratch():
        return [pltpu.SemaphoreType.DMA((CHIPS,)), pltpu.SemaphoreType.DMA((CHIPS,))]

    def __init__(self, parts, staged, sends, arrivals):
        self.parts, self.staged = parts, staged
        self.sems = (sends, arrivals)
        self.width = parts.shape[2]
        me = lax.axis_index("shard")
        self.core, self.chip = lax.rem(me, 2), me // 2
        self.mate = {"shard": me + 1 - 2 * self.core}

    def chip_at(self, step):
        base = self.chip + (1 - lax.rem(step, 2)) * (1 - 2 * lax.rem(self.chip, 2))
        b = step // 2
        ahead = 2 - b + 3 * (b // 2) - 2 * (b // 3)
        return 2 * lax.rem(base // 2 + ahead, 4) + lax.rem(base, 2)

    def stage(self, slot, core):
        if len(self.staged.shape) == 2:
            return self.staged.at[pl.ds(pl.multiple_of((2 * slot + core) * 128, 128), 128), :]
        return self.staged.at[slot, core]

    def columns_at(self, step):
        return pl.ds(pl.multiple_of(self.chip_at(step) * 256, 256), 256)

    def _pair(self, step):
        return remote(
            self.stage(lax.rem(step, 3), 1 - self.core).at[:, pl.ds(0, self.width)],
            self.parts.at[self.chip_at(step)],
            *self.sems,
            step,
            self.mate,
        )

    def finish(self, step):
        chip, slot, width = self.chip_at(step), lax.rem(step, 3), self.width
        ref = self.parts.at[chip]
        remote(ref, ref, *self.sems, step, self.mate).wait_recv()

        def add(there):
            total = self.parts[chip, there, :].astype(jnp.float32)
            total = total + self.stage(slot, self.core)[there, 0:width].astype(jnp.float32)
            self.parts[chip, there, :] = total.astype(jnp.bfloat16)

        by_rows(128, add)

    def run(self, left, right, turned, between):
        width = self.width
        tile = 896 if width % 896 == 0 else min(width, 1024)

        def step_of(step, carry):
            @pl.when(step >= 3)
            def _():
                self._pair(step - 3).wait_send()

            slot = lax.rem(step, 3)
            rows = left(step)
            depth = rows.shape[0]
            turned[:, 0:depth] = rows.T
            for start in range(0, width, tile):
                made = jnp.dot(
                    turned[:, 0:depth], right(start, tile), preferred_element_type=jnp.float32
                ).astype(jnp.bfloat16)
                self.stage(slot, 0)[:, start : start + tile] = made[:128]
                self.stage(slot, 1)[:, start : start + tile] = made[128:]
            self._pair(step).start()

            @pl.when(step >= 2)
            def _():
                self.finish(step - 2)

            for at, events in between.items():

                @pl.when(step == at)
                def _(events=events):
                    for event in events:
                        event()

            return carry

        lax.fori_loop(0, CHIPS, step_of, 0)
        self.finish(CHIPS - 2)
        self.finish(CHIPS - 1)
        for step in range(CHIPS - 3, CHIPS):
            self._pair(step).wait_send()


def feed_forward(second, grad_out, assigned, w_gate, w_up, w_down, out_weight, small, residual, own_grad, own_valid):
    _, rows, width = second.shape
    seq = rows * N_CTX
    hidden = w_gate.shape[1]
    lanes = 128
    n_shard = small.shape[0]
    pair = 2 * rows
    tile = 896
    f32, bf16 = jnp.float32, jnp.bfloat16

    def kernel(
        second, grad_out, assigned, w_gate, w_up, w_down, out_weight, small, residual, own_grad, own_valid,
        grad_residual, grad_low, grad_mixed, output, grad_gain, grad_logits, act_out, grad_gu_out,
        out_weights, out_owned,
        second_held, grad_held, in_held, down_held, act, grad_gu, weights, dots, dots_in, gain_sum,
        logit_low, out_sems,
        back_parts, ffn_parts, dot_sends, dot_arrivals, loads, weight_loads, stores, *scratch,
    ):
        back = Reduce(back_parts, back_parts, *scratch[:5])
        ahead = Reduce(ffn_parts, ffn_parts, *scratch[5:10])
        gather_out = Gather(out_weight, out_weights, *scratch[10:12], axis="shard")
        share, act_held = down_held.at[pl.ds(0, CHIPS)], down_held.at[pl.ds(CHIPS, N_CTX)]
        staged = in_held.at[pl.ds(0, 768), pl.ds(0, hidden)]
        turned = in_held.at[pl.ds(768, 256), pl.ds(0, seq)]
        exchange = Exchange(share, staged, *scratch[12:14])
        sums = Reduce(share, share, *scratch[14:19], axis="shard")
        free = scratch[19]
        own, other = back.places
        me = own[0]
        peers = [lax.rem(me + k, N_CTX) for k in range(1, N_CTX)]
        copies = [
            pltpu.make_async_copy(source, target, loads.at[k])
            for k, (source, target) in enumerate(((second, second_held), (grad_out, grad_held)))
        ]
        for copy in copies:
            copy.start()

        def weight_copies(t):
            copies = []
            for k, (source, target, here) in enumerate(
                ((w_gate, in_held, 0), (w_up, in_held, hidden), (w_down, down_held, 0))
            ):
                every = (slice(None),) * (len(target.shape) - 1)
                source = source.at[every + (pl.ds(pl.multiple_of(tile * t, tile), tile),)]
                target = target.at[every + (pl.ds(pl.multiple_of(here + tile * t, tile), tile),)]
                copies.append(pltpu.make_async_copy(source, target, weight_loads.at[3 * t + k]))
            return copies

        def start_weights(t, carry):
            for copy in weight_copies(t):
                copy.start()
            return carry

        lax.fori_loop(0, hidden // tile, start_weights, 0)
        shard_peers = [gather_out.peer(p) for p in (gather_out.up, gather_out.down, gather_out.other)]
        greet([{"ctx": p} for p in peers] + shard_peers + [gather_out.mate])
        gather_out.begin()
        out_kept = pltpu.make_async_copy(
            out_weight, out_weights.at[gather_out.me, gather_out.core], loads.at[2]
        )
        out_kept.start()
        logit_low[...] = jnp.zeros_like(logit_low)
        gains = []
        for s in range(n_shard):
            held = small[s].astype(f32)
            gains.append(held[1:2])
            part = jnp.concatenate([held[2 : 3 + EXPERTS], jnp.zeros((15 - EXPERTS, 128), f32)], axis=0)
            logit_low[0:16, 128 * s : 128 * (s + 1)] = part.astype(bf16)
        gain = jnp.concatenate(gains, axis=1)
        for copy in copies:
            copy.wait()

        def stored(slot, start):
            there = pl.ds(start, pair)
            return [
                pltpu.make_async_copy(
                    act.at[slot, pl.ds(rows * k, rows)], act_out.at[start // rows + k], stores.at[slot, 1 + k]
                )
                for k in range(2)
            ] + [
                pltpu.make_async_copy(grad_gu.at[slot], grad_gu_out.at[there, :], stores.at[slot, 0]),
            ]

        def dot_copy(slot, place):
            return remote(
                dots.at[place], dots_in.at[slot], dot_sends, dot_arrivals, slot, {"ctx": place}
            )

        def start_of(b):
            ahead = 2 - b + 3 * (b // 2) - 2 * (b // 3)
            return pl.multiple_of(lax.rem(me // 2 + ahead, N_CTX // 2) * pair, pair)

        def branch_of(j):
            at = me * (hidden // LANE) + j
            routed = (at // SHARED_BLOCKS + 1) // 2
            expert = (at - SHARED_BLOCKS) // EXPERT_BLOCKS
            return (1 - routed) * EXPERTS + routed * expert + 100 * (at // HIDDEN_BLOCKS)

        def block(b, carry):
            start = start_of(b)
            slot = 0
            first = pl.multiple_of(start // rows, 2)

            @pl.when(b >= 1)
            def _():
                for copy in stored(slot, start_of(b - 1)):
                    copy.wait()

            def rows_of(ref):
                return ref[pl.ds(first, 2)].reshape(pair, width)

            logits = contract_last(rows_of(second_held), logit_low[...])
            lane = lax.broadcasted_iota(jnp.int32, logits.shape, 1)
            named = assigned[pl.ds(start, pair), :] > 0
            raised = jnp.where(named, logits, -1e30)
            raised = jnp.exp(raised - jnp.max(raised, axis=-1, keepdims=True))
            raised = jnp.where(named, raised, 0.0)
            gates = raised / jnp.sum(raised, axis=-1, keepdims=True)
            gates = jnp.where(lane == EXPERTS, jax.nn.sigmoid(logits), gates)
            weights[pl.ds(start, pair), :] = gates
            dots[pl.ds(first, 2)] = jnp.zeros((2, rows, lanes), f32)

            def hidden_tile(t, carry):
                @pl.when(b == 0)
                def _():
                    for copy in weight_copies(t):
                        copy.wait()

                low = pl.ds(pl.multiple_of(tile * t, tile), tile)
                high = pl.ds(pl.multiple_of(hidden + tile * t, tile), tile)
                rows_in = rows_of(second_held)
                gate = jnp.dot(rows_in, in_held[:, low], preferred_element_type=f32)
                upward = jnp.dot(rows_in, in_held[:, high], preferred_element_type=f32)
                raw = jnp.dot(
                    rows_of(grad_held),
                    down_held[:, :, low].reshape(width, tile),
                    preferred_element_type=f32,
                )
                gates = weights[pl.ds(start, pair), :]
                lane = lax.broadcasted_iota(jnp.int32, gates.shape, 1)
                branches = [branch_of(tile // LANE * t + j) for j in range(tile // LANE)]
                held = jnp.concatenate(
                    [
                        jnp.broadcast_to(
                            jnp.sum(jnp.where(lane == n, gates, 0.0), axis=1, keepdims=True),
                            (pair, LANE),
                        )
                        for n in branches
                    ],
                    axis=1,
                )
                squashed = jax.nn.sigmoid(gate)
                swished = gate * squashed
                value = swished * upward
                act[slot, :, low] = (value * held).astype(bf16)
                products = raw * value
                part = dots[pl.ds(first, 2)].reshape(pair, lanes)
                for j, n in enumerate(branches):
                    inner = jnp.sum(products[:, LANE * j : LANE * (j + 1)], axis=1, keepdims=True)
                    part = part + jnp.where(lane == n, inner, 0.0)
                dots[pl.ds(first, 2)] = part.reshape(2, rows, lanes)
                grad = raw * held
                grad_gu[slot, :, low] = (
                    grad * upward * squashed * (1.0 + gate * (1.0 - squashed))
                ).astype(bf16)
                grad_gu[slot, :, high] = (grad * swished).astype(bf16)
                return carry

            lax.fori_loop(0, hidden // tile, hidden_tile, 0)
            for copy in stored(slot, start):
                copy.start()

            def out_tile(t, carry):
                there = pl.ds(pl.multiple_of(512 * t, 512), 512)
                for parts, left, right in (
                    (back_parts, grad_gu, lambda: in_held[there, :]),
                    (ffn_parts, act, lambda: down_held[pl.ds(4 * t, 4)].reshape(512, hidden)),
                ):
                    made = contract_last(left[slot], right())
                    parts[pl.ds(first, 2), :, there] = made.astype(bf16).reshape(2, rows, 512)
                return carry

            lax.fori_loop(0, width // 512, out_tile, 0)

            def far():
                back.send_far()
                ahead.send_far()
                dot_copy(0, own[3]).start()
                dot_copy(1, other[3]).start()

            def near(side):
                back.send_near(side)
                back.pass_side(side)
                ahead.send_near(side)
                ahead.pass_side(side)
                dot_copy(2 + 2 * side, own[1 + side]).start()
                dot_copy(3 + 2 * side, other[1 + side]).start()

            pl.when(b == 0)(far)
            pl.when(b == 1)(lambda: near(0))
            pl.when(b == 2)(lambda: near(1))
            pl.when(b == 0)(gather_out.pass_other)
            pl.when(b == 1)(lambda: gather_out.pass_ring(0))
            pl.when(b == 2)(lambda: gather_out.pass_ring(1))
            return carry

        lax.fori_loop(0, 4, block, 0)
        dot_copy(6, other[0]).start()
        for copy in stored(0, start_of(3)):
            copy.wait()
        act_load = pltpu.make_async_copy(act_out, act_held, loads.at[0])
        act_load.start()
        pl.semaphore_signal(free, inc=1, device_id=gather_out.mate, device_id_type=MESH)
        out_kept.wait()
        gather_out.end()
        pl.semaphore_wait(free, 1)
        act_load.wait()
        exchange.run(
            lambda step: grad_held[:, :, exchange.columns_at(step)].reshape(seq, 256),
            lambda start, count: down_held[CHIPS:, :, start : start + count].reshape(seq, count),
            turned,
            {
                2: [back.cross],
                3: [sums.send_far],
                5: [lambda: sums.send_near(0)],
                7: [lambda: sums.send_near(1)],
            },
        )
        out_loads = [
            pltpu.make_async_copy(
                out_weights.at[n // 2, n % 2], in_held.at[128 * n : 128 * (n + 1), 0:width], out_sems.at[n]
            )
            for n in range(n_shard)
        ]
        for copy in out_loads:
            copy.start()
        ahead.cross()
        sums.pass_side(0)
        sums.pass_side(1)
        back.ready()
        for k in range(7):
            ref = dots_in.at[k]
            remote(ref, ref, dot_sends, dot_arrivals, k, {"ctx": other[0]}).wait_recv()
        total_dots = dots[me]
        for k in range(7):
            total_dots = total_dots + dots_in[k]
        held = weights[pl.ds(pl.multiple_of(me * rows, rows), rows), :]
        lane = lax.broadcasted_iota(jnp.int32, held.shape, 1)
        routed = lane < EXPERTS
        centre = jnp.sum(jnp.where(routed, held * total_dots, 0.0), axis=-1, keepdims=True)
        both = jnp.where(
            routed,
            held * (total_dots - centre),
            jnp.where(lane == EXPERTS, total_dots * held * (1.0 - held), 0.0),
        )
        grad_logits[...] = lax.dot_general(
            both,
            second_held[me].astype(f32),
            (((0,), (0,)), ((), ())),
            precision=highest,
            preferred_element_type=f32,
        )[0:8]
        for t in range(width // 512):
            there = slice(512 * t, 512 * (t + 1))
            grad_residual[:, there] = jnp.dot(
                both, logit_low[:, there].astype(f32), precision=highest, preferred_element_type=f32
            )
        gain_sum[...] = jnp.zeros_like(gain_sum)

        def norm(there):
            normed, factor = normalize(residual[there, :])
            grad = back.total(there) + grad_residual[there, :]
            gain_sum[...] += grad * normed
            grad = own_grad[there, :].astype(f32) + norm_back(grad, normed, factor, gain)
            grad_residual[there, :] = grad
            grad_low[there, :] = grad.astype(bf16)

        by_rows(rows, norm)
        grad_gain[...] = jnp.sum(gain_sum[...], axis=0, keepdims=True)
        for copy in out_loads:
            copy.wait()
        for t in range(width // 512):
            there = slice(512 * t, 512 * (t + 1))
            grad_mixed[:, there] = jnp.dot(
                grad_low[...], in_held[:, there], preferred_element_type=f32
            ).astype(bf16)
        ahead.ready()

        def finish(there):
            total = residual[there, :] + ahead.total(there)
            output[there, :] = (total * own_valid[there, :]).astype(bf16)

        by_rows(rows, finish)
        sums.cross()
        sums.ready()

        def keep(there):
            out_owned[there, :] = sums.total(there).astype(bf16)

        by_rows(128, keep)
        sums.end()
        back.end()
        ahead.end()
        for slot, place in enumerate((own[3], other[3], own[1], other[1], own[2], other[2], other[0])):
            dot_copy(slot, place).wait_send()

    return pl.pallas_call(
        kernel,
        out_shape=(
            jax.ShapeDtypeStruct((rows, width), f32),
            jax.ShapeDtypeStruct((rows, width), bf16),
            jax.ShapeDtypeStruct((rows, width), bf16),
            jax.ShapeDtypeStruct((rows, width), bf16),
            jax.ShapeDtypeStruct((1, width), f32),
            jax.ShapeDtypeStruct((8, width), f32),
            jax.ShapeDtypeStruct((N_CTX, rows, hidden), bf16),
            jax.ShapeDtypeStruct((seq, 2 * hidden), bf16),
            jax.ShapeDtypeStruct((CHIPS, 2, rows, width), bf16),
            jax.ShapeDtypeStruct((128, hidden), bf16),
        ),
        in_specs=[ANY, ANY, VMEM] + [ANY] * 4 + [VMEM] * 4,
        out_specs=(VMEM,) * 6 + (ANY,) * 3 + (VMEM,),
        scratch_shapes=[
            pltpu.VMEM(second.shape, bf16),
            pltpu.VMEM(grad_out.shape, bf16),
            pltpu.VMEM((width, 2 * hidden), bf16),
            pltpu.VMEM((width // 128, 128, hidden), bf16),
            pltpu.VMEM((1, pair, hidden), bf16),
            pltpu.VMEM((1, pair, 2 * hidden), bf16),
            pltpu.VMEM((seq, lanes), f32),
            pltpu.VMEM((N_CTX, rows, lanes), f32),
            pltpu.VMEM((N_CTX - 1, rows, lanes), f32),
            pltpu.VMEM((16, width), f32),
            pltpu.VMEM((lanes, width), bf16),
            pltpu.SemaphoreType.DMA((n_shard,)),
            pltpu.VMEM(second.shape, bf16),
            pltpu.VMEM(second.shape, bf16),
            pltpu.SemaphoreType.DMA((N_CTX - 1,)),
            pltpu.SemaphoreType.DMA((N_CTX - 1,)),
            pltpu.SemaphoreType.DMA((3,)),
            pltpu.SemaphoreType.DMA((3 * hidden // tile,)),
            pltpu.SemaphoreType.DMA((1, 3)),
        ]
        + Reduce.scratch(rows, width, 1) * 2
        + [pltpu.SemaphoreType.DMA((Gather.PAIRED,))] * 2
        + Exchange.scratch()
        + Reduce.scratch(128, hidden, 1)
        + [pltpu.SemaphoreType.REGULAR],
        compiler_params=params(2, 64 << 20),
        name="feed_forward",
    )(second, grad_out, assigned, w_gate, w_up, w_down.reshape(width // 128, 128, hidden), out_weight, small, residual, own_grad, own_valid)


class Share:
    @staticmethod
    def scratch(width, split=1):
        own = width // split
        return (
            [pltpu.VMEM((CHIPS, 128, width), jnp.bfloat16), pltpu.VMEM((128, own), jnp.bfloat16)]
            + Exchange.scratch()
            + Reduce.scratch(128, width, 1)
            + [pltpu.SemaphoreType.DMA((Both.SEMAPHORES,))] * 2
            + [pltpu.SemaphoreType.DMA]
        )

    COUNT = 2 + 2 + 5 + 2 + 1

    def __init__(self, staged, out, scratch):
        parts, self.owned = scratch[0:2]
        self.exchange = Exchange(parts, staged, *scratch[2:4])
        self.reduce = Reduce(parts, parts, *scratch[4:9], axis="shard")
        if out.shape[-1] > 2 * AFTER:
            self.gather = Both(self.owned, out, *scratch[9:11], AFTER)
        else:
            self.gather = Gather(self.owned, out, *scratch[9:11])
        self.local = scratch[11]

    def near(self, side):
        return lambda: self.reduce.send_near(side)

    def side(self, side):
        return lambda: self.reduce.pass_side(side)

    def ring(self, column):
        return lambda: self.gather.pass_ring(column)

    def own(self):
        self.sum_into(self.owned)
        self.pass_own()

    def sum_into(self, ref):
        self.reduce.ready()

        def keep(there):
            ref[there, :] = self.reduce.total(there).astype(jnp.bfloat16)

        by_rows(128, keep)

    def pass_own(self):
        self.gather.begin()
        self._kept().start()

    def _kept(self):
        return pltpu.make_async_copy(
            self.owned, self.gather.out.at[self.gather.me], self.local
        )

    def end(self):
        self._kept().wait()
        self.gather.end()
        self.reduce.end()


def backward(own, grad_mixed, mixed, out_own, second, grad_gu, qkv, weights, first, cosines, sines, key_pos, query_pos, inputs, grad_residual, gain, second_gain_grad, logits_grad):
    rows, width = own.shape
    seq = rows * N_CTX
    hidden = out_own.shape[1]
    heads_width = width // N_CTX
    heads = heads_width // HEAD
    n_shard = width // 128
    f32, bf16 = jnp.float32, jnp.bfloat16
    scale = HEAD ** (-0.5)
    tile = 256
    half = width // 2
    columns_grad = 3 * heads_width

    def kernel(
        own, grad_mixed, mixed, out_own, second, grad_gu, qkv, weights, first,
        cosines, sines, key_pos, query_pos, inputs, grad_residual, gain, second_gain_grad, logits_grad,
        input_grad, small_out, out_share, gate_share, up_share, mixed_share, qkv_share,
        grad_held, parts, left_held, gu_held, w_held, turned, staged, key_sum, value_sum, gain_sum,
        small, small_in, small_kept, small_across, mixed_in,
        loads, left_loads, grad_sends, grad_arrivals, mixed_sends, mixed_arrivals,
        small_sends, small_arrivals, across_sends, across_arrivals, *scratch,
    ):
        reduce = Reduce(parts, parts, *scratch[0:5])
        shares = []
        for k, out in enumerate((gate_share, up_share, mixed_share, qkv_share)):
            start = 8 + Share.COUNT * k
            shares.append(Share(staged, out, scratch[start : start + Share.COUNT]))
        b, c, d, e = shares
        gather = Both(out_own, out_share, *scratch[5:7], AFTER)
        local = scratch[7]
        me = reduce.places[0][0]
        shard = lax.axis_index("shard")
        owners = [lax.rem(shard + k, n_shard) for k in range(1, n_shard)]
        places = [lax.rem(me + k, N_CTX) for k in range(1, N_CTX)]

        def load(k, source, target):
            return pltpu.make_async_copy(source, target, loads.at[k])

        def columns_of(place):
            return pl.ds(pl.multiple_of(heads_width * place, heads_width), heads_width)

        def left_copy(source, step):
            slot = lax.rem(step, 2)
            return pltpu.make_async_copy(
                source.at[:, :, b.exchange.columns_at(step)], left_held.at[slot], left_loads.at[slot]
            )

        def streamed(source):
            left_copy(source, 0).start()

            def left(step):
                @pl.when(step < CHIPS - 1)
                def _():
                    left_copy(source, step + 1).start()

                left_copy(source, step).wait()
                return left_held[lax.rem(step, 2)].reshape(seq, 256)

            return left

        early = [load(1, grad_gu, gu_held), load(3, grad_residual, input_grad)]
        for copy in early:
            copy.start()
        left = streamed(second)
        greet([{"ctx": p} for p in places] + [{"shard": s} for s in owners])
        to_heads = [
            remote(
                grad_mixed.at[:, columns_of(p)], grad_held.at[me], grad_sends, grad_arrivals, k, {"ctx": p}
            )
            for k, p in enumerate(places)
        ]
        for copy in to_heads:
            copy.start()
        grad_held[me] = grad_mixed[:, columns_of(me)]
        gather.begin()
        kept = pltpu.make_async_copy(out_own, out_share.at[me], local)
        kept.start()
        late = [
            load(
                2 * k,
                weights.at[pl.ds(half * k, half), pl.ds(0, columns_grad)],
                w_held.at[:, columns_grad * k : columns_grad * (k + 1)],
            )
            for k in range(2)
        ]
        for copy in late:
            copy.start()
        early[0].wait()
        b.exchange.run(
            left,
            lambda start, count: gu_held[:, start : start + count],
            turned,
            {
                3: [b.reduce.send_far],
                4: [gather.pass_other],
                5: [b.near(0)],
                7: [b.near(1)],
            },
        )
        c.exchange.run(
            streamed(second),
            lambda start, count: gu_held[:, hidden + start : hidden + start + count],
            turned,
            {
                0: [lambda: gather.pass_ring(0)],
                1: [b.side(0)],
                2: [b.side(1)],
                3: [c.reduce.send_far],
                4: [lambda: gather.pass_ring(1)],
                5: [c.near(0)],
                7: [c.near(1)],
            },
        )
        late.append(load(1, qkv, gu_held.at[:, 0:columns_grad]))
        late[-1].start()
        small[...] = jnp.zeros_like(small)
        for s in range(n_shard):
            there = slice(128 * s, 128 * (s + 1))
            small[s, 1:2, :] = second_gain_grad[:, there]
            small[s, 2 : 3 + EXPERTS, :] = logits_grad[: EXPERTS + 1, there]
        for k, p in enumerate(places):
            place = lax.rem(me + N_CTX - 1 - k, N_CTX)
            ref = grad_held.at[place]
            remote(ref, ref, grad_sends, grad_arrivals, k, {"ctx": p}).wait_recv()
        for copy in late:
            copy.wait()
        events = {
            1: [b.reduce.cross],
            3: [c.side(0)],
            4: [c.side(1)],
            5: [b.own],
        }

        def attend(n, carry):
            head, i = n // (seq // tile), lax.rem(n, seq // tile)
            there = pl.ds(pl.multiple_of(i * tile, tile), tile)

            def lanes_of(start):
                return pl.ds(pl.multiple_of(start + HEAD * head, HEAD), HEAD)

            query = gu_held[there, lanes_of(0)]
            key = gu_held[:, lanes_of(heads_width)]
            value = gu_held[:, lanes_of(2 * heads_width)]
            grad = grad_held[pl.ds(2 * i, 2), :, lanes_of(0)].reshape(tile, HEAD)
            scores = contract_last(key, query) * scale
            scores = jnp.where(key_pos[...] <= query_pos[:, there], scores, -1e30)
            raised = jnp.exp(scores - jnp.max(scores, axis=0, keepdims=True))
            probs = raised * (1.0 / jnp.sum(raised, axis=0, keepdims=True))
            grad_probs = contract_last(value, grad)
            centre = jnp.sum(probs * grad_probs, axis=0, keepdims=True)
            grad_scores = (probs * (grad_probs - centre)).astype(bf16)

            @pl.when(i == 0)
            def _():
                key_sum[...] = jnp.zeros_like(key_sum)
                value_sum[...] = jnp.zeros_like(value_sum)

            key_sum[...] += jnp.dot(grad_scores, query, preferred_element_type=f32)
            value_sum[...] += jnp.dot(probs.astype(bf16), grad, preferred_element_type=f32)
            grad_query = contract_first(grad_scores, key) * scale

            def turn_back(values, cosines, sines):
                return (values * cosines - pltpu.roll(values, HEAD // 2, 1) * sines).astype(bf16)

            gu_held[there, lanes_of(columns_grad)] = turn_back(
                grad_query, cosines[there, :], sines[there, :]
            )

            @pl.when(i == seq // tile - 1)
            def _():
                gu_held[:, lanes_of(columns_grad + heads_width)] = turn_back(
                    key_sum[...] * scale, cosines[...], sines[...]
                )
                gu_held[:, lanes_of(columns_grad + 2 * heads_width)] = value_sum[...].astype(bf16)

            for at, todo in events.items():

                @pl.when(n == at)
                def _(todo=todo):
                    for event in todo:
                        event()

            return carry

        lax.fori_loop(0, heads * (seq // tile), attend, 0)

        def start_of(k):
            ahead = 2 - k + 3 * (k // 2) - 2 * (k // 3)
            return lax.rem(me // 2 + ahead, N_CTX // 2) * 2

        def grad_first(k, carry):
            block = start_of(k)
            left = gu_held[
                pl.ds(pl.multiple_of(block * rows, tile), tile), columns_grad : 2 * columns_grad
            ]
            for t in range(4):
                low, start = 512 * (t % 2), columns_grad * (t // 2)
                made = contract_last(left, w_held[low : low + 512, start : start + columns_grad])
                parts[pl.ds(block, 2), :, 512 * t : 512 * (t + 1)] = made.astype(bf16).reshape(
                    2, rows, 512
                )
            pl.when(k == 0)(reduce.send_far)
            pl.when(k == 1)(lambda: reduce.send_near(0))
            pl.when(k == 2)(lambda: reduce.send_near(1))
            return carry

        lax.fori_loop(0, 4, grad_first, 0)
        e.exchange.run(
            streamed(first),
            lambda start, count: gu_held[:, columns_grad + start : columns_grad + start + count],
            turned,
            {
                0: [c.reduce.cross],
                2: [b.gather.pass_other],
                3: [e.reduce.send_far],
                5: [e.near(0), b.ring(0)],
                7: [e.near(1), c.own],
            },
        )
        d.exchange.run(
            lambda step: own[:, b.exchange.columns_at(step)],
            lambda start, count: mixed[:, start : start + count],
            turned,
            {
                0: [lambda: reduce.pass_side(0)],
                1: [lambda: reduce.pass_side(1)],
                3: [d.reduce.send_far],
                4: [b.ring(1)],
                5: [d.near(0)],
                6: [e.side(0), e.side(1)],
                7: [d.near(1), reduce.cross],
            },
        )
        mixed_sum = staged.at[0, 0]
        own_inputs = staged.at[1, 0]
        inputs_load = load(1, inputs, own_inputs)
        inputs_load.start()
        bias = jnp.sum(
            gu_held[:, columns_grad : 2 * columns_grad].astype(f32), axis=0, keepdims=True
        )
        per = heads_width // 128
        for i in range(3):
            for j in range(per):
                block = n_shard * i + per * me + j
                there = slice(heads_width * i + 128 * j, heads_width * i + 128 * (j + 1))
                small[block // 3, pl.ds(3 + EXPERTS + lax.rem(block, 3), 1), :] = bias[:, there]
        e.reduce.cross()
        reduce.ready()
        early[1].wait()
        inputs_load.wait()
        gain_sum[...] = jnp.zeros_like(gain_sum)

        def norm(there):
            normed, factor = normalize(own_inputs[there, :].astype(f32))
            grad = reduce.total(there)
            gain_sum[...] += grad * normed
            input_grad[there, :] += norm_back(grad, normed, factor, gain[...])

        by_rows(rows, norm)
        first_gain_grad = jnp.sum(gain_sum[...], axis=0, keepdims=True)
        for s in range(n_shard):
            small[s, 0:1, :] = first_gain_grad[:, 128 * s : 128 * (s + 1)]
        to_owners = [
            remote(small.at[s], small_in.at[k], small_sends, small_arrivals, k, {"shard": s})
            for k, s in enumerate(owners)
        ]
        for copy in to_owners:
            copy.start()
        d.side(0)()
        d.side(1)()
        c.gather.pass_other()
        e.own()
        c.ring(0)()
        d.reduce.cross()
        e.gather.pass_other()
        total = small[shard]
        for k, copy in enumerate(to_owners):
            copy.wait_recv()
            total = total + small_in[k]
        small_kept[...] = total
        to_places = [
            remote(small_kept, small_across.at[k], across_sends, across_arrivals, k, {"ctx": p})
            for k, p in enumerate(places)
        ]
        for copy in to_places:
            copy.start()
        c.ring(1)()
        e.ring(0)()
        d.sum_into(mixed_sum)
        to_columns = [
            remote(
                mixed_sum.at[:, columns_of(p)], mixed_in.at[k], mixed_sends, mixed_arrivals, k, {"ctx": p}
            )
            for k, p in enumerate(places)
        ]
        for copy in to_columns:
            copy.start()
        e.ring(1)()
        for k, copy in enumerate(to_columns):
            copy.wait_recv()
        part = mixed_sum[:, columns_of(me)].astype(f32)
        for k in range(N_CTX - 1):
            part = part + mixed_in[k].astype(f32)
        d.owned[...] = part.astype(bf16)
        d.pass_own()
        for k, copy in enumerate(to_places):
            copy.wait_recv()
            total = total + small_across[k]
        small_out[...] = total
        d.gather.pass_other()
        d.ring(0)()
        d.ring(1)()
        for copy in to_heads + to_owners + to_places + to_columns:
            copy.wait_send()
        reduce.end()
        kept.wait()
        gather.end()
        for share in (b, c, e, d):
            share.end()

    def shared(count):
        return jax.ShapeDtypeStruct((N_CTX, 128, count), bf16)

    return pl.pallas_call(
        kernel,
        out_shape=(
            jax.ShapeDtypeStruct((rows, width), f32),
            jax.ShapeDtypeStruct((16, 128), f32),
            shared(hidden),
            shared(hidden),
            shared(hidden),
            shared(heads_width),
            shared(3 * heads_width),
        ),
        in_specs=[VMEM] * 4 + [ANY] * 5 + [VMEM] * 4 + [ANY] * 2 + [VMEM] * 3,
        out_specs=(VMEM, VMEM) + (ANY,) * 5,
        scratch_shapes=[
            pltpu.VMEM((N_CTX, rows, heads_width), bf16),
            pltpu.VMEM((N_CTX, rows, width), bf16),
            pltpu.VMEM((2, N_CTX, rows, 256), bf16),
            pltpu.VMEM(grad_gu.shape, bf16),
            pltpu.VMEM((half, 2 * columns_grad), bf16),
            pltpu.VMEM((256, seq), bf16),
            pltpu.VMEM((3, 2, 128, width), bf16),
            pltpu.VMEM((seq, HEAD), f32),
            pltpu.VMEM((seq, HEAD), f32),
            pltpu.VMEM((16, width), f32),
            pltpu.VMEM((n_shard, 16, 128), f32),
            pltpu.VMEM((n_shard - 1, 16, 128), f32),
            pltpu.VMEM((16, 128), f32),
            pltpu.VMEM((N_CTX - 1, 16, 128), f32),
            pltpu.VMEM((N_CTX - 1, 128, heads_width), bf16),
            pltpu.SemaphoreType.DMA((4,)),
            pltpu.SemaphoreType.DMA((2,)),
        ]
        + [pltpu.SemaphoreType.DMA((N_CTX - 1,))] * 4
        + [pltpu.SemaphoreType.DMA((n_shard - 1,))] * 2
        + [pltpu.SemaphoreType.DMA((N_CTX - 1,))] * 2
        + Reduce.scratch(rows, width, 1)
        + [pltpu.SemaphoreType.DMA((Both.SEMAPHORES,))] * 2
        + [pltpu.SemaphoreType.DMA]
        + Share.scratch(hidden) * 2
        + Share.scratch(width, N_CTX)
        + Share.scratch(3 * heads_width),
        compiler_params=params(3, 64 << 20),
        name="backward",
    )(own, grad_mixed, mixed, out_own, second, grad_gu, qkv, weights, first, cosines, sines, key_pos, query_pos, inputs, grad_residual, gain, second_gain_grad, logits_grad)


def local(
    tokens,
    cotangent,
    lengths,
    routes,
    block_order,
    norm_gains,
    qkv_weight,
    qkv_bias,
    out_weight,
    router,
    shared_gate,
    ffn_in,
    ffn_out,
):
    bf16, f32 = jnp.bfloat16, jnp.float32
    n_ctx = lax.axis_size("ctx")
    n_shard = lax.axis_size("shard")
    rows_dev = tokens.shape[1]
    seq_len = rows_dev * n_ctx
    n_blocks = block_order.shape[0]
    block = seq_len // n_blocks
    place = lax.axis_index("ctx")

    every = jnp.arange(seq_len, dtype=jnp.int32)
    matches = (every // block)[:, None] == jnp.arange(n_blocks, dtype=jnp.int32)[None, :]
    pos = jnp.sum(jnp.where(matches, block_order[None, :], 0), axis=1) * block + every % block
    valid = pos < lengths[0]
    valid_rows = valid.astype(f32)[:, None]

    own_valid = lax.dynamic_slice_in_dim(valid_rows, place * rows_dev, rows_dev)
    own_grad = jnp.where(own_valid > 0, cotangent[0], 0).astype(bf16)
    picks = routes[0][:, :, None] == jnp.arange(LANE, dtype=jnp.int32)[None, None, :]
    own_assigned = jnp.sum(picks.astype(f32), axis=1).astype(bf16)
    small = jnp.concatenate(
        [
            norm_gains,
            router.T,
            shared_gate.reshape(1, LANE),
            qkv_bias.reshape(3, LANE),
            jnp.zeros((4, LANE), bf16),
        ]
    )
    cosines, sines = rope_tables(pos)
    key_pos = jnp.where(valid, pos, 2 * seq_len)[:, None]
    (
        residual,
        second_all,
        g_all,
        attn_weights,
        small_all,
        first_all,
        w_gate,
        w_up,
        w_down,
        qkv,
        mixed,
        assigned,
    ) = front(
        jnp.concatenate([tokens[0], own_assigned], axis=1),
        own_grad,
        qkv_weight,
        out_weight,
        ffn_in,
        ffn_out,
        small,
        cosines,
        sines,
        key_pos,
        pos[None],
    )

    (
        grad_residual,
        grad_low,
        grad_mixed,
        output,
        grad_second_gain,
        grad_both,
        _,
        grad_gu,
        _,
        out_own,
    ) = feed_forward(
        second_all,
        g_all,
        assigned,
        w_gate.reshape(D, -1),
        w_up.reshape(D, -1),
        w_down.reshape(D, -1),
        out_weight,
        small_all,
        residual,
        own_grad,
        own_valid,
    )
    first_gain = small_all[:, 0, :].reshape(1, D).astype(f32)
    input_grad, own_small, out_share, gate_share, up_share, mixed_share, qkv_share = backward(
        grad_low,
        grad_mixed,
        mixed,
        out_own,
        second_all,
        grad_gu,
        qkv,
        attn_weights.reshape(D, -1),
        first_all,
        cosines,
        sines,
        key_pos,
        pos[None],
        tokens[0],
        grad_residual,
        first_gain,
        grad_second_gain,
        grad_both,
    )
    own_small = own_small.reshape(-1)
    grad_gains = own_small[: 2 * LANE].reshape(2, LANE)
    grad_router = own_small[2 * LANE : 8 * LANE].reshape(EXPERTS, LANE).T
    grad_shared_gate = own_small[8 * LANE : 9 * LANE]
    grad_bias_out = own_small[9 * LANE : 12 * LANE]

    grad_ffn_out, grad_ffn_in, grad_out, grad_qkv = assemble(
        out_share, gate_share, up_share, mixed_share, qkv_share
    )
    return (
        output[None],
        input_grad[None],
        grad_gains,
        grad_qkv,
        grad_bias_out,
        grad_out,
        grad_router,
        grad_shared_gate,
        grad_ffn_in,
        grad_ffn_out,
    )


def solution(mesh):
    placed = (
        P("shard", "ctx", None),
        P("shard", "ctx", None),
        P("shard"),
        P("shard", "ctx", None),
        P(),
        P(None, "shard"),
        P("shard", None),
        P("shard"),
        P("shard", None),
        P("shard", None),
        P("shard"),
        P("shard", None),
        P("shard", None),
    )
    return jax.shard_map(
        local,
        mesh=mesh,
        in_specs=placed,
        out_specs=(
            P("shard", "ctx", None),
            P("shard", "ctx", None),
            P(None, "shard"),
            P("shard", None),
            P("shard"),
            P("shard", None),
            P("shard", None),
            P("shard"),
            P("shard", None),
            P("shard", None),
        ),
        check_vma=False,
    )
```

```python
import jax
import jax.numpy as jnp
from jax import lax
from jax.experimental import pallas as pl
from jax.experimental.pallas import tpu as pltpu
from jax.sharding import PartitionSpec as P

D = 2048
HEAD = 128
HE = 1408
FS = 5632
EXPERTS = 6
FIN = 28160
FOUT = 14080
LANE = 128
SHARED_BLOCKS = FS // LANE
EXPERT_BLOCKS = HE // LANE
HIDDEN_BLOCKS = SHARED_BLOCKS + EXPERTS * EXPERT_BLOCKS

highest = lax.Precision.HIGHEST
epsilon = 1e-06
rope_base = 1000000.0


def contract_last(left, right):
    return lax.dot_general(
        left, right, (((1,), (1,)), ((), ())), preferred_element_type=jnp.float32
    )


def contract_first(left, right):
    return lax.dot_general(
        left, right, (((0,), (0,)), ((), ())), preferred_element_type=jnp.float32
    )


def dot(left, right):
    return jnp.dot(left, right, preferred_element_type=jnp.float32)


def rope_tables(positions):
    half = HEAD // 2
    lane = jnp.arange(HEAD, dtype=jnp.int32)
    freqs = rope_base ** (-(lane % half).astype(jnp.float32) * 2.0 / HEAD)
    phase = positions.astype(jnp.float32)[:, None] * freqs[None, :]
    return jnp.cos(phase), jnp.where(lane < half, -1.0, 1.0) * jnp.sin(phase)


def normalize(values):
    factor = lax.rsqrt(jnp.mean(values * values, axis=-1, keepdims=True) + epsilon)
    return (values * factor, factor)


def norm_back(grad_normed, normalized, factor, gain):
    scaled = grad_normed * gain
    return factor * (scaled - normalized * jnp.mean(scaled * normalized, axis=-1, keepdims=True))


MESH = pl.DeviceIdType.MESH
ANY = pl.BlockSpec(memory_space=pl.ANY)
VMEM = pl.BlockSpec(memory_space=pltpu.VMEM)
N_CTX = 8
CHIPS = 8
AFTER = 512


def params(number, limit=None):
    return pltpu.CompilerParams(
        collective_id=number, has_side_effects=True, vmem_limit_bytes=limit
    )


def greet(peers):
    semaphore = pltpu.get_barrier_semaphore()
    for peer in peers:
        pl.semaphore_signal(semaphore, inc=1, device_id=peer, device_id_type=MESH)
    pl.semaphore_wait(semaphore, len(peers))


def remote(source, target, sends, arrivals, slot, peer):
    return pltpu.make_async_remote_copy(
        src_ref=source,
        dst_ref=target,
        send_sem=sends.at[slot],
        recv_sem=arrivals.at[slot],
        device_id=peer,
        device_id_type=MESH,
    )


def places_of(axis):
    me = lax.axis_index(axis)
    if axis == "ctx":
        peer = lambda place: {"ctx": place}
    else:
        core, me = lax.rem(me, 2), me // 2
        peer = lambda place: {"shard": 2 * place + core}
    other = me + 1 - 2 * lax.rem(me, 2)
    places = [[lax.rem(base + 2 * k, N_CTX) for k in (0, 1, 3, 2)] for base in (me, other)]
    return places, peer


def by_rows(rows, body):
    step = 16

    def run(i, carry):
        body(pl.ds(pl.multiple_of(i * step, step), step))
        return carry

    lax.fori_loop(0, rows // step, run, 0)


class Gather:
    SEMAPHORES = 9
    PAIRED = 9 + CHIPS

    def __init__(self, own, out, sends, arrivals, axis="ctx", columns=None, offset=0):
        self.block, self.out, self.sends, self.arrivals = own, out, sends, arrivals
        self.columns, self.offset = columns, offset
        self.places, self.peer = places_of(axis)
        (self.me, self.up, self.down, self.far), other = self.places
        self.other = other[0]
        self.half = out.shape[-2] // 2
        self.paired = axis == "shard"
        if self.paired:
            shard = lax.axis_index("shard")
            self.core = lax.rem(shard, 2)
            self.mate = {"shard": shard + 1 - 2 * self.core}
        self.started = []

    def at(self, place, *half):
        if self.paired:
            return self.out.at[(place, self.core) + half]
        if self.columns is None:
            return self.out.at[(place,) + half]
        rows = half[0] if half else pl.ds(0, self.out.shape[1])
        return self.out.at[place, rows, pl.ds(*self.columns)]

    def own(self):
        if self.columns is None:
            return self.block
        return self.block.at[:, pl.ds(*self.columns)]

    def _send(self, slot, source, target, peer):
        def copy():
            return remote(
                source(), target(), self.sends, self.arrivals, slot + self.offset, peer()
            )

        copy().start()
        self.started.append(copy)

    def _await(self, slot, ref):
        peer = self.peer(self.other)
        remote(ref, ref, self.sends, self.arrivals, slot + self.offset, peer).wait_recv()

    def _hand(self, number, place, source=None):
        if self.paired:
            block = lambda: self.at(place)
            self._send(9 + number, source or block, block, lambda: self.mate)

    def _begin(self, slot, place):
        self._send(slot, self.own, lambda: self.at(self.me), lambda: self.peer(place))

    def begin_other(self):
        self._begin(0, self.other)
        self._hand(0, self.me, self.own)

    def begin_ring(self):
        self._begin(1, self.up)
        self._begin(2, self.down)

    def begin(self):
        self.begin_other()
        self.begin_ring()

    def pass_other(self):
        block = lambda: self.at(self.other)
        self._await(0, block())
        self._send(3, block, block, lambda: self.peer(self.up))
        self._send(4, block, block, lambda: self.peer(self.down))
        self._hand(1, self.other)

    def pass_ring(self, column):
        _, up, down, _ = self.places[column]
        first = 1 + 2 * column
        low, high = pl.ds(0, self.half), pl.ds(self.half, self.half)
        self._await(first, self.at(down))
        lower = lambda: self.at(down, low)
        self._send(5 + 2 * column, lower, lower, lambda: self.peer(self.up))
        self._await(first + 1, self.at(up))
        upper = lambda: self.at(up, high)
        self._send(6 + 2 * column, upper, upper, lambda: self.peer(self.down))
        self._hand(2 + 2 * column, down)
        self._hand(3 + 2 * column, up)

    def end(self):
        low, high = pl.ds(0, self.half), pl.ds(self.half, self.half)
        for column in range(2):
            far = self.places[column][3]
            self._await(5 + 2 * column, self.at(far, low))
            self._await(6 + 2 * column, self.at(far, high))
            self._hand(6 + column, far)
        if self.paired:
            (me, up, down, far), (other, other_up, other_down, other_far) = self.places
            for number, place in enumerate(
                (me, other, down, up, other_down, other_up, far, other_far)
            ):
                self._await(9 + number, self.out.at[place, 1 - self.core])
        for copy in self.started:
            copy().wait_send()


class RingFirst(Gather):
    def _across(self, slot, block):
        self._send(slot, block, block, lambda: self.peer(self.other))

    def pass_other(self):
        pass

    def pass_ring(self, column):
        _, up, down, far = self.places[0]
        low, high = pl.ds(0, self.half), pl.ds(self.half, self.half)
        if column:
            for slot, half in ((5, low), (6, high)):
                self._await(slot, self.at(far, half))
                self._across(slot + 2, lambda half=half: self.at(far, half))
            return
        for slot, place, half, toward in ((1, down, low, self.up), (2, up, high, self.down)):
            self._await(slot, self.at(place))
            self._on(slot + 4, place, half, toward)
            self._across(slot + 2, lambda place=place: self.at(place))

    def _on(self, slot, place, half, toward):
        block = lambda: self.at(place, half)
        self._send(slot, block, block, lambda: self.peer(toward))

    def end(self):
        low, high = pl.ds(0, self.half), pl.ds(self.half, self.half)
        other, up, down, far = self.places[1]
        for slot, block in (
            (0, self.at(other)),
            (3, self.at(down)),
            (4, self.at(up)),
            (7, self.at(far, low)),
            (8, self.at(far, high)),
        ):
            self._await(slot, block)
        for copy in self.started:
            copy().wait_send()


class Both:
    SEMAPHORES = 2 * Gather.SEMAPHORES

    def __init__(self, own, out, sends, arrivals, after):
        width = out.shape[-1]
        first = Gather(own, out, sends, arrivals, columns=(0, width - after))
        last = RingFirst(
            own, out, sends, arrivals, columns=(width - after, after), offset=Gather.SEMAPHORES
        )
        self.parts, self.out = (first, last), out
        self.me, self.up, self.down, self.other = first.me, first.up, first.down, first.other

    def begin(self):
        for part in self.parts:
            part.begin()

    def pass_other(self):
        for part in self.parts:
            part.pass_other()

    def pass_ring(self, column):
        for part in self.parts:
            part.pass_ring(column)

    def end(self):
        for part in self.parts:
            part.end()


class Reduce:
    SEMAPHORES = 13

    @staticmethod
    def scratch(rows, width, across=2):
        return [
            pltpu.VMEM((4, rows // 2, width), jnp.bfloat16),
            pltpu.VMEM((4, rows, width), jnp.bfloat16),
            pltpu.VMEM((across, rows, width), jnp.bfloat16),
            pltpu.SemaphoreType.DMA((Reduce.SEMAPHORES,)),
            pltpu.SemaphoreType.DMA((Reduce.SEMAPHORES,)),
        ]

    def __init__(self, parts, held, passing, near, across, sends, arrivals, axis="ctx"):
        self.parts, self.held = parts, held
        self.passing, self.near, self.across = passing, near, across
        self.sends, self.arrivals = sends, arrivals
        self.places, self.peer = places_of(axis)
        _, self.up, self.down, _ = self.places[0]
        self.other = self.places[1][0]
        self.rows, self.width = near.shape[1], near.shape[2]
        self.half = self.rows // 2
        self.started = []

    def _send(self, slot, source, target, place):
        def copy():
            return remote(source(), target(), self.sends, self.arrivals, slot, self.peer(place))

        copy().start()
        self.started.append(copy)

    def _await(self, slot, ref):
        remote(ref, ref, self.sends, self.arrivals, slot, self.peer(self.other)).wait_recv()

    def begin(self):
        self.send_far()
        self.send_near(0)
        self.send_near(1)

    def send_far(self):
        for column in (1, 0):
            self._send_far(column)

    def _send_far(self, column):
        low, high = pl.ds(0, self.half), pl.ds(self.half, self.half)
        far = self.places[column][3]
        slot, a, b = 6 * column, 2 * column, 2 * column + 1
        parts, passing = self.parts, self.passing
        self._send(slot, lambda: parts.at[far, low], lambda: passing.at[a], self.up)
        self._send(slot + 1, lambda: parts.at[far, high], lambda: passing.at[b], self.down)

    def send_near(self, side):
        for column in (1, 0):
            self._send_near(column, side)

    def _send_near(self, column, side):
        half = pl.ds((1 - side) * self.half, self.half)
        toward, place = self.places[column][1 + side], (self.up, self.down)[side]
        index, parts, near = 2 * column + side, self.parts, self.near
        self._send(
            6 * column + 2 + side,
            lambda: parts.at[toward, half],
            lambda: near.at[index, half],
            place,
        )

    def pass_side(self, side):
        for column in (1, 0):
            self._pass_side(column, side)

    def _loop(self, rows, body):
        step = 16

        def run(i, carry):
            body(pl.multiple_of(i * step, step), step)
            return carry

        lax.fori_loop(0, rows // step, run, 0)

    def pass_on(self, column):
        self._pass_side(column, 0)
        self._pass_side(column, 1)

    def _pass_side(self, column, side):
        slot, index, start = 6 * column, 2 * column + side, side * self.half
        toward, place = self.places[column][1 + side], (self.up, self.down)[side]
        passing, near, held = self.passing, self.near, self.held
        self._await(slot + side, passing.at[index])

        def add(row, step):
            there = pl.ds(row, step)
            total = passing[index, there, :].astype(jnp.float32)
            total = total + held[toward, pl.ds(start + row, step), :].astype(jnp.float32)
            passing[index, there, :] = total.astype(jnp.bfloat16)

        self._loop(self.half, add)
        target = pl.ds(start, self.half)
        self._send(
            slot + 4 + side, lambda: passing.at[index], lambda: near.at[index, target], place
        )

    def _near(self, column):
        low, high = pl.ds(0, self.half), pl.ds(self.half, self.half)
        slot = 6 * column
        self._await(slot + 2, self.near.at[2 * column, high])
        self._await(slot + 3, self.near.at[2 * column + 1, low])
        self._await(slot + 4, self.near.at[2 * column, low])
        self._await(slot + 5, self.near.at[2 * column + 1, high])

    def _sum(self, column, there):
        place = self.places[column][0]
        total = self.held[place, there, :].astype(jnp.float32)
        total = total + self.near[2 * column, there, :].astype(jnp.float32)
        return total + self.near[2 * column + 1, there, :].astype(jnp.float32)

    def cross(self):
        self._near(1)
        place, held, across = self.places[1][0], self.held, self.across
        if across.shape[0] == 1:
            kept = lambda: held.at[place]
        else:
            kept = lambda: across.at[1]

        def add(row, step):
            there = pl.ds(row, step)
            kept()[there, :] = self._sum(1, there).astype(jnp.bfloat16)

        self._loop(self.rows, add)
        self._send(12, kept, lambda: across.at[0], self.other)

    def ready(self):
        self._near(0)
        self._await(12, self.across.at[0])

    def total(self, there):
        return self._sum(0, there) + self.across[0, there, :].astype(jnp.float32)

    def end(self):
        for copy in self.started:
            copy().wait_send()


class Spread:
    SEMAPHORES = 7 + 8

    def __init__(self, own, out, sends, arrivals):
        self.own, self.out, self.sends, self.arrivals = own, out, sends, arrivals
        self.me = lax.axis_index("shard")
        self.core, self.chip = lax.rem(self.me, 2), self.me // 2
        self.mate = {"shard": self.me + 1 - 2 * self.core}
        self.started = []

    def _send(self, slot, source, target, peer):
        copy = remote(source, target, self.sends, self.arrivals, slot, peer)
        copy.start()
        self.started.append(copy)

    def _await(self, slot, ref):
        remote(ref, ref, self.sends, self.arrivals, slot, self.mate).wait_recv()

    def _from(self, k, core):
        return self.out.at[2 * lax.rem(self.chip + CHIPS - k, CHIPS) + core]

    def peers(self):
        return [self.mate] + [
            {"shard": 2 * lax.rem(self.chip + k, CHIPS) + self.core} for k in range(1, CHIPS)
        ]

    def begin(self):
        target = self.out.at[self.me]
        for k in range(1, CHIPS):
            peer = {"shard": 2 * lax.rem(self.chip + k, CHIPS) + self.core}
            self._send(k - 1, self.own, target, peer)
        self._send(7, self.own, target, self.mate)

    def hand_on(self):
        for k in range(1, CHIPS):
            block = self._from(k, self.core)
            self._await(k - 1, block)
            self._send(7 + k, block, block, self.mate)

    def end(self):
        for k in range(CHIPS):
            self._await(7 + k, self._from(k, 1 - self.core))
        for copy in self.started:
            copy.wait_send()


def pick_copies(ffn_in, ffn_out, picked, sems):
    count = -(-HIDDEN_BLOCKS // N_CTX)
    place = lax.axis_index("ctx")
    copies = []
    for j in range(count):
        block = place * count + j
        block = block - (block // HIDDEN_BLOCKS) * (block - HIDDEN_BLOCKS + 1)
        routed = (block // SHARED_BLOCKS + 1) // 2
        rest = block - SHARED_BLOCKS
        expert = (rest + SHARED_BLOCKS * (1 - routed)) // EXPERT_BLOCKS * routed
        gate = block * (1 - routed) + (2 * SHARED_BLOCKS + EXPERT_BLOCKS * expert + rest) * routed
        up = gate + SHARED_BLOCKS * (1 - routed) + EXPERT_BLOCKS * routed
        for k, (source, at) in enumerate(((ffn_in, gate), (ffn_in, up), (ffn_out, block))):
            copies.append(
                pltpu.make_async_copy(
                    source.at[:, pl.ds(pl.multiple_of(at * LANE, LANE), LANE)],
                    picked.at[:, LANE * (count * k + j) : LANE * (count * k + j + 1)],
                    sems.at[3 * j + k],
                )
            )
    return copies


def assemble(out_share, gate_share, up_share, mixed_share, qkv_share):
    rows, hidden = out_share.shape[1:]
    width = mixed_share.shape[2]
    count = hidden // LANE
    spans = [(0, SHARED_BLOCKS)] + [
        (SHARED_BLOCKS + EXPERT_BLOCKS * e, EXPERT_BLOCKS) for e in range(EXPERTS)
    ]

    def moves(place, kind):
        result = []
        for index, (first, size) in enumerate(spans):
            low, high = max(first, count * place), min(first + size, count * (place + 1))
            if low >= high:
                continue
            there = low if kind == 0 else first + low + (kind - 1) * size
            result.append(((low - count * place) * LANE, there * LANE, (high - low) * LANE))
        return result

    jobs = []
    for place in range(N_CTX):
        for kind in range(3):
            jobs.append((kind, place, hidden, min(kind, 1), moves(place, kind)))
        jobs.append((3, place, width, 2, [(0, width * place, width)]))
        jobs.append(
            (4, place, 3 * width, 3, [(width * i, D * i + width * place, width) for i in range(3)])
        )
    depth = 6
    most = max(len(job[4]) for job in jobs)

    def kernel(*refs):
        shares, outs = refs[0:5], refs[5:9]
        low, full, loads, stores = refs[9:]

        def load(n):
            kind, place, size, _, _ = jobs[n]
            return pltpu.make_async_copy(
                shares[kind].at[place], low.at[n % depth, :, 0:size], loads.at[n % depth]
            )

        def store(n):
            _, _, _, to, spans_of = jobs[n]
            return [
                pltpu.make_async_copy(
                    full.at[n % depth, :, start : start + size],
                    outs[to].at[:, there : there + size],
                    stores.at[n % depth, k],
                )
                for k, (start, there, size) in enumerate(spans_of)
            ]

        for n in range(depth - 1):
            load(n).start()
        for n in range(len(jobs)):
            if n + depth - 1 < len(jobs):
                load(n + depth - 1).start()
            load(n).wait()
            if n >= depth:
                for copy in store(n - depth):
                    copy.wait()
            slot, size = n % depth, jobs[n][2]

            def widen(there, slot=slot, size=size):
                full[slot, there, 0:size] = low[slot, there, 0:size].astype(jnp.float32)

            by_rows(rows, widen)
            for copy in store(n):
                copy.start()
        for n in range(len(jobs) - depth, len(jobs)):
            for copy in store(n):
                copy.wait()

    f32 = jnp.float32
    return pl.pallas_call(
        kernel,
        out_shape=(
            jax.ShapeDtypeStruct((rows, FOUT), f32),
            jax.ShapeDtypeStruct((rows, FIN), f32),
            jax.ShapeDtypeStruct((rows, D), f32),
            jax.ShapeDtypeStruct((rows, 3 * D), f32),
        ),
        in_specs=[ANY] * 5,
        out_specs=(ANY,) * 4,
        scratch_shapes=[
            pltpu.VMEM((depth, rows, hidden), jnp.bfloat16),
            pltpu.VMEM((depth, rows, hidden), f32),
            pltpu.SemaphoreType.DMA((depth,)),
            pltpu.SemaphoreType.DMA((depth, most)),
        ],
        compiler_params=pltpu.CompilerParams(vmem_limit_bytes=60 << 20),
        name="assemble",
    )(out_share, gate_share, up_share, mixed_share, qkv_share)


def front(block, grad_out, own_valid, qkv_weight, out_weight, ffn_in, ffn_out, small, cosines, sines, key_pos, query_pos):
    rows, width = qkv_weight.shape[0], out_weight.shape[1]
    n_shard = width // rows
    heads_width = width // N_CTX
    heads = heads_width // HEAD
    seq = rows * N_CTX
    extra = block.shape[1] - width
    tile = 256
    scale = HEAD ** (-0.5)
    hidden = -(-HIDDEN_BLOCKS // N_CTX) * LANE
    f32, bf16 = jnp.float32, jnp.bfloat16

    def kernel(
        block, grad_out, own_valid, qkv_weight, out_weight, ffn_in, ffn_out, small, cosines, sines,
        key_pos, query_pos,
        residual, second_all, g_all, weights_out, out_out, small_all, first_out, w_gate, w_up, w_down,
        qkv, mixed_own, assigned,
        own_grad, x_all, weights, out_all, first, staged, picked, params_all, mixed, own, loads, picks, local,
        mixed_sends, mixed_arrivals, *scratch,
    ):
        gather = Gather(block, x_all, *scratch[0:2])
        gather_qkv = Gather(staged, weights, *scratch[2:4], axis="shard")
        spread_small = Spread(small, small_all, *scratch[4:6])
        gather_grad = Both(own_grad, g_all, *scratch[6:8], 768)
        gather_second = Both(own, second_all, *scratch[8:10], 768)
        w_outs = (w_gate, w_up, w_down)
        ffn = [
            Gather(
                picked.at[:, pl.ds(hidden * k, hidden)], out, *scratch[10 + 2 * k : 12 + 2 * k], axis="shard"
            )
            for k, out in enumerate(w_outs)
        ]
        gather_out = Gather(out_weight, out_all, *scratch[16:18], axis="shard")
        me = gather.me
        loaded = [
            pltpu.make_async_copy(
                source.at[:, pl.ds(pl.multiple_of(start + heads_width * me, heads_width), heads_width)],
                staged.at[:, heads_width * i : heads_width * (i + 1)],
                loads.at[i],
            )
            for i, (source, start) in enumerate(
                ((qkv_weight, 0), (qkv_weight, width), (qkv_weight, 2 * width))
            )
        ]
        for copy in loaded:
            copy.start()
        picking = pick_copies(ffn_in, ffn_out, picked, picks)
        for copy in picking:
            copy.start()
        places = [lax.rem(me + k, N_CTX) for k in range(1, N_CTX)]
        greet([{"ctx": p} for p in places] + spread_small.peers())
        gather.begin()
        spread_small.begin()
        for copy in loaded:
            copy.wait()
        gather_qkv.begin()
        gather_out.begin()
        own_grad[...] = (grad_out[...].astype(f32) * own_valid[...]).astype(bf16)
        for copy in picking:
            copy.wait()
        kept = [
            pltpu.make_async_copy(source, target, local.at[k])
            for k, (source, target) in enumerate(
                (
                    (block, x_all.at[me]),
                    (staged, weights.at[spread_small.chip, spread_small.core]),
                    (small, small_all.at[spread_small.me]),
                    (out_weight, gather_out.at(gather_out.me)),
                    (own_grad, g_all.at[me]),
                )
            )
        ] + [
            pltpu.make_async_copy(gather_w.block, gather_w.at(gather_w.me), local.at[5 + k])
            for k, gather_w in enumerate(ffn)
        ]
        for copy in kept:
            copy.start()
        gather.pass_other()
        gather_qkv.pass_other()
        gather_qkv.pass_ring(0)
        spread_small.hand_on()
        gather.pass_ring(0)
        gather_qkv.pass_ring(1)
        gather_out.pass_other()
        gather.pass_ring(1)
        gather_out.pass_ring(0)
        spread_small.end()
        gather_qkv.end()
        gather.end()
        gather_grad.begin()
        ffn[0].begin()
        for copy in kept:
            copy.wait()
        weights_kept = pltpu.make_async_copy(weights, weights_out, local.at[0])
        weights_kept.start()
        assigned[...] = x_all[:, :, width:].reshape(seq, extra)
        params_all[...] = small_all[...].astype(f32)
        gains = [
            jnp.concatenate([params_all[s, k : k + 1, :] for s in range(n_shard)], axis=1)
            for k in range(2)
        ]
        per = heads_width // 128

        def bias_of(i):
            parts_of = []
            for j in range(per):
                at = n_shard * i + per * me + j
                parts_of.append(params_all[at // 3, pl.ds(3 + EXPERTS + lax.rem(at, 3), 1), :])
            return jnp.concatenate(parts_of, axis=1)

        biases = [bias_of(i) for i in range(3)]

        def project(n, carry):
            there = pl.ds(pl.multiple_of(n * tile, tile), tile)

            def norm(k, inner):
                inner_rows = pl.ds(pl.multiple_of(lax.rem(k, rows // 16) * 16, 16), 16)
                at = 2 * n + k // (rows // 16)
                normed, _ = normalize(x_all[at, inner_rows, 0:width].astype(f32))
                first[at, inner_rows, :] = (normed * gains[0]).astype(bf16)
                return inner

            lax.fori_loop(0, tile // 16, norm, 0)
            left = first[pl.ds(2 * n, 2)].reshape(tile, width)
            for i in range(3):
                columns = slice(heads_width * i, heads_width * (i + 1))
                made = biases[i] + jnp.dot(
                    left,
                    weights[:, :, :, columns].reshape(width, heads_width),
                    preferred_element_type=f32,
                )
                if i == 2:
                    qkv[there, columns] = made.astype(bf16)
                    continue
                for h in range(heads):
                    part = made[:, HEAD * h : HEAD * (h + 1)]
                    turned = part * cosines[there, :] + pltpu.roll(part, HEAD // 2, 1) * sines[there, :]
                    start = heads_width * i + HEAD * h
                    qkv[there, start : start + HEAD] = turned.astype(bf16)

            @pl.when(n == 0)
            def _():
                gather_out.pass_ring(1)

            @pl.when(n == 1)
            def _():
                ffn[0].pass_other()

            @pl.when(n == 2)
            def _():
                gather_grad.pass_other()

            return carry

        lax.fori_loop(0, seq // tile, project, 0)
        first_kept = pltpu.make_async_copy(first, first_out, local.at[1])
        first_kept.start()
        events = {
            0: [lambda: gather_grad.pass_ring(0)],
            1: [lambda: ffn[0].pass_ring(0)],
            2: [lambda: ffn[0].pass_ring(1), ffn[1].begin],
            3: [lambda: gather_grad.pass_ring(1)],
            4: [gather_out.end],
            6: [ffn[1].pass_other],
        }

        def attend(n, carry):
            head, i = n // (seq // tile), lax.rem(n, seq // tile)
            there = pl.ds(pl.multiple_of(i * tile, tile), tile)

            def lanes_of(start):
                return pl.ds(pl.multiple_of(start + HEAD * head, HEAD), HEAD)

            scores = scale * contract_last(qkv[:, lanes_of(heads_width)], qkv[there, lanes_of(0)])
            scores = jnp.where(key_pos[...] <= query_pos[:, there], scores, -1e30)
            raised = jnp.exp(scores - jnp.max(scores, axis=0, keepdims=True))
            probs = (raised * (1.0 / jnp.sum(raised, axis=0, keepdims=True))).astype(bf16)
            mixed[there, lanes_of(0)] = contract_first(
                probs, qkv[:, lanes_of(2 * heads_width)]
            ).astype(bf16)
            for at, todo in events.items():

                @pl.when(n == at)
                def _(todo=todo):
                    for event in todo:
                        event()

            return carry

        lax.fori_loop(0, heads * (seq // tile), attend, 0)

        def columns_of(place):
            return pl.ds(pl.multiple_of(heads_width * place, heads_width), heads_width)

        def rows_of(place):
            return pl.ds(pl.multiple_of(rows * place, rows), rows)

        to_rows = [
            remote(
                mixed.at[rows_of(p), :],
                mixed_own.at[:, columns_of(me)],
                mixed_sends,
                mixed_arrivals,
                k,
                {"ctx": p},
            )
            for k, p in enumerate(places)
        ]

        for copy in to_rows:
            copy.start()
        mixed_own[:, columns_of(me)] = mixed[rows_of(me), :]
        out_kept = pltpu.make_async_copy(out_all, out_out, local.at[3])
        out_kept.start()
        ffn[1].pass_ring(0)
        for k, p in enumerate(places):
            ref = mixed_own.at[:, columns_of(lax.rem(me + N_CTX - 1 - k, N_CTX))]
            remote(ref, ref, mixed_sends, mixed_arrivals, k, {"ctx": p}).wait_recv()
        for t in range(width // 512):
            right = out_all[2 * t : 2 * (t + 1)].reshape(512, width)
            residual[:, 512 * t : 512 * (t + 1)] = contract_last(mixed_own[...], right)

        def norm_second(there):
            total = x_all[me, there, 0:width].astype(f32) + residual[there, :]
            residual[there, :] = total
            normed, _ = normalize(total)
            own[there, :] = (normed * gains[1]).astype(bf16)

        by_rows(rows, norm_second)
        gather_second.begin()
        second_kept = pltpu.make_async_copy(own, second_all.at[me], local.at[2])
        second_kept.start()
        ffn[2].begin()
        gather_second.pass_other()
        ffn[1].pass_ring(1)
        ffn[0].end()
        gather_second.pass_ring(0)
        ffn[2].pass_other()
        gather_second.pass_ring(1)
        ffn[2].pass_ring(0)
        ffn[1].end()
        ffn[2].pass_ring(1)
        gather_grad.end()
        for copy in to_rows:
            copy.wait_send()
        for copy in (weights_kept, first_kept, second_kept, out_kept):
            copy.wait()
        gather_second.end()
        ffn[2].end()

    def shape(*dims, kind=bf16):
        return jax.ShapeDtypeStruct(dims, kind)

    pair = [pltpu.SemaphoreType.DMA((Both.SEMAPHORES,))] * 2
    paired = [pltpu.SemaphoreType.DMA((Gather.PAIRED,))] * 2
    return pl.pallas_call(
        kernel,
        out_shape=(
            shape(rows, width, kind=f32),
            shape(N_CTX, rows, width),
            shape(N_CTX, rows, width),
            shape(CHIPS, 2, rows, 3 * heads_width),
            shape(CHIPS, 2, rows, width),
            shape(n_shard, 16, 128),
            shape(N_CTX, rows, width),
            shape(CHIPS, 2, rows, hidden),
            shape(CHIPS, 2, rows, hidden),
            shape(CHIPS, 2, rows, hidden),
            shape(seq, 3 * heads_width),
            shape(rows, width),
            shape(seq, extra),
        ),
        in_specs=[ANY, VMEM, VMEM] + [ANY] * 5 + [VMEM] * 4,
        out_specs=(VMEM, ANY, ANY, ANY, ANY, VMEM, ANY, ANY, ANY, ANY, VMEM, VMEM, VMEM),
        scratch_shapes=[
            pltpu.VMEM((rows, width), bf16),
            pltpu.VMEM((N_CTX,) + block.shape, bf16),
            pltpu.VMEM((CHIPS, 2, rows, 3 * heads_width), bf16),
            pltpu.VMEM((CHIPS, 2, rows, width), bf16),
            pltpu.VMEM((N_CTX, rows, width), bf16),
            pltpu.VMEM((rows, 3 * heads_width), bf16),
            pltpu.VMEM((rows, 3 * hidden), bf16),
            pltpu.VMEM((n_shard, 16, 128), f32),
            pltpu.VMEM((seq, heads_width), bf16),
            pltpu.VMEM((rows, width), bf16),
            pltpu.SemaphoreType.DMA((3,)),
            pltpu.SemaphoreType.DMA((3 * hidden // LANE,)),
            pltpu.SemaphoreType.DMA((8,)),
            pltpu.SemaphoreType.DMA((N_CTX - 1,)),
            pltpu.SemaphoreType.DMA((N_CTX - 1,)),
        ]
        + pair
        + paired
        + [pltpu.SemaphoreType.DMA((Spread.SEMAPHORES,))] * 2
        + pair * 2
        + paired * 4,
        compiler_params=params(0, 56 << 20),
        name="front",
    )(block, grad_out, own_valid, qkv_weight, out_weight, ffn_in, ffn_out, small, cosines, sines, key_pos, query_pos)


class Exchange:
    @staticmethod
    def scratch():
        return [pltpu.SemaphoreType.DMA((CHIPS,)), pltpu.SemaphoreType.DMA((CHIPS,))]

    def __init__(self, parts, staged, sends, arrivals):
        self.parts, self.staged = parts, staged
        self.sems = (sends, arrivals)
        self.width = parts.shape[2]
        me = lax.axis_index("shard")
        self.core, self.chip = lax.rem(me, 2), me // 2
        self.mate = {"shard": me + 1 - 2 * self.core}

    def chip_at(self, step):
        base = self.chip + (1 - lax.rem(step, 2)) * (1 - 2 * lax.rem(self.chip, 2))
        b = step // 2
        ahead = 2 - b + 3 * (b // 2) - 2 * (b // 3)
        return 2 * lax.rem(base // 2 + ahead, 4) + lax.rem(base, 2)

    def stage(self, slot, core):
        if len(self.staged.shape) == 2:
            return self.staged.at[pl.ds(pl.multiple_of((2 * slot + core) * 128, 128), 128), :]
        return self.staged.at[slot, core]

    def columns_at(self, step):
        return pl.ds(pl.multiple_of(self.chip_at(step) * 256, 256), 256)

    def _pair(self, step):
        return remote(
            self.stage(lax.rem(step, 3), 1 - self.core).at[:, pl.ds(0, self.width)],
            self.parts.at[self.chip_at(step)],
            *self.sems,
            step,
            self.mate,
        )

    def finish(self, step):
        chip, slot, width = self.chip_at(step), lax.rem(step, 3), self.width
        ref = self.parts.at[chip]
        remote(ref, ref, *self.sems, step, self.mate).wait_recv()

        def add(there):
            total = self.parts[chip, there, :].astype(jnp.float32)
            total = total + self.stage(slot, self.core)[there, 0:width].astype(jnp.float32)
            self.parts[chip, there, :] = total.astype(jnp.bfloat16)

        by_rows(128, add)

    def run(self, left, right, turned, between):
        width = self.width
        tile = 896 if width % 896 == 0 else min(width, 1024)

        def step_of(step, carry):
            @pl.when(step >= 3)
            def _():
                self._pair(step - 3).wait_send()

            slot = lax.rem(step, 3)
            rows = left(step)
            depth = rows.shape[0]
            turned[:, 0:depth] = rows.T
            for start in range(0, width, tile):
                made = jnp.dot(
                    turned[:, 0:depth], right(start, tile), preferred_element_type=jnp.float32
                ).astype(jnp.bfloat16)
                self.stage(slot, 0)[:, start : start + tile] = made[:128]
                self.stage(slot, 1)[:, start : start + tile] = made[128:]
            self._pair(step).start()

            @pl.when(step >= 2)
            def _():
                self.finish(step - 2)

            for at, events in between.items():

                @pl.when(step == at)
                def _(events=events):
                    for event in events:
                        event()

            return carry

        lax.fori_loop(0, CHIPS, step_of, 0)
        self.finish(CHIPS - 2)
        self.finish(CHIPS - 1)
        for step in range(CHIPS - 3, CHIPS):
            self._pair(step).wait_send()


def feed_forward(second, grad_out, assigned, w_gate, w_up, w_down, out_weights, small, residual, own_grad, own_valid):
    _, rows, width = second.shape
    seq = rows * N_CTX
    hidden = w_gate.shape[1]
    lanes = 128
    n_shard = small.shape[0]
    pair = 2 * rows
    tile = 896
    f32, bf16 = jnp.float32, jnp.bfloat16

    def kernel(
        second, grad_out, assigned, w_gate, w_up, w_down, out_weights, small, residual, own_grad, own_valid,
        grad_residual, grad_low, grad_mixed, output, grad_gain, grad_logits, act_out, grad_gu_out,
        out_owned,
        second_held, grad_held, in_held, down_held, act, grad_gu, weights, dots, dots_in, gain_sum,
        logit_low,
        back_parts, ffn_parts, dot_sends, dot_arrivals, loads, weight_loads, stores, *scratch,
    ):
        back = Reduce(back_parts, back_parts, *scratch[:5])
        ahead = Reduce(ffn_parts, ffn_parts, *scratch[5:10])
        share, act_held = down_held.at[pl.ds(0, CHIPS)], down_held.at[pl.ds(CHIPS, N_CTX)]
        staged = in_held.at[pl.ds(0, 768), pl.ds(0, hidden)]
        turned = in_held.at[pl.ds(768, 256), pl.ds(0, seq)]
        exchange = Exchange(share, staged, *scratch[10:12])
        sums = Reduce(share, share, *scratch[12:17], axis="shard")
        free = scratch[17]
        own, other = back.places
        me = own[0]
        peers = [lax.rem(me + k, N_CTX) for k in range(1, N_CTX)]
        copies = [
            pltpu.make_async_copy(source, target, loads.at[k])
            for k, (source, target) in enumerate(((second, second_held), (grad_out, grad_held)))
        ]
        for copy in copies:
            copy.start()

        def weight_copies(t):
            copies = []
            for k, (source, target, here) in enumerate(
                ((w_gate, in_held, 0), (w_up, in_held, hidden), (w_down, down_held, 0))
            ):
                every = (slice(None),) * (len(target.shape) - 1)
                source = source.at[every + (pl.ds(pl.multiple_of(tile * t, tile), tile),)]
                target = target.at[every + (pl.ds(pl.multiple_of(here + tile * t, tile), tile),)]
                copies.append(pltpu.make_async_copy(source, target, weight_loads.at[3 * t + k]))
            return copies

        def start_weights(t, carry):
            for copy in weight_copies(t):
                copy.start()
            return carry

        lax.fori_loop(0, hidden // tile, start_weights, 0)
        plane_peers = [sums.peer(p) for p in (sums.up, sums.down, sums.other)]
        greet([{"ctx": p} for p in peers] + plane_peers + [exchange.mate])
        logit_low[...] = jnp.zeros_like(logit_low)
        gains = []
        for s in range(n_shard):
            held = small[s].astype(f32)
            gains.append(held[1:2])
            part = jnp.concatenate([held[2 : 3 + EXPERTS], jnp.zeros((15 - EXPERTS, 128), f32)], axis=0)
            logit_low[0:16, 128 * s : 128 * (s + 1)] = part.astype(bf16)
        gain = jnp.concatenate(gains, axis=1)
        for copy in copies:
            copy.wait()

        def stored(slot, start):
            there = pl.ds(start, pair)
            return [
                pltpu.make_async_copy(
                    act.at[slot, pl.ds(rows * k, rows)], act_out.at[start // rows + k], stores.at[slot, 1 + k]
                )
                for k in range(2)
            ] + [
                pltpu.make_async_copy(grad_gu.at[slot], grad_gu_out.at[there, :], stores.at[slot, 0]),
            ]

        def dot_copy(slot, place):
            return remote(
                dots.at[place], dots_in.at[slot], dot_sends, dot_arrivals, slot, {"ctx": place}
            )

        def start_of(b):
            ahead = 2 - b + 3 * (b // 2) - 2 * (b // 3)
            return pl.multiple_of(lax.rem(me // 2 + ahead, N_CTX // 2) * pair, pair)

        def branch_of(j):
            at = me * (hidden // LANE) + j
            routed = (at // SHARED_BLOCKS + 1) // 2
            expert = (at - SHARED_BLOCKS) // EXPERT_BLOCKS
            return (1 - routed) * EXPERTS + routed * expert + 100 * (at // HIDDEN_BLOCKS)

        def block(b, carry):
            start = start_of(b)
            slot = 0
            first = pl.multiple_of(start // rows, 2)

            @pl.when(b >= 1)
            def _():
                for copy in stored(slot, start_of(b - 1)):
                    copy.wait()

            def rows_of(ref):
                return ref[pl.ds(first, 2)].reshape(pair, width)

            logits = contract_last(rows_of(second_held), logit_low[...])
            lane = lax.broadcasted_iota(jnp.int32, logits.shape, 1)
            named = assigned[pl.ds(start, pair), :] > 0
            raised = jnp.where(named, logits, -1e30)
            raised = jnp.exp(raised - jnp.max(raised, axis=-1, keepdims=True))
            raised = jnp.where(named, raised, 0.0)
            gates = raised / jnp.sum(raised, axis=-1, keepdims=True)
            gates = jnp.where(lane == EXPERTS, jax.nn.sigmoid(logits), gates)
            weights[pl.ds(start, pair), :] = gates
            dots[pl.ds(first, 2)] = jnp.zeros((2, rows, lanes), f32)

            def hidden_tile(t, carry):
                @pl.when(b == 0)
                def _():
                    for copy in weight_copies(t):
                        copy.wait()

                low = pl.ds(pl.multiple_of(tile * t, tile), tile)
                high = pl.ds(pl.multiple_of(hidden + tile * t, tile), tile)
                rows_in = rows_of(second_held)
                gate = jnp.dot(rows_in, in_held[:, low], preferred_element_type=f32)
                upward = jnp.dot(rows_in, in_held[:, high], preferred_element_type=f32)
                raw = jnp.dot(
                    rows_of(grad_held),
                    down_held[:, :, low].reshape(width, tile),
                    preferred_element_type=f32,
                )
                gates = weights[pl.ds(start, pair), :]
                lane = lax.broadcasted_iota(jnp.int32, gates.shape, 1)
                branches = [branch_of(tile // LANE * t + j) for j in range(tile // LANE)]
                held = jnp.concatenate(
                    [
                        jnp.broadcast_to(
                            jnp.sum(jnp.where(lane == n, gates, 0.0), axis=1, keepdims=True),
                            (pair, LANE),
                        )
                        for n in branches
                    ],
                    axis=1,
                )
                squashed = jax.nn.sigmoid(gate)
                swished = gate * squashed
                value = swished * upward
                act[slot, :, low] = (value * held).astype(bf16)
                products = raw * value
                part = dots[pl.ds(first, 2)].reshape(pair, lanes)
                for j, n in enumerate(branches):
                    inner = jnp.sum(products[:, LANE * j : LANE * (j + 1)], axis=1, keepdims=True)
                    part = part + jnp.where(lane == n, inner, 0.0)
                dots[pl.ds(first, 2)] = part.reshape(2, rows, lanes)
                grad = raw * held
                grad_gu[slot, :, low] = (
                    grad * upward * squashed * (1.0 + gate * (1.0 - squashed))
                ).astype(bf16)
                grad_gu[slot, :, high] = (grad * swished).astype(bf16)
                return carry

            lax.fori_loop(0, hidden // tile, hidden_tile, 0)
            for copy in stored(slot, start):
                copy.start()

            def out_tile(t, carry):
                there = pl.ds(pl.multiple_of(1024 * t, 1024), 1024)
                for parts, left, right in (
                    (back_parts, grad_gu, lambda: in_held[there, :]),
                    (ffn_parts, act, lambda: down_held[pl.ds(8 * t, 8)].reshape(1024, hidden)),
                ):
                    made = contract_last(left[slot], right())
                    parts[pl.ds(first, 2), :, there] = made.astype(bf16).reshape(2, rows, 1024)
                return carry

            lax.fori_loop(0, width // 1024, out_tile, 0)

            def far():
                back.send_far()
                ahead.send_far()
                dot_copy(0, own[3]).start()
                dot_copy(1, other[3]).start()

            def near(side):
                back.send_near(side)
                back.pass_side(side)
                ahead.send_near(side)
                ahead.pass_side(side)
                dot_copy(2 + 2 * side, own[1 + side]).start()
                dot_copy(3 + 2 * side, other[1 + side]).start()

            pl.when(b == 0)(far)
            pl.when(b == 1)(lambda: near(0))
            pl.when(b == 2)(lambda: near(1))
            return carry

        lax.fori_loop(0, 4, block, 0)
        dot_copy(6, other[0]).start()
        for copy in stored(0, start_of(3)):
            copy.wait()
        act_load = pltpu.make_async_copy(act_out, act_held, loads.at[0])
        act_load.start()
        pl.semaphore_signal(free, inc=1, device_id=exchange.mate, device_id_type=MESH)
        pl.semaphore_wait(free, 1)
        act_load.wait()
        exchange.run(
            lambda step: grad_held[:, :, exchange.columns_at(step)].reshape(seq, 256),
            lambda start, count: down_held[CHIPS:, :, start : start + count].reshape(seq, count),
            turned,
            {
                2: [back.cross],
                3: [sums.send_far],
                5: [lambda: sums.send_near(0)],
                7: [lambda: sums.send_near(1)],
            },
        )
        out_load = pltpu.make_async_copy(out_weights, in_held.at[:, 0:width], loads.at[1])
        out_load.start()
        ahead.cross()
        sums.pass_side(0)
        sums.pass_side(1)
        back.ready()
        for k in range(7):
            ref = dots_in.at[k]
            remote(ref, ref, dot_sends, dot_arrivals, k, {"ctx": other[0]}).wait_recv()
        total_dots = dots[me]
        for k in range(7):
            total_dots = total_dots + dots_in[k]
        held = weights[pl.ds(pl.multiple_of(me * rows, rows), rows), :]
        lane = lax.broadcasted_iota(jnp.int32, held.shape, 1)
        routed = lane < EXPERTS
        centre = jnp.sum(jnp.where(routed, held * total_dots, 0.0), axis=-1, keepdims=True)
        both = jnp.where(
            routed,
            held * (total_dots - centre),
            jnp.where(lane == EXPERTS, total_dots * held * (1.0 - held), 0.0),
        )
        grad_logits[...] = lax.dot_general(
            both,
            second_held[me].astype(f32),
            (((0,), (0,)), ((), ())),
            precision=highest,
            preferred_element_type=f32,
        )[0:8]
        for t in range(width // 512):
            there = slice(512 * t, 512 * (t + 1))
            grad_residual[:, there] = jnp.dot(
                both, logit_low[:, there].astype(f32), precision=highest, preferred_element_type=f32
            )
        gain_sum[...] = jnp.zeros_like(gain_sum)

        def norm(there):
            normed, factor = normalize(residual[there, :])
            grad = back.total(there) + grad_residual[there, :]
            gain_sum[...] += grad * normed
            grad = norm_back(grad, normed, factor, gain)
            grad = grad + own_grad[there, :].astype(f32) * own_valid[there, :]
            grad_residual[there, :] = grad
            grad_low[there, :] = grad.astype(bf16)

        by_rows(rows, norm)
        grad_gain[...] = jnp.sum(gain_sum[...], axis=0, keepdims=True)
        out_load.wait()
        for t in range(width // 512):
            there = slice(512 * t, 512 * (t + 1))
            grad_mixed[:, there] = jnp.dot(
                grad_low[...], in_held[:, there], preferred_element_type=f32
            ).astype(bf16)
        ahead.ready()

        def finish(there):
            total = residual[there, :] + ahead.total(there)
            output[there, :] = (total * own_valid[there, :]).astype(bf16)

        by_rows(rows, finish)
        sums.cross()
        sums.ready()

        def keep(there):
            out_owned[there, :] = sums.total(there).astype(bf16)

        by_rows(128, keep)
        sums.end()
        back.end()
        ahead.end()
        for slot, place in enumerate((own[3], other[3], own[1], other[1], own[2], other[2], other[0])):
            dot_copy(slot, place).wait_send()

    return pl.pallas_call(
        kernel,
        out_shape=(
            jax.ShapeDtypeStruct((rows, width), f32),
            jax.ShapeDtypeStruct((rows, width), bf16),
            jax.ShapeDtypeStruct((rows, width), bf16),
            jax.ShapeDtypeStruct((rows, width), bf16),
            jax.ShapeDtypeStruct((1, width), f32),
            jax.ShapeDtypeStruct((8, width), f32),
            jax.ShapeDtypeStruct((N_CTX, rows, hidden), bf16),
            jax.ShapeDtypeStruct((seq, 2 * hidden), bf16),
            jax.ShapeDtypeStruct((128, hidden), bf16),
        ),
        in_specs=[ANY, ANY, VMEM] + [ANY] * 4 + [VMEM] * 4,
        out_specs=(VMEM,) * 6 + (ANY,) * 2 + (VMEM,),
        scratch_shapes=[
            pltpu.VMEM(second.shape, bf16),
            pltpu.VMEM(grad_out.shape, bf16),
            pltpu.VMEM((width, 2 * hidden), bf16),
            pltpu.VMEM((width // 128, 128, hidden), bf16),
            pltpu.VMEM((1, pair, hidden), bf16),
            pltpu.VMEM((1, pair, 2 * hidden), bf16),
            pltpu.VMEM((seq, lanes), f32),
            pltpu.VMEM((N_CTX, rows, lanes), f32),
            pltpu.VMEM((N_CTX - 1, rows, lanes), f32),
            pltpu.VMEM((16, width), f32),
            pltpu.VMEM((lanes, width), bf16),
            pltpu.VMEM(second.shape, bf16),
            pltpu.VMEM(second.shape, bf16),
            pltpu.SemaphoreType.DMA((N_CTX - 1,)),
            pltpu.SemaphoreType.DMA((N_CTX - 1,)),
            pltpu.SemaphoreType.DMA((3,)),
            pltpu.SemaphoreType.DMA((3 * hidden // tile,)),
            pltpu.SemaphoreType.DMA((1, 3)),
        ]
        + Reduce.scratch(rows, width, 1) * 2
        + Exchange.scratch()
        + Reduce.scratch(128, hidden, 1)
        + [pltpu.SemaphoreType.REGULAR],
        compiler_params=params(2, 64 << 20),
        name="feed_forward",
    )(second, grad_out, assigned, w_gate, w_up, w_down.reshape(width // 128, 128, hidden), out_weights, small, residual, own_grad, own_valid)


class Share:
    @staticmethod
    def scratch(width, split=1):
        own = width // split
        return (
            [pltpu.VMEM((CHIPS, 128, width), jnp.bfloat16), pltpu.VMEM((128, own), jnp.bfloat16)]
            + Exchange.scratch()
            + Reduce.scratch(128, width, 1)
            + [pltpu.SemaphoreType.DMA((Both.SEMAPHORES,))] * 2
            + [pltpu.SemaphoreType.DMA]
        )

    COUNT = 2 + 2 + 5 + 2 + 1

    def __init__(self, staged, out, scratch):
        parts, self.owned = scratch[0:2]
        self.exchange = Exchange(parts, staged, *scratch[2:4])
        self.reduce = Reduce(parts, parts, *scratch[4:9], axis="shard")
        if out.shape[-1] > 2 * AFTER:
            self.gather = Both(self.owned, out, *scratch[9:11], AFTER)
        else:
            self.gather = Gather(self.owned, out, *scratch[9:11])
        self.local = scratch[11]

    def near(self, side):
        return lambda: self.reduce.send_near(side)

    def side(self, side):
        return lambda: self.reduce.pass_side(side)

    def ring(self, column):
        return lambda: self.gather.pass_ring(column)

    def own(self):
        self.sum_into(self.owned)
        self.pass_own()

    def sum_into(self, ref):
        self.reduce.ready()

        def keep(there):
            ref[there, :] = self.reduce.total(there).astype(jnp.bfloat16)

        by_rows(128, keep)

    def pass_own(self):
        self.gather.begin()
        self._kept().start()

    def _kept(self):
        return pltpu.make_async_copy(
            self.owned, self.gather.out.at[self.gather.me], self.local
        )

    def end(self):
        self._kept().wait()
        self.gather.end()
        self.reduce.end()


def backward(own, grad_mixed, mixed, out_own, second, grad_gu, qkv, weights, first, cosines, sines, key_pos, query_pos, inputs, grad_residual, gain, second_gain_grad, logits_grad):
    rows, width = own.shape
    seq = rows * N_CTX
    hidden = out_own.shape[1]
    heads_width = width // N_CTX
    heads = heads_width // HEAD
    n_shard = width // 128
    f32, bf16 = jnp.float32, jnp.bfloat16
    scale = HEAD ** (-0.5)
    tile = 256
    half = width // 2
    columns_grad = 3 * heads_width

    def kernel(
        own, grad_mixed, mixed, out_own, second, grad_gu, qkv, weights, first,
        cosines, sines, key_pos, query_pos, inputs, grad_residual, gain, second_gain_grad, logits_grad,
        input_grad, small_out, out_share, gate_share, up_share, mixed_share, qkv_share,
        grad_held, parts, left_held, gu_held, w_held, turned, staged, key_sum, value_sum, gain_sum,
        small, small_in, small_kept, small_across, mixed_in,
        loads, left_loads, grad_sends, grad_arrivals, mixed_sends, mixed_arrivals,
        small_sends, small_arrivals, across_sends, across_arrivals, *scratch,
    ):
        reduce = Reduce(parts, parts, *scratch[0:5])
        shares = []
        for k, out in enumerate((gate_share, up_share, mixed_share, qkv_share)):
            start = 8 + Share.COUNT * k
            shares.append(Share(staged, out, scratch[start : start + Share.COUNT]))
        b, c, d, e = shares
        gather = Both(out_own, out_share, *scratch[5:7], AFTER)
        local = scratch[7]
        me = reduce.places[0][0]
        shard = lax.axis_index("shard")
        owners = [lax.rem(shard + k, n_shard) for k in range(1, n_shard)]
        places = [lax.rem(me + k, N_CTX) for k in range(1, N_CTX)]

        def load(k, source, target):
            return pltpu.make_async_copy(source, target, loads.at[k])

        def columns_of(place):
            return pl.ds(pl.multiple_of(heads_width * place, heads_width), heads_width)

        def left_copy(source, step):
            slot = lax.rem(step, 2)
            return pltpu.make_async_copy(
                source.at[:, :, b.exchange.columns_at(step)], left_held.at[slot], left_loads.at[slot]
            )

        def streamed(source):
            left_copy(source, 0).start()

            def left(step):
                @pl.when(step < CHIPS - 1)
                def _():
                    left_copy(source, step + 1).start()

                left_copy(source, step).wait()
                return left_held[lax.rem(step, 2)].reshape(seq, 256)

            return left

        early = [load(1, grad_gu, gu_held), load(3, grad_residual, input_grad)]
        for copy in early:
            copy.start()
        left = streamed(second)
        greet([{"ctx": p} for p in places] + [{"shard": s} for s in owners])
        to_heads = [
            remote(
                grad_mixed.at[:, columns_of(p)], grad_held.at[me], grad_sends, grad_arrivals, k, {"ctx": p}
            )
            for k, p in enumerate(places)
        ]
        for copy in to_heads:
            copy.start()
        grad_held[me] = grad_mixed[:, columns_of(me)]
        gather.begin()
        kept = pltpu.make_async_copy(out_own, out_share.at[me], local)
        kept.start()
        late = [
            load(
                2 * k,
                weights.at[pl.ds(half * k, half), pl.ds(0, columns_grad)],
                w_held.at[:, columns_grad * k : columns_grad * (k + 1)],
            )
            for k in range(2)
        ]
        for copy in late:
            copy.start()
        early[0].wait()
        b.exchange.run(
            left,
            lambda start, count: gu_held[:, start : start + count],
            turned,
            {
                3: [b.reduce.send_far],
                4: [gather.pass_other],
                5: [b.near(0)],
                7: [b.near(1)],
            },
        )
        c.exchange.run(
            streamed(second),
            lambda start, count: gu_held[:, hidden + start : hidden + start + count],
            turned,
            {
                0: [lambda: gather.pass_ring(0)],
                1: [b.side(0)],
                2: [b.side(1)],
                3: [c.reduce.send_far],
                4: [lambda: gather.pass_ring(1)],
                5: [c.near(0)],
                7: [c.near(1)],
            },
        )
        late.append(load(1, qkv, gu_held.at[:, 0:columns_grad]))
        late[-1].start()
        small[...] = jnp.zeros_like(small)
        for s in range(n_shard):
            there = slice(128 * s, 128 * (s + 1))
            small[s, 1:2, :] = second_gain_grad[:, there]
            small[s, 2 : 3 + EXPERTS, :] = logits_grad[: EXPERTS + 1, there]
        for k, p in enumerate(places):
            place = lax.rem(me + N_CTX - 1 - k, N_CTX)
            ref = grad_held.at[place]
            remote(ref, ref, grad_sends, grad_arrivals, k, {"ctx": p}).wait_recv()
        for copy in late:
            copy.wait()
        events = {
            1: [b.reduce.cross],
            3: [c.side(0)],
            4: [c.side(1)],
            5: [b.own],
        }

        def attend(n, carry):
            head, i = n // (seq // tile), lax.rem(n, seq // tile)
            there = pl.ds(pl.multiple_of(i * tile, tile), tile)

            def lanes_of(start):
                return pl.ds(pl.multiple_of(start + HEAD * head, HEAD), HEAD)

            query = gu_held[there, lanes_of(0)]
            key = gu_held[:, lanes_of(heads_width)]
            value = gu_held[:, lanes_of(2 * heads_width)]
            grad = grad_held[pl.ds(2 * i, 2), :, lanes_of(0)].reshape(tile, HEAD)
            scores = contract_last(key, query) * scale
            scores = jnp.where(key_pos[...] <= query_pos[:, there], scores, -1e30)
            raised = jnp.exp(scores - jnp.max(scores, axis=0, keepdims=True))
            probs = raised * (1.0 / jnp.sum(raised, axis=0, keepdims=True))
            grad_probs = contract_last(value, grad)
            centre = jnp.sum(probs * grad_probs, axis=0, keepdims=True)
            grad_scores = (probs * (grad_probs - centre)).astype(bf16)

            @pl.when(i == 0)
            def _():
                key_sum[...] = jnp.zeros_like(key_sum)
                value_sum[...] = jnp.zeros_like(value_sum)

            key_sum[...] += jnp.dot(grad_scores, query, preferred_element_type=f32)
            value_sum[...] += jnp.dot(probs.astype(bf16), grad, preferred_element_type=f32)
            grad_query = contract_first(grad_scores, key) * scale

            def turn_back(values, cosines, sines):
                return (values * cosines - pltpu.roll(values, HEAD // 2, 1) * sines).astype(bf16)

            gu_held[there, lanes_of(columns_grad)] = turn_back(
                grad_query, cosines[there, :], sines[there, :]
            )

            @pl.when(i == seq // tile - 1)
            def _():
                gu_held[:, lanes_of(columns_grad + heads_width)] = turn_back(
                    key_sum[...] * scale, cosines[...], sines[...]
                )
                gu_held[:, lanes_of(columns_grad + 2 * heads_width)] = value_sum[...].astype(bf16)

            for at, todo in events.items():

                @pl.when(n == at)
                def _(todo=todo):
                    for event in todo:
                        event()

            return carry

        lax.fori_loop(0, heads * (seq // tile), attend, 0)

        def start_of(k):
            ahead = 2 - k + 3 * (k // 2) - 2 * (k // 3)
            return lax.rem(me // 2 + ahead, N_CTX // 2) * 2

        def grad_first(k, carry):
            block = start_of(k)
            left = gu_held[
                pl.ds(pl.multiple_of(block * rows, tile), tile), columns_grad : 2 * columns_grad
            ]
            for t in range(4):
                low, start = 512 * (t % 2), columns_grad * (t // 2)
                made = contract_last(left, w_held[low : low + 512, start : start + columns_grad])
                parts[pl.ds(block, 2), :, 512 * t : 512 * (t + 1)] = made.astype(bf16).reshape(
                    2, rows, 512
                )
            pl.when(k == 0)(reduce.send_far)
            pl.when(k == 1)(lambda: reduce.send_near(0))
            pl.when(k == 2)(lambda: reduce.send_near(1))
            return carry

        lax.fori_loop(0, 4, grad_first, 0)
        e.exchange.run(
            streamed(first),
            lambda start, count: gu_held[:, columns_grad + start : columns_grad + start + count],
            turned,
            {
                0: [c.reduce.cross],
                2: [b.gather.pass_other],
                3: [e.reduce.send_far],
                5: [e.near(0), b.ring(0)],
                7: [e.near(1), c.own],
            },
        )
        d.exchange.run(
            lambda step: own[:, b.exchange.columns_at(step)],
            lambda start, count: mixed[:, start : start + count],
            turned,
            {
                0: [lambda: reduce.pass_side(0)],
                1: [lambda: reduce.pass_side(1)],
                3: [d.reduce.send_far],
                4: [b.ring(1)],
                5: [d.near(0)],
                6: [e.side(0), e.side(1)],
                7: [d.near(1), reduce.cross],
            },
        )
        mixed_sum = staged.at[0, 0]
        own_inputs = staged.at[1, 0]
        inputs_load = load(1, inputs, own_inputs)
        inputs_load.start()
        bias = jnp.sum(
            gu_held[:, columns_grad : 2 * columns_grad].astype(f32), axis=0, keepdims=True
        )
        per = heads_width // 128
        for i in range(3):
            for j in range(per):
                block = n_shard * i + per * me + j
                there = slice(heads_width * i + 128 * j, heads_width * i + 128 * (j + 1))
                small[block // 3, pl.ds(3 + EXPERTS + lax.rem(block, 3), 1), :] = bias[:, there]
        e.reduce.cross()
        reduce.ready()
        early[1].wait()
        inputs_load.wait()
        gain_sum[...] = jnp.zeros_like(gain_sum)

        def norm(there):
            normed, factor = normalize(own_inputs[there, :].astype(f32))
            grad = reduce.total(there)
            gain_sum[...] += grad * normed
            input_grad[there, :] += norm_back(grad, normed, factor, gain[...])

        by_rows(rows, norm)
        first_gain_grad = jnp.sum(gain_sum[...], axis=0, keepdims=True)
        for s in range(n_shard):
            small[s, 0:1, :] = first_gain_grad[:, 128 * s : 128 * (s + 1)]
        to_owners = [
            remote(small.at[s], small_in.at[k], small_sends, small_arrivals, k, {"shard": s})
            for k, s in enumerate(owners)
        ]
        for copy in to_owners:
            copy.start()
        d.side(0)()
        d.side(1)()
        c.gather.pass_other()
        e.own()
        c.ring(0)()
        d.reduce.cross()
        e.gather.pass_other()
        total = small[shard]
        for k, copy in enumerate(to_owners):
            copy.wait_recv()
            total = total + small_in[k]
        small_kept[...] = total
        to_places = [
            remote(small_kept, small_across.at[k], across_sends, across_arrivals, k, {"ctx": p})
            for k, p in enumerate(places)
        ]
        for copy in to_places:
            copy.start()
        c.ring(1)()
        e.ring(0)()
        d.sum_into(mixed_sum)
        to_columns = [
            remote(
                mixed_sum.at[:, columns_of(p)], mixed_in.at[k], mixed_sends, mixed_arrivals, k, {"ctx": p}
            )
            for k, p in enumerate(places)
        ]
        for copy in to_columns:
            copy.start()
        e.ring(1)()
        for k, copy in enumerate(to_columns):
            copy.wait_recv()
        part = mixed_sum[:, columns_of(me)].astype(f32)
        for k in range(N_CTX - 1):
            part = part + mixed_in[k].astype(f32)
        d.owned[...] = part.astype(bf16)
        d.pass_own()
        for k, copy in enumerate(to_places):
            copy.wait_recv()
            total = total + small_across[k]
        small_out[...] = total
        d.gather.pass_other()
        d.ring(0)()
        d.ring(1)()
        for copy in to_heads + to_owners + to_places + to_columns:
            copy.wait_send()
        reduce.end()
        kept.wait()
        gather.end()
        for share in (b, c, e, d):
            share.end()

    def shared(count):
        return jax.ShapeDtypeStruct((N_CTX, 128, count), bf16)

    return pl.pallas_call(
        kernel,
        out_shape=(
            jax.ShapeDtypeStruct((rows, width), f32),
            jax.ShapeDtypeStruct((16, 128), f32),
            shared(hidden),
            shared(hidden),
            shared(hidden),
            shared(heads_width),
            shared(3 * heads_width),
        ),
        in_specs=[VMEM] * 4 + [ANY] * 5 + [VMEM] * 4 + [ANY] * 2 + [VMEM] * 3,
        out_specs=(VMEM, VMEM) + (ANY,) * 5,
        scratch_shapes=[
            pltpu.VMEM((N_CTX, rows, heads_width), bf16),
            pltpu.VMEM((N_CTX, rows, width), bf16),
            pltpu.VMEM((2, N_CTX, rows, 256), bf16),
            pltpu.VMEM(grad_gu.shape, bf16),
            pltpu.VMEM((half, 2 * columns_grad), bf16),
            pltpu.VMEM((256, seq), bf16),
            pltpu.VMEM((3, 2, 128, width), bf16),
            pltpu.VMEM((seq, HEAD), f32),
            pltpu.VMEM((seq, HEAD), f32),
            pltpu.VMEM((16, width), f32),
            pltpu.VMEM((n_shard, 16, 128), f32),
            pltpu.VMEM((n_shard - 1, 16, 128), f32),
            pltpu.VMEM((16, 128), f32),
            pltpu.VMEM((N_CTX - 1, 16, 128), f32),
            pltpu.VMEM((N_CTX - 1, 128, heads_width), bf16),
            pltpu.SemaphoreType.DMA((4,)),
            pltpu.SemaphoreType.DMA((2,)),
        ]
        + [pltpu.SemaphoreType.DMA((N_CTX - 1,))] * 4
        + [pltpu.SemaphoreType.DMA((n_shard - 1,))] * 2
        + [pltpu.SemaphoreType.DMA((N_CTX - 1,))] * 2
        + Reduce.scratch(rows, width, 1)
        + [pltpu.SemaphoreType.DMA((Both.SEMAPHORES,))] * 2
        + [pltpu.SemaphoreType.DMA]
        + Share.scratch(hidden) * 2
        + Share.scratch(width, N_CTX)
        + Share.scratch(3 * heads_width),
        compiler_params=params(3, 64 << 20),
        name="backward",
    )(own, grad_mixed, mixed, out_own, second, grad_gu, qkv, weights, first, cosines, sines, key_pos, query_pos, inputs, grad_residual, gain, second_gain_grad, logits_grad)


def local(
    tokens,
    cotangent,
    lengths,
    routes,
    block_order,
    norm_gains,
    qkv_weight,
    qkv_bias,
    out_weight,
    router,
    shared_gate,
    ffn_in,
    ffn_out,
):
    bf16, f32 = jnp.bfloat16, jnp.float32
    n_ctx = lax.axis_size("ctx")
    n_shard = lax.axis_size("shard")
    rows_dev = tokens.shape[1]
    seq_len = rows_dev * n_ctx
    n_blocks = block_order.shape[0]
    block = seq_len // n_blocks
    place = lax.axis_index("ctx")

    every = jnp.arange(seq_len, dtype=jnp.int32)
    matches = (every // block)[:, None] == jnp.arange(n_blocks, dtype=jnp.int32)[None, :]
    pos = jnp.sum(jnp.where(matches, block_order[None, :], 0), axis=1) * block + every % block
    valid = pos < lengths[0]
    valid_rows = valid.astype(f32)[:, None]

    own_valid = lax.dynamic_slice_in_dim(valid_rows, place * rows_dev, rows_dev)
    picks = routes[0][:, :, None] == jnp.arange(LANE, dtype=jnp.int32)[None, None, :]
    own_assigned = jnp.sum(picks.astype(f32), axis=1).astype(bf16)
    small = jnp.concatenate(
        [
            norm_gains,
            router.T,
            shared_gate.reshape(1, LANE),
            qkv_bias.reshape(3, LANE),
            jnp.zeros((4, LANE), bf16),
        ]
    )
    cosines, sines = rope_tables(pos)
    key_pos = jnp.where(valid, pos, 2 * seq_len)[:, None]
    (
        residual,
        second_all,
        g_all,
        attn_weights,
        out_weights,
        small_all,
        first_all,
        w_gate,
        w_up,
        w_down,
        qkv,
        mixed,
        assigned,
    ) = front(
        jnp.concatenate([tokens[0], own_assigned], axis=1),
        cotangent[0],
        own_valid,
        qkv_weight,
        out_weight,
        ffn_in,
        ffn_out,
        small,
        cosines,
        sines,
        key_pos,
        pos[None],
    )

    (
        grad_residual,
        grad_low,
        grad_mixed,
        output,
        grad_second_gain,
        grad_both,
        _,
        grad_gu,
        out_own,
    ) = feed_forward(
        second_all,
        g_all,
        assigned,
        w_gate.reshape(D, -1),
        w_up.reshape(D, -1),
        w_down.reshape(D, -1),
        out_weights.reshape(D, D),
        small_all,
        residual,
        cotangent[0],
        own_valid,
    )
    first_gain = small_all[:, 0, :].reshape(1, D).astype(f32)
    input_grad, own_small, out_share, gate_share, up_share, mixed_share, qkv_share = backward(
        grad_low,
        grad_mixed,
        mixed,
        out_own,
        second_all,
        grad_gu,
        qkv,
        attn_weights.reshape(D, -1),
        first_all,
        cosines,
        sines,
        key_pos,
        pos[None],
        tokens[0],
        grad_residual,
        first_gain,
        grad_second_gain,
        grad_both,
    )
    own_small = own_small.reshape(-1)
    grad_gains = own_small[: 2 * LANE].reshape(2, LANE)
    grad_router = own_small[2 * LANE : 8 * LANE].reshape(EXPERTS, LANE).T
    grad_shared_gate = own_small[8 * LANE : 9 * LANE]
    grad_bias_out = own_small[9 * LANE : 12 * LANE]

    grad_ffn_out, grad_ffn_in, grad_out, grad_qkv = assemble(
        out_share, gate_share, up_share, mixed_share, qkv_share
    )
    return (
        output[None],
        input_grad[None],
        grad_gains,
        grad_qkv,
        grad_bias_out,
        grad_out,
        grad_router,
        grad_shared_gate,
        grad_ffn_in,
        grad_ffn_out,
    )


def solution(mesh):
    placed = (
        P("shard", "ctx", None),
        P("shard", "ctx", None),
        P("shard"),
        P("shard", "ctx", None),
        P(),
        P(None, "shard"),
        P("shard", None),
        P("shard"),
        P("shard", None),
        P("shard", None),
        P("shard"),
        P("shard", None),
        P("shard", None),
    )
    return jax.shard_map(
        local,
        mesh=mesh,
        in_specs=placed,
        out_specs=(
            P("shard", "ctx", None),
            P("shard", "ctx", None),
            P(None, "shard"),
            P("shard", None),
            P("shard"),
            P("shard", None),
            P("shard", None),
            P("shard"),
            P("shard", None),
            P("shard", None),
        ),
        check_vma=False,
    )
```

```python
import jax
import jax.numpy as jnp
from jax import lax
from jax.experimental import pallas as pl
from jax.experimental.pallas import tpu as pltpu
from jax.sharding import PartitionSpec as P

D = 2048
HEAD = 128
HE = 1408
FS = 5632
EXPERTS = 6
FIN = 28160
FOUT = 14080
LANE = 128
SHARED_BLOCKS = FS // LANE
EXPERT_BLOCKS = HE // LANE
HIDDEN_BLOCKS = SHARED_BLOCKS + EXPERTS * EXPERT_BLOCKS

highest = lax.Precision.HIGHEST
epsilon = 1e-06
rope_base = 1000000.0


def contract_last(left, right):
    return lax.dot_general(
        left, right, (((1,), (1,)), ((), ())), preferred_element_type=jnp.float32
    )


def contract_first(left, right):
    return lax.dot_general(
        left, right, (((0,), (0,)), ((), ())), preferred_element_type=jnp.float32
    )


def dot(left, right):
    return jnp.dot(left, right, preferred_element_type=jnp.float32)


def rope_tables(positions):
    half = HEAD // 2
    lane = jnp.arange(HEAD, dtype=jnp.int32)
    freqs = rope_base ** (-(lane % half).astype(jnp.float32) * 2.0 / HEAD)
    phase = positions.astype(jnp.float32)[:, None] * freqs[None, :]
    return jnp.cos(phase), jnp.where(lane < half, -1.0, 1.0) * jnp.sin(phase)


def normalize(values):
    factor = lax.rsqrt(jnp.mean(values * values, axis=-1, keepdims=True) + epsilon)
    return (values * factor, factor)


def norm_back(grad_normed, normalized, factor, gain):
    scaled = grad_normed * gain
    return factor * (scaled - normalized * jnp.mean(scaled * normalized, axis=-1, keepdims=True))


MESH = pl.DeviceIdType.MESH
ANY = pl.BlockSpec(memory_space=pl.ANY)
VMEM = pl.BlockSpec(memory_space=pltpu.VMEM)
N_CTX = 8
CHIPS = 8
AFTER = 512


def params(number, limit=None):
    return pltpu.CompilerParams(
        collective_id=number, has_side_effects=True, vmem_limit_bytes=limit
    )


def greet(peers):
    semaphore = pltpu.get_barrier_semaphore()
    for peer in peers:
        pl.semaphore_signal(semaphore, inc=1, device_id=peer, device_id_type=MESH)
    pl.semaphore_wait(semaphore, len(peers))


def remote(source, target, sends, arrivals, slot, peer):
    return pltpu.make_async_remote_copy(
        src_ref=source,
        dst_ref=target,
        send_sem=sends.at[slot],
        recv_sem=arrivals.at[slot],
        device_id=peer,
        device_id_type=MESH,
    )


def places_of(axis):
    me = lax.axis_index(axis)
    if axis == "ctx":
        peer = lambda place: {"ctx": place}
    else:
        core, me = lax.rem(me, 2), me // 2
        peer = lambda place: {"shard": 2 * place + core}
    other = me + 1 - 2 * lax.rem(me, 2)
    places = [[lax.rem(base + 2 * k, N_CTX) for k in (0, 1, 3, 2)] for base in (me, other)]
    return places, peer


def by_rows(rows, body):
    step = 16

    def run(i, carry):
        body(pl.ds(pl.multiple_of(i * step, step), step))
        return carry

    lax.fori_loop(0, rows // step, run, 0)


class Gather:
    SEMAPHORES = 9
    PAIRED = 9 + CHIPS

    def __init__(self, own, out, sends, arrivals, axis="ctx", columns=None, offset=0):
        self.block, self.out, self.sends, self.arrivals = own, out, sends, arrivals
        self.columns, self.offset = columns, offset
        self.places, self.peer = places_of(axis)
        (self.me, self.up, self.down, self.far), other = self.places
        self.other = other[0]
        self.half = out.shape[-2] // 2
        self.paired = axis == "shard"
        if self.paired:
            shard = lax.axis_index("shard")
            self.core = lax.rem(shard, 2)
            self.mate = {"shard": shard + 1 - 2 * self.core}
        self.started = []

    def at(self, place, *half):
        if self.paired:
            return self.out.at[(place, self.core) + half]
        if self.columns is None:
            return self.out.at[(place,) + half]
        rows = half[0] if half else pl.ds(0, self.out.shape[1])
        return self.out.at[place, rows, pl.ds(*self.columns)]

    def own(self):
        if self.columns is None:
            return self.block
        return self.block.at[:, pl.ds(*self.columns)]

    def _send(self, slot, source, target, peer):
        def copy():
            return remote(
                source(), target(), self.sends, self.arrivals, slot + self.offset, peer()
            )

        copy().start()
        self.started.append(copy)

    def _await(self, slot, ref):
        peer = self.peer(self.other)
        remote(ref, ref, self.sends, self.arrivals, slot + self.offset, peer).wait_recv()

    def _hand(self, number, place, source=None):
        if self.paired:
            block = lambda: self.at(place)
            self._send(9 + number, source or block, block, lambda: self.mate)

    def _begin(self, slot, place):
        self._send(slot, self.own, lambda: self.at(self.me), lambda: self.peer(place))

    def begin_other(self):
        self._begin(0, self.other)
        self._hand(0, self.me, self.own)

    def begin_ring(self):
        self._begin(1, self.up)
        self._begin(2, self.down)

    def begin(self):
        self.begin_other()
        self.begin_ring()

    def pass_other(self):
        block = lambda: self.at(self.other)
        self._await(0, block())
        self._send(3, block, block, lambda: self.peer(self.up))
        self._send(4, block, block, lambda: self.peer(self.down))
        self._hand(1, self.other)

    def pass_ring(self, column):
        _, up, down, _ = self.places[column]
        first = 1 + 2 * column
        low, high = pl.ds(0, self.half), pl.ds(self.half, self.half)
        self._await(first, self.at(down))
        lower = lambda: self.at(down, low)
        self._send(5 + 2 * column, lower, lower, lambda: self.peer(self.up))
        self._await(first + 1, self.at(up))
        upper = lambda: self.at(up, high)
        self._send(6 + 2 * column, upper, upper, lambda: self.peer(self.down))
        self._hand(2 + 2 * column, down)
        self._hand(3 + 2 * column, up)

    def end(self):
        low, high = pl.ds(0, self.half), pl.ds(self.half, self.half)
        for column in range(2):
            far = self.places[column][3]
            self._await(5 + 2 * column, self.at(far, low))
            self._await(6 + 2 * column, self.at(far, high))
            self._hand(6 + column, far)
        if self.paired:
            (me, up, down, far), (other, other_up, other_down, other_far) = self.places
            for number, place in enumerate(
                (me, other, down, up, other_down, other_up, far, other_far)
            ):
                self._await(9 + number, self.out.at[place, 1 - self.core])
        for copy in self.started:
            copy().wait_send()


class RingFirst(Gather):
    def _across(self, slot, block):
        self._send(slot, block, block, lambda: self.peer(self.other))

    def pass_other(self):
        pass

    def pass_ring(self, column):
        _, up, down, far = self.places[0]
        low, high = pl.ds(0, self.half), pl.ds(self.half, self.half)
        if column:
            for slot, half in ((5, low), (6, high)):
                self._await(slot, self.at(far, half))
                self._across(slot + 2, lambda half=half: self.at(far, half))
            return
        for slot, place, half, toward in ((1, down, low, self.up), (2, up, high, self.down)):
            self._await(slot, self.at(place))
            self._on(slot + 4, place, half, toward)
            self._across(slot + 2, lambda place=place: self.at(place))

    def _on(self, slot, place, half, toward):
        block = lambda: self.at(place, half)
        self._send(slot, block, block, lambda: self.peer(toward))

    def end(self):
        low, high = pl.ds(0, self.half), pl.ds(self.half, self.half)
        other, up, down, far = self.places[1]
        for slot, block in (
            (0, self.at(other)),
            (3, self.at(down)),
            (4, self.at(up)),
            (7, self.at(far, low)),
            (8, self.at(far, high)),
        ):
            self._await(slot, block)
        for copy in self.started:
            copy().wait_send()


class Both:
    SEMAPHORES = 2 * Gather.SEMAPHORES

    def __init__(self, own, out, sends, arrivals, after):
        width = out.shape[-1]
        first = Gather(own, out, sends, arrivals, columns=(0, width - after))
        last = RingFirst(
            own, out, sends, arrivals, columns=(width - after, after), offset=Gather.SEMAPHORES
        )
        self.parts, self.out = (first, last), out
        self.me, self.up, self.down, self.other = first.me, first.up, first.down, first.other

    def begin(self):
        for part in self.parts:
            part.begin()

    def pass_other(self):
        for part in self.parts:
            part.pass_other()

    def pass_ring(self, column):
        for part in self.parts:
            part.pass_ring(column)

    def end(self):
        for part in self.parts:
            part.end()


class Reduce:
    SEMAPHORES = 13

    @staticmethod
    def scratch(rows, width, across=2):
        return [
            pltpu.VMEM((4, rows // 2, width), jnp.bfloat16),
            pltpu.VMEM((4, rows, width), jnp.bfloat16),
            pltpu.VMEM((across, rows, width), jnp.bfloat16),
            pltpu.SemaphoreType.DMA((Reduce.SEMAPHORES,)),
            pltpu.SemaphoreType.DMA((Reduce.SEMAPHORES,)),
        ]

    def __init__(self, parts, held, passing, near, across, sends, arrivals, axis="ctx"):
        self.parts, self.held = parts, held
        self.passing, self.near, self.across = passing, near, across
        self.sends, self.arrivals = sends, arrivals
        self.places, self.peer = places_of(axis)
        _, self.up, self.down, _ = self.places[0]
        self.other = self.places[1][0]
        self.rows, self.width = near.shape[1], near.shape[2]
        self.half = self.rows // 2
        self.started = []

    def _send(self, slot, source, target, place):
        def copy():
            return remote(source(), target(), self.sends, self.arrivals, slot, self.peer(place))

        copy().start()
        self.started.append(copy)

    def _await(self, slot, ref):
        remote(ref, ref, self.sends, self.arrivals, slot, self.peer(self.other)).wait_recv()

    def begin(self):
        self.send_far()
        self.send_near(0)
        self.send_near(1)

    def send_far(self):
        for column in (1, 0):
            self._send_far(column)

    def _send_far(self, column):
        low, high = pl.ds(0, self.half), pl.ds(self.half, self.half)
        far = self.places[column][3]
        slot, a, b = 6 * column, 2 * column, 2 * column + 1
        parts, passing = self.parts, self.passing
        self._send(slot, lambda: parts.at[far, low], lambda: passing.at[a], self.up)
        self._send(slot + 1, lambda: parts.at[far, high], lambda: passing.at[b], self.down)

    def send_near(self, side):
        for column in (1, 0):
            self._send_near(column, side)

    def _send_near(self, column, side):
        half = pl.ds((1 - side) * self.half, self.half)
        toward, place = self.places[column][1 + side], (self.up, self.down)[side]
        index, parts, near = 2 * column + side, self.parts, self.near
        self._send(
            6 * column + 2 + side,
            lambda: parts.at[toward, half],
            lambda: near.at[index, half],
            place,
        )

    def pass_side(self, side):
        for column in (1, 0):
            self._pass_side(column, side)

    def _loop(self, rows, body):
        step = 16

        def run(i, carry):
            body(pl.multiple_of(i * step, step), step)
            return carry

        lax.fori_loop(0, rows // step, run, 0)

    def pass_on(self, column):
        self._pass_side(column, 0)
        self._pass_side(column, 1)

    def _pass_side(self, column, side):
        slot, index, start = 6 * column, 2 * column + side, side * self.half
        toward, place = self.places[column][1 + side], (self.up, self.down)[side]
        passing, near, held = self.passing, self.near, self.held
        self._await(slot + side, passing.at[index])

        def add(row, step):
            there = pl.ds(row, step)
            total = passing[index, there, :].astype(jnp.float32)
            total = total + held[toward, pl.ds(start + row, step), :].astype(jnp.float32)
            passing[index, there, :] = total.astype(jnp.bfloat16)

        self._loop(self.half, add)
        target = pl.ds(start, self.half)
        self._send(
            slot + 4 + side, lambda: passing.at[index], lambda: near.at[index, target], place
        )

    def _near(self, column):
        low, high = pl.ds(0, self.half), pl.ds(self.half, self.half)
        slot = 6 * column
        self._await(slot + 2, self.near.at[2 * column, high])
        self._await(slot + 3, self.near.at[2 * column + 1, low])
        self._await(slot + 4, self.near.at[2 * column, low])
        self._await(slot + 5, self.near.at[2 * column + 1, high])

    def _sum(self, column, there):
        place = self.places[column][0]
        total = self.held[place, there, :].astype(jnp.float32)
        total = total + self.near[2 * column, there, :].astype(jnp.float32)
        return total + self.near[2 * column + 1, there, :].astype(jnp.float32)

    def cross(self):
        self._near(1)
        place, held, across = self.places[1][0], self.held, self.across
        if across.shape[0] == 1:
            kept = lambda: held.at[place]
        else:
            kept = lambda: across.at[1]

        def add(row, step):
            there = pl.ds(row, step)
            kept()[there, :] = self._sum(1, there).astype(jnp.bfloat16)

        self._loop(self.rows, add)
        self._send(12, kept, lambda: across.at[0], self.other)

    def ready(self):
        self._near(0)
        self._await(12, self.across.at[0])

    def total(self, there):
        return self._sum(0, there) + self.across[0, there, :].astype(jnp.float32)

    def end(self):
        for copy in self.started:
            copy().wait_send()


class Spread:
    SEMAPHORES = 7 + 8

    def __init__(self, own, out, sends, arrivals):
        self.own, self.out, self.sends, self.arrivals = own, out, sends, arrivals
        self.me = lax.axis_index("shard")
        self.core, self.chip = lax.rem(self.me, 2), self.me // 2
        self.mate = {"shard": self.me + 1 - 2 * self.core}
        self.started = []

    def _send(self, slot, source, target, peer):
        copy = remote(source, target, self.sends, self.arrivals, slot, peer)
        copy.start()
        self.started.append(copy)

    def _await(self, slot, ref):
        remote(ref, ref, self.sends, self.arrivals, slot, self.mate).wait_recv()

    def _from(self, k, core):
        return self.out.at[2 * lax.rem(self.chip + CHIPS - k, CHIPS) + core]

    def peers(self):
        return [self.mate] + [
            {"shard": 2 * lax.rem(self.chip + k, CHIPS) + self.core} for k in range(1, CHIPS)
        ]

    def begin(self):
        target = self.out.at[self.me]
        for k in range(1, CHIPS):
            peer = {"shard": 2 * lax.rem(self.chip + k, CHIPS) + self.core}
            self._send(k - 1, self.own, target, peer)
        self._send(7, self.own, target, self.mate)

    def hand_on(self):
        for k in range(1, CHIPS):
            block = self._from(k, self.core)
            self._await(k - 1, block)
            self._send(7 + k, block, block, self.mate)

    def end(self):
        for k in range(CHIPS):
            self._await(7 + k, self._from(k, 1 - self.core))
        for copy in self.started:
            copy.wait_send()


def pick_copies(ffn_in, ffn_out, picked, sems):
    count = -(-HIDDEN_BLOCKS // N_CTX)
    place = lax.axis_index("ctx")
    copies = []
    for j in range(count):
        block = place * count + j
        block = block - (block // HIDDEN_BLOCKS) * (block - HIDDEN_BLOCKS + 1)
        routed = (block // SHARED_BLOCKS + 1) // 2
        rest = block - SHARED_BLOCKS
        expert = (rest + SHARED_BLOCKS * (1 - routed)) // EXPERT_BLOCKS * routed
        gate = block * (1 - routed) + (2 * SHARED_BLOCKS + EXPERT_BLOCKS * expert + rest) * routed
        up = gate + SHARED_BLOCKS * (1 - routed) + EXPERT_BLOCKS * routed
        for k, (source, at) in enumerate(((ffn_in, gate), (ffn_in, up), (ffn_out, block))):
            copies.append(
                pltpu.make_async_copy(
                    source.at[:, pl.ds(pl.multiple_of(at * LANE, LANE), LANE)],
                    picked.at[:, LANE * (count * k + j) : LANE * (count * k + j + 1)],
                    sems.at[3 * j + k],
                )
            )
    return copies


def assemble(out_share, gate_share, up_share, mixed_share, qkv_share):
    rows, hidden = out_share.shape[1:]
    width = mixed_share.shape[2]
    count = hidden // LANE
    spans = [(0, SHARED_BLOCKS)] + [
        (SHARED_BLOCKS + EXPERT_BLOCKS * e, EXPERT_BLOCKS) for e in range(EXPERTS)
    ]

    def moves(place, kind):
        result = []
        for index, (first, size) in enumerate(spans):
            low, high = max(first, count * place), min(first + size, count * (place + 1))
            if low >= high:
                continue
            there = low if kind == 0 else first + low + (kind - 1) * size
            result.append(((low - count * place) * LANE, there * LANE, (high - low) * LANE))
        return result

    jobs = []
    for place in range(N_CTX):
        for kind in range(3):
            jobs.append((kind, place, hidden, min(kind, 1), moves(place, kind)))
        jobs.append((3, place, width, 2, [(0, width * place, width)]))
        jobs.append(
            (4, place, 3 * width, 3, [(width * i, D * i + width * place, width) for i in range(3)])
        )
    depth = 6
    most = max(len(job[4]) for job in jobs)

    def kernel(*refs):
        shares, outs = refs[0:5], refs[5:9]
        low, full, loads, stores = refs[9:]

        def load(n):
            kind, place, size, _, _ = jobs[n]
            return pltpu.make_async_copy(
                shares[kind].at[place], low.at[n % depth, :, 0:size], loads.at[n % depth]
            )

        def store(n):
            _, _, _, to, spans_of = jobs[n]
            return [
                pltpu.make_async_copy(
                    full.at[n % depth, :, start : start + size],
                    outs[to].at[:, there : there + size],
                    stores.at[n % depth, k],
                )
                for k, (start, there, size) in enumerate(spans_of)
            ]

        for n in range(depth - 1):
            load(n).start()
        for n in range(len(jobs)):
            if n + depth - 1 < len(jobs):
                load(n + depth - 1).start()
            load(n).wait()
            if n >= depth:
                for copy in store(n - depth):
                    copy.wait()
            slot, size = n % depth, jobs[n][2]

            def widen(there, slot=slot, size=size):
                full[slot, there, 0:size] = low[slot, there, 0:size].astype(jnp.float32)

            by_rows(rows, widen)
            for copy in store(n):
                copy.start()
        for n in range(len(jobs) - depth, len(jobs)):
            for copy in store(n):
                copy.wait()

    f32 = jnp.float32
    return pl.pallas_call(
        kernel,
        out_shape=(
            jax.ShapeDtypeStruct((rows, FOUT), f32),
            jax.ShapeDtypeStruct((rows, FIN), f32),
            jax.ShapeDtypeStruct((rows, D), f32),
            jax.ShapeDtypeStruct((rows, 3 * D), f32),
        ),
        in_specs=[ANY] * 5,
        out_specs=(ANY,) * 4,
        scratch_shapes=[
            pltpu.VMEM((depth, rows, hidden), jnp.bfloat16),
            pltpu.VMEM((depth, rows, hidden), f32),
            pltpu.SemaphoreType.DMA((depth,)),
            pltpu.SemaphoreType.DMA((depth, most)),
        ],
        compiler_params=pltpu.CompilerParams(vmem_limit_bytes=60 << 20),
        name="assemble",
    )(out_share, gate_share, up_share, mixed_share, qkv_share)


def front(block, grad_out, own_valid, qkv_weight, out_weight, ffn_in, ffn_out, small, cosines, sines, key_pos, query_pos):
    rows, width = qkv_weight.shape[0], out_weight.shape[1]
    n_shard = width // rows
    heads_width = width // N_CTX
    heads = heads_width // HEAD
    seq = rows * N_CTX
    extra = block.shape[1] - width
    tile = 256
    scale = HEAD ** (-0.5)
    hidden = -(-HIDDEN_BLOCKS // N_CTX) * LANE
    f32, bf16 = jnp.float32, jnp.bfloat16

    def kernel(
        block, grad_out, own_valid, qkv_weight, out_weight, ffn_in, ffn_out, small, cosines, sines,
        key_pos, query_pos,
        residual, second_all, g_all, weights_out, out_out, small_all, first_out, w_gate, w_up, w_down,
        qkv, mixed_own, assigned,
        own_grad, x_all, weights, out_all, first, staged, picked, params_all, mixed, own, loads, picks, local,
        mixed_sends, mixed_arrivals, *scratch,
    ):
        gather = Gather(block, x_all, *scratch[0:2])
        gather_qkv = Gather(staged, weights, *scratch[2:4], axis="shard")
        spread_small = Spread(small, small_all, *scratch[4:6])
        gather_grad = Both(own_grad, g_all, *scratch[6:8], 768)
        gather_second = Both(own, second_all, *scratch[8:10], 768)
        w_outs = (w_gate, w_up, w_down)
        ffn = [
            Gather(
                picked.at[:, pl.ds(hidden * k, hidden)], out, *scratch[10 + 2 * k : 12 + 2 * k], axis="shard"
            )
            for k, out in enumerate(w_outs)
        ]
        gather_out = Gather(out_weight, out_all, *scratch[16:18], axis="shard")
        me = gather.me
        loaded = [
            pltpu.make_async_copy(
                source.at[:, pl.ds(pl.multiple_of(start + heads_width * me, heads_width), heads_width)],
                staged.at[:, heads_width * i : heads_width * (i + 1)],
                loads.at[i],
            )
            for i, (source, start) in enumerate(
                ((qkv_weight, 0), (qkv_weight, width), (qkv_weight, 2 * width))
            )
        ]
        for copy in loaded:
            copy.start()
        picking = pick_copies(ffn_in, ffn_out, picked, picks)
        for copy in picking:
            copy.start()
        places = [lax.rem(me + k, N_CTX) for k in range(1, N_CTX)]
        greet([{"ctx": p} for p in places] + spread_small.peers())
        gather.begin()
        spread_small.begin()
        for copy in loaded:
            copy.wait()
        gather_qkv.begin()
        gather_out.begin()
        own_grad[...] = (grad_out[...].astype(f32) * own_valid[...]).astype(bf16)
        for copy in picking:
            copy.wait()
        kept = [
            pltpu.make_async_copy(source, target, local.at[k])
            for k, (source, target) in enumerate(
                (
                    (block, x_all.at[me]),
                    (staged, weights.at[spread_small.chip, spread_small.core]),
                    (small, small_all.at[spread_small.me]),
                    (out_weight, gather_out.at(gather_out.me)),
                    (own_grad, g_all.at[me]),
                )
            )
        ] + [
            pltpu.make_async_copy(gather_w.block, gather_w.at(gather_w.me), local.at[5 + k])
            for k, gather_w in enumerate(ffn)
        ]
        for copy in kept:
            copy.start()
        gather.pass_other()
        gather_qkv.pass_other()
        gather_qkv.pass_ring(0)
        spread_small.hand_on()
        gather.pass_ring(0)
        gather_qkv.pass_ring(1)
        gather_out.pass_other()
        gather.pass_ring(1)
        gather_out.pass_ring(0)
        spread_small.end()
        gather_qkv.end()
        gather.end()
        gather_grad.begin()
        ffn[0].begin()
        for copy in kept:
            copy.wait()
        weights_kept = pltpu.make_async_copy(weights, weights_out, local.at[0])
        weights_kept.start()
        assigned[...] = x_all[:, :, width:].reshape(seq, extra)
        params_all[...] = small_all[...].astype(f32)
        gains = [
            jnp.concatenate([params_all[s, k : k + 1, :] for s in range(n_shard)], axis=1)
            for k in range(2)
        ]
        per = heads_width // 128

        def bias_of(i):
            parts_of = []
            for j in range(per):
                at = n_shard * i + per * me + j
                parts_of.append(params_all[at // 3, pl.ds(3 + EXPERTS + lax.rem(at, 3), 1), :])
            return jnp.concatenate(parts_of, axis=1)

        biases = [bias_of(i) for i in range(3)]

        def project(n, carry):
            there = pl.ds(pl.multiple_of(n * tile, tile), tile)

            def norm(k, inner):
                inner_rows = pl.ds(pl.multiple_of(lax.rem(k, rows // 16) * 16, 16), 16)
                at = 2 * n + k // (rows // 16)
                normed, _ = normalize(x_all[at, inner_rows, 0:width].astype(f32))
                first[at, inner_rows, :] = (normed * gains[0]).astype(bf16)
                return inner

            lax.fori_loop(0, tile // 16, norm, 0)
            left = first[pl.ds(2 * n, 2)].reshape(tile, width)
            for i in range(3):
                columns = slice(heads_width * i, heads_width * (i + 1))
                made = biases[i] + jnp.dot(
                    left,
                    weights[:, :, :, columns].reshape(width, heads_width),
                    preferred_element_type=f32,
                )
                if i == 2:
                    qkv[there, columns] = made.astype(bf16)
                    continue
                for h in range(heads):
                    part = made[:, HEAD * h : HEAD * (h + 1)]
                    turned = part * cosines[there, :] + pltpu.roll(part, HEAD // 2, 1) * sines[there, :]
                    start = heads_width * i + HEAD * h
                    qkv[there, start : start + HEAD] = turned.astype(bf16)

            @pl.when(n == 0)
            def _():
                gather_out.pass_ring(1)

            @pl.when(n == 1)
            def _():
                ffn[0].pass_other()

            @pl.when(n == 2)
            def _():
                gather_grad.pass_other()

            return carry

        lax.fori_loop(0, seq // tile, project, 0)
        first_kept = pltpu.make_async_copy(first, first_out, local.at[1])
        first_kept.start()
        events = {
            0: [lambda: gather_grad.pass_ring(0)],
            1: [lambda: ffn[0].pass_ring(0)],
            2: [lambda: ffn[0].pass_ring(1), ffn[1].begin],
            3: [lambda: gather_grad.pass_ring(1)],
            4: [gather_out.end],
            6: [ffn[1].pass_other],
        }

        def attend(n, carry):
            head, i = n // (seq // tile), lax.rem(n, seq // tile)
            there = pl.ds(pl.multiple_of(i * tile, tile), tile)

            def lanes_of(start):
                return pl.ds(pl.multiple_of(start + HEAD * head, HEAD), HEAD)

            scores = scale * contract_last(qkv[:, lanes_of(heads_width)], qkv[there, lanes_of(0)])
            scores = jnp.where(key_pos[...] <= query_pos[:, there], scores, -1e30)
            raised = jnp.exp(scores - jnp.max(scores, axis=0, keepdims=True))
            probs = (raised * (1.0 / jnp.sum(raised, axis=0, keepdims=True))).astype(bf16)
            mixed[there, lanes_of(0)] = contract_first(
                probs, qkv[:, lanes_of(2 * heads_width)]
            ).astype(bf16)
            for at, todo in events.items():

                @pl.when(n == at)
                def _(todo=todo):
                    for event in todo:
                        event()

            return carry

        lax.fori_loop(0, heads * (seq // tile), attend, 0)

        def columns_of(place):
            return pl.ds(pl.multiple_of(heads_width * place, heads_width), heads_width)

        def rows_of(place):
            return pl.ds(pl.multiple_of(rows * place, rows), rows)

        to_rows = [
            remote(
                mixed.at[rows_of(p), :],
                mixed_own.at[:, columns_of(me)],
                mixed_sends,
                mixed_arrivals,
                k,
                {"ctx": p},
            )
            for k, p in enumerate(places)
        ]

        for copy in to_rows:
            copy.start()
        mixed_own[:, columns_of(me)] = mixed[rows_of(me), :]
        out_kept = pltpu.make_async_copy(out_all, out_out, local.at[3])
        out_kept.start()
        ffn[1].pass_ring(0)
        for k, p in enumerate(places):
            ref = mixed_own.at[:, columns_of(lax.rem(me + N_CTX - 1 - k, N_CTX))]
            remote(ref, ref, mixed_sends, mixed_arrivals, k, {"ctx": p}).wait_recv()
        for t in range(width // 512):
            right = out_all[2 * t : 2 * (t + 1)].reshape(512, width)
            residual[:, 512 * t : 512 * (t + 1)] = contract_last(mixed_own[...], right)

        def norm_second(there):
            total = x_all[me, there, 0:width].astype(f32) + residual[there, :]
            residual[there, :] = total
            normed, _ = normalize(total)
            own[there, :] = (normed * gains[1]).astype(bf16)

        by_rows(rows, norm_second)
        gather_second.begin()
        second_kept = pltpu.make_async_copy(own, second_all.at[me], local.at[2])
        second_kept.start()
        ffn[2].begin()
        gather_second.pass_other()
        ffn[1].pass_ring(1)
        ffn[0].end()
        gather_second.pass_ring(0)
        ffn[2].pass_other()
        gather_second.pass_ring(1)
        ffn[2].pass_ring(0)
        ffn[1].end()
        ffn[2].pass_ring(1)
        gather_grad.end()
        for copy in to_rows:
            copy.wait_send()
        for copy in (weights_kept, first_kept, second_kept, out_kept):
            copy.wait()
        gather_second.end()
        ffn[2].end()

    def shape(*dims, kind=bf16):
        return jax.ShapeDtypeStruct(dims, kind)

    pair = [pltpu.SemaphoreType.DMA((Both.SEMAPHORES,))] * 2
    paired = [pltpu.SemaphoreType.DMA((Gather.PAIRED,))] * 2
    return pl.pallas_call(
        kernel,
        out_shape=(
            shape(rows, width, kind=f32),
            shape(N_CTX, rows, width),
            shape(N_CTX, rows, width),
            shape(CHIPS, 2, rows, 3 * heads_width),
            shape(CHIPS, 2, rows, width),
            shape(n_shard, 16, 128),
            shape(N_CTX, rows, width),
            shape(CHIPS, 2, rows, hidden),
            shape(CHIPS, 2, rows, hidden),
            shape(CHIPS, 2, rows, hidden),
            shape(seq, 3 * heads_width),
            shape(rows, width),
            shape(seq, extra),
        ),
        in_specs=[ANY, VMEM, VMEM] + [ANY] * 5 + [VMEM] * 4,
        out_specs=(VMEM, ANY, ANY, ANY, ANY, VMEM, ANY, ANY, ANY, ANY, VMEM, VMEM, VMEM),
        scratch_shapes=[
            pltpu.VMEM((rows, width), bf16),
            pltpu.VMEM((N_CTX,) + block.shape, bf16),
            pltpu.VMEM((CHIPS, 2, rows, 3 * heads_width), bf16),
            pltpu.VMEM((CHIPS, 2, rows, width), bf16),
            pltpu.VMEM((N_CTX, rows, width), bf16),
            pltpu.VMEM((rows, 3 * heads_width), bf16),
            pltpu.VMEM((rows, 3 * hidden), bf16),
            pltpu.VMEM((n_shard, 16, 128), f32),
            pltpu.VMEM((seq, heads_width), bf16),
            pltpu.VMEM((rows, width), bf16),
            pltpu.SemaphoreType.DMA((3,)),
            pltpu.SemaphoreType.DMA((3 * hidden // LANE,)),
            pltpu.SemaphoreType.DMA((8,)),
            pltpu.SemaphoreType.DMA((N_CTX - 1,)),
            pltpu.SemaphoreType.DMA((N_CTX - 1,)),
        ]
        + pair
        + paired
        + [pltpu.SemaphoreType.DMA((Spread.SEMAPHORES,))] * 2
        + pair * 2
        + paired * 4,
        compiler_params=params(0, 56 << 20),
        name="front",
    )(block, grad_out, own_valid, qkv_weight, out_weight, ffn_in, ffn_out, small, cosines, sines, key_pos, query_pos)


class Exchange:
    @staticmethod
    def scratch():
        return [pltpu.SemaphoreType.DMA((CHIPS,)), pltpu.SemaphoreType.DMA((CHIPS,))]

    def __init__(self, parts, staged, sends, arrivals):
        self.parts, self.staged = parts, staged
        self.sems = (sends, arrivals)
        self.width = parts.shape[2]
        me = lax.axis_index("shard")
        self.core, self.chip = lax.rem(me, 2), me // 2
        self.mate = {"shard": me + 1 - 2 * self.core}

    def chip_at(self, step):
        base = self.chip + (1 - lax.rem(step, 2)) * (1 - 2 * lax.rem(self.chip, 2))
        b = step // 2
        ahead = 2 - b + 3 * (b // 2) - 2 * (b // 3)
        return 2 * lax.rem(base // 2 + ahead, 4) + lax.rem(base, 2)

    def stage(self, slot, core):
        if len(self.staged.shape) == 2:
            return self.staged.at[pl.ds(pl.multiple_of((2 * slot + core) * 128, 128), 128), :]
        return self.staged.at[slot, core]

    def columns_at(self, step):
        return pl.ds(pl.multiple_of(self.chip_at(step) * 256, 256), 256)

    def _pair(self, step):
        return remote(
            self.stage(lax.rem(step, 3), 1 - self.core).at[:, pl.ds(0, self.width)],
            self.parts.at[self.chip_at(step)],
            *self.sems,
            step,
            self.mate,
        )

    def finish(self, step):
        chip, slot, width = self.chip_at(step), lax.rem(step, 3), self.width
        ref = self.parts.at[chip]
        remote(ref, ref, *self.sems, step, self.mate).wait_recv()

        def add(there):
            total = self.parts[chip, there, :].astype(jnp.float32)
            total = total + self.stage(slot, self.core)[there, 0:width].astype(jnp.float32)
            self.parts[chip, there, :] = total.astype(jnp.bfloat16)

        by_rows(128, add)

    def run(self, left, right, turned, between):
        width = self.width
        tile = 896 if width % 896 == 0 else min(width, 1024)

        def step_of(step, carry):
            @pl.when(step >= 3)
            def _():
                self._pair(step - 3).wait_send()

            slot = lax.rem(step, 3)
            rows = left(step)
            depth = rows.shape[0]
            turned[:, 0:depth] = rows.T
            for start in range(0, width, tile):
                made = jnp.dot(
                    turned[:, 0:depth], right(start, tile), preferred_element_type=jnp.float32
                ).astype(jnp.bfloat16)
                self.stage(slot, 0)[:, start : start + tile] = made[:128]
                self.stage(slot, 1)[:, start : start + tile] = made[128:]
            self._pair(step).start()

            @pl.when(step >= 2)
            def _():
                self.finish(step - 2)

            for at, events in between.items():

                @pl.when(step == at)
                def _(events=events):
                    for event in events:
                        event()

            return carry

        lax.fori_loop(0, CHIPS, step_of, 0)
        self.finish(CHIPS - 2)
        self.finish(CHIPS - 1)
        for step in range(CHIPS - 3, CHIPS):
            self._pair(step).wait_send()


def feed_forward(second, grad_out, assigned, w_gate, w_up, w_down, out_weights, small, residual, own_grad, own_valid):
    _, rows, width = second.shape
    seq = rows * N_CTX
    hidden = w_gate.shape[1]
    lanes = 128
    n_shard = small.shape[0]
    pair = 2 * rows
    tile = 896
    f32, bf16 = jnp.float32, jnp.bfloat16

    def kernel(
        second, grad_out, assigned, w_gate, w_up, w_down, out_weights, small, residual, own_grad, own_valid,
        grad_residual, grad_low, grad_mixed, output, grad_gain, grad_logits, act_out, grad_gu_out,
        out_owned,
        second_held, grad_held, in_held, down_held, act, grad_gu, weights, dots, dots_in, gain_sum,
        logit_low,
        back_parts, ffn_parts, dot_sends, dot_arrivals, loads, row_loads, weight_loads, stores, *scratch,
    ):
        back = Reduce(back_parts, back_parts, *scratch[:5])
        ahead = Reduce(ffn_parts, ffn_parts, *scratch[5:10])
        share, act_held = down_held.at[pl.ds(0, CHIPS)], down_held.at[pl.ds(CHIPS, N_CTX)]
        staged = in_held.at[pl.ds(0, 768), pl.ds(0, hidden)]
        turned = in_held.at[pl.ds(768, 256), pl.ds(0, seq)]
        exchange = Exchange(share, staged, *scratch[10:12])
        sums = Reduce(share, share, *scratch[12:17], axis="shard")
        free = scratch[17]
        own, other = back.places
        me = own[0]
        peers = [lax.rem(me + k, N_CTX) for k in range(1, N_CTX)]

        def start_of(b):
            ahead = 2 - b + 3 * (b // 2) - 2 * (b // 3)
            return pl.multiple_of(lax.rem(me // 2 + ahead, N_CTX // 2) * pair, pair)

        def row_copies(b):
            there = pl.ds(start_of(b) // rows, 2)
            return [
                pltpu.make_async_copy(source.at[there], target.at[there], row_loads.at[2 * b + k])
                for k, (source, target) in enumerate(((second, second_held), (grad_out, grad_held)))
            ]

        def start_rows(b, carry):
            for copy in row_copies(b):
                copy.start()
            return carry

        def weight_copies(t):
            copies = []
            for k, (source, target, here) in enumerate(
                ((w_gate, in_held, 0), (w_up, in_held, hidden), (w_down, down_held, 0))
            ):
                every = (slice(None),) * (len(target.shape) - 1)
                source = source.at[every + (pl.ds(pl.multiple_of(tile * t, tile), tile),)]
                target = target.at[every + (pl.ds(pl.multiple_of(here + tile * t, tile), tile),)]
                copies.append(pltpu.make_async_copy(source, target, weight_loads.at[3 * t + k]))
            return copies

        def start_weights(t, carry):
            for copy in weight_copies(t):
                copy.start()
            return carry

        start_rows(0, 0)
        start_weights(0, 0)
        lax.fori_loop(1, N_CTX // 2, start_rows, 0)
        lax.fori_loop(1, hidden // tile, start_weights, 0)
        plane_peers = [sums.peer(p) for p in (sums.up, sums.down, sums.other)]
        greet([{"ctx": p} for p in peers] + plane_peers + [exchange.mate])
        logit_low[...] = jnp.zeros_like(logit_low)
        gains = []
        for s in range(n_shard):
            held = small[s].astype(f32)
            gains.append(held[1:2])
            part = jnp.concatenate([held[2 : 3 + EXPERTS], jnp.zeros((15 - EXPERTS, 128), f32)], axis=0)
            logit_low[0:16, 128 * s : 128 * (s + 1)] = part.astype(bf16)
        gain = jnp.concatenate(gains, axis=1)
        def stored(slot, start):
            there = pl.ds(start, pair)
            return [
                pltpu.make_async_copy(
                    act.at[slot, pl.ds(rows * k, rows)], act_out.at[start // rows + k], stores.at[slot, 1 + k]
                )
                for k in range(2)
            ] + [
                pltpu.make_async_copy(grad_gu.at[slot], grad_gu_out.at[there, :], stores.at[slot, 0]),
            ]

        def dot_copy(slot, place):
            return remote(
                dots.at[place], dots_in.at[slot], dot_sends, dot_arrivals, slot, {"ctx": place}
            )

        def branch_of(j):
            at = me * (hidden // LANE) + j
            routed = (at // SHARED_BLOCKS + 1) // 2
            expert = (at - SHARED_BLOCKS) // EXPERT_BLOCKS
            return (1 - routed) * EXPERTS + routed * expert + 100 * (at // HIDDEN_BLOCKS)

        def block(b, carry):
            start = start_of(b)
            slot = 0
            first = pl.multiple_of(start // rows, 2)
            for copy in row_copies(b):
                copy.wait()

            @pl.when(b >= 1)
            def _():
                for copy in stored(slot, start_of(b - 1)):
                    copy.wait()

            def rows_of(ref):
                return ref[pl.ds(first, 2)].reshape(pair, width)

            logits = contract_last(rows_of(second_held), logit_low[...])
            lane = lax.broadcasted_iota(jnp.int32, logits.shape, 1)
            named = assigned[pl.ds(start, pair), :] > 0
            raised = jnp.where(named, logits, -1e30)
            raised = jnp.exp(raised - jnp.max(raised, axis=-1, keepdims=True))
            raised = jnp.where(named, raised, 0.0)
            gates = raised / jnp.sum(raised, axis=-1, keepdims=True)
            gates = jnp.where(lane == EXPERTS, jax.nn.sigmoid(logits), gates)
            weights[pl.ds(start, pair), :] = gates
            dots[pl.ds(first, 2)] = jnp.zeros((2, rows, lanes), f32)

            def hidden_tile(t, carry):
                @pl.when(b == 0)
                def _():
                    for copy in weight_copies(t):
                        copy.wait()

                low = pl.ds(pl.multiple_of(tile * t, tile), tile)
                high = pl.ds(pl.multiple_of(hidden + tile * t, tile), tile)
                rows_in = rows_of(second_held)
                gate = jnp.dot(rows_in, in_held[:, low], preferred_element_type=f32)
                upward = jnp.dot(rows_in, in_held[:, high], preferred_element_type=f32)
                raw = jnp.dot(
                    rows_of(grad_held),
                    down_held[:, :, low].reshape(width, tile),
                    preferred_element_type=f32,
                )
                gates = weights[pl.ds(start, pair), :]
                lane = lax.broadcasted_iota(jnp.int32, gates.shape, 1)
                branches = [branch_of(tile // LANE * t + j) for j in range(tile // LANE)]
                held = jnp.concatenate(
                    [
                        jnp.broadcast_to(
                            jnp.sum(jnp.where(lane == n, gates, 0.0), axis=1, keepdims=True),
                            (pair, LANE),
                        )
                        for n in branches
                    ],
                    axis=1,
                )
                squashed = jax.nn.sigmoid(gate)
                swished = gate * squashed
                value = swished * upward
                act[slot, :, low] = (value * held).astype(bf16)
                products = raw * value
                part = dots[pl.ds(first, 2)].reshape(pair, lanes)
                for j, n in enumerate(branches):
                    inner = jnp.sum(products[:, LANE * j : LANE * (j + 1)], axis=1, keepdims=True)
                    part = part + jnp.where(lane == n, inner, 0.0)
                dots[pl.ds(first, 2)] = part.reshape(2, rows, lanes)
                grad = raw * held
                grad_gu[slot, :, low] = (
                    grad * upward * squashed * (1.0 + gate * (1.0 - squashed))
                ).astype(bf16)
                grad_gu[slot, :, high] = (grad * swished).astype(bf16)
                return carry

            lax.fori_loop(0, hidden // tile, hidden_tile, 0)
            for copy in stored(slot, start):
                copy.start()

            def out_tile(t, carry):
                there = pl.ds(pl.multiple_of(1024 * t, 1024), 1024)
                for parts, left, right in (
                    (back_parts, grad_gu, lambda: in_held[there, :]),
                    (ffn_parts, act, lambda: down_held[pl.ds(8 * t, 8)].reshape(1024, hidden)),
                ):
                    made = contract_last(left[slot], right())
                    parts[pl.ds(first, 2), :, there] = made.astype(bf16).reshape(2, rows, 1024)
                return carry

            lax.fori_loop(0, width // 1024, out_tile, 0)

            def far():
                back.send_far()
                ahead.send_far()
                dot_copy(0, own[3]).start()
                dot_copy(1, other[3]).start()

            def near(side):
                back.send_near(side)
                back.pass_side(side)
                ahead.send_near(side)
                ahead.pass_side(side)
                dot_copy(2 + 2 * side, own[1 + side]).start()
                dot_copy(3 + 2 * side, other[1 + side]).start()

            pl.when(b == 0)(far)
            pl.when(b == 1)(lambda: near(0))
            pl.when(b == 2)(lambda: near(1))
            return carry

        lax.fori_loop(0, 4, block, 0)
        dot_copy(6, other[0]).start()
        for copy in stored(0, start_of(3)):
            copy.wait()
        act_load = pltpu.make_async_copy(act_out, act_held, loads.at[0])
        act_load.start()
        pl.semaphore_signal(free, inc=1, device_id=exchange.mate, device_id_type=MESH)
        pl.semaphore_wait(free, 1)
        act_load.wait()
        exchange.run(
            lambda step: grad_held[:, :, exchange.columns_at(step)].reshape(seq, 256),
            lambda start, count: down_held[CHIPS:, :, start : start + count].reshape(seq, count),
            turned,
            {
                2: [back.cross],
                3: [sums.send_far],
                5: [lambda: sums.send_near(0)],
                7: [lambda: sums.send_near(1)],
            },
        )
        out_load = pltpu.make_async_copy(out_weights, in_held.at[:, 0:width], loads.at[1])
        out_load.start()
        ahead.cross()
        sums.pass_side(0)
        sums.pass_side(1)
        back.ready()
        for k in range(7):
            ref = dots_in.at[k]
            remote(ref, ref, dot_sends, dot_arrivals, k, {"ctx": other[0]}).wait_recv()
        total_dots = dots[me]
        for k in range(7):
            total_dots = total_dots + dots_in[k]
        held = weights[pl.ds(pl.multiple_of(me * rows, rows), rows), :]
        lane = lax.broadcasted_iota(jnp.int32, held.shape, 1)
        routed = lane < EXPERTS
        centre = jnp.sum(jnp.where(routed, held * total_dots, 0.0), axis=-1, keepdims=True)
        both = jnp.where(
            routed,
            held * (total_dots - centre),
            jnp.where(lane == EXPERTS, total_dots * held * (1.0 - held), 0.0),
        )
        grad_logits[...] = lax.dot_general(
            both,
            second_held[me].astype(f32),
            (((0,), (0,)), ((), ())),
            precision=highest,
            preferred_element_type=f32,
        )[0:8]
        for t in range(width // 512):
            there = slice(512 * t, 512 * (t + 1))
            grad_residual[:, there] = jnp.dot(
                both, logit_low[:, there].astype(f32), precision=highest, preferred_element_type=f32
            )
        gain_sum[...] = jnp.zeros_like(gain_sum)

        def norm(there):
            normed, factor = normalize(residual[there, :])
            grad = back.total(there) + grad_residual[there, :]
            gain_sum[...] += grad * normed
            grad = norm_back(grad, normed, factor, gain)
            grad = grad + own_grad[there, :].astype(f32) * own_valid[there, :]
            grad_residual[there, :] = grad
            grad_low[there, :] = grad.astype(bf16)

        by_rows(rows, norm)
        grad_gain[...] = jnp.sum(gain_sum[...], axis=0, keepdims=True)
        out_load.wait()
        for t in range(width // 512):
            there = slice(512 * t, 512 * (t + 1))
            grad_mixed[:, there] = jnp.dot(
                grad_low[...], in_held[:, there], preferred_element_type=f32
            ).astype(bf16)
        ahead.ready()

        def finish(there):
            total = residual[there, :] + ahead.total(there)
            output[there, :] = (total * own_valid[there, :]).astype(bf16)

        by_rows(rows, finish)
        sums.cross()
        sums.ready()

        def keep(there):
            out_owned[there, :] = sums.total(there).astype(bf16)

        by_rows(128, keep)
        sums.end()
        back.end()
        ahead.end()
        for slot, place in enumerate((own[3], other[3], own[1], other[1], own[2], other[2], other[0])):
            dot_copy(slot, place).wait_send()

    return pl.pallas_call(
        kernel,
        out_shape=(
            jax.ShapeDtypeStruct((rows, width), f32),
            jax.ShapeDtypeStruct((rows, width), bf16),
            jax.ShapeDtypeStruct((rows, width), bf16),
            jax.ShapeDtypeStruct((rows, width), bf16),
            jax.ShapeDtypeStruct((1, width), f32),
            jax.ShapeDtypeStruct((8, width), f32),
            jax.ShapeDtypeStruct((N_CTX, rows, hidden), bf16),
            jax.ShapeDtypeStruct((seq, 2 * hidden), bf16),
            jax.ShapeDtypeStruct((128, hidden), bf16),
        ),
        in_specs=[ANY, ANY, VMEM] + [ANY] * 4 + [VMEM] * 4,
        out_specs=(VMEM,) * 6 + (ANY,) * 2 + (VMEM,),
        scratch_shapes=[
            pltpu.VMEM(second.shape, bf16),
            pltpu.VMEM(grad_out.shape, bf16),
            pltpu.VMEM((width, 2 * hidden), bf16),
            pltpu.VMEM((width // 128, 128, hidden), bf16),
            pltpu.VMEM((1, pair, hidden), bf16),
            pltpu.VMEM((1, pair, 2 * hidden), bf16),
            pltpu.VMEM((seq, lanes), f32),
            pltpu.VMEM((N_CTX, rows, lanes), f32),
            pltpu.VMEM((N_CTX - 1, rows, lanes), f32),
            pltpu.VMEM((16, width), f32),
            pltpu.VMEM((lanes, width), bf16),
            pltpu.VMEM(second.shape, bf16),
            pltpu.VMEM(second.shape, bf16),
            pltpu.SemaphoreType.DMA((N_CTX - 1,)),
            pltpu.SemaphoreType.DMA((N_CTX - 1,)),
            pltpu.SemaphoreType.DMA((3,)),
            pltpu.SemaphoreType.DMA((N_CTX,)),
            pltpu.SemaphoreType.DMA((3 * hidden // tile,)),
            pltpu.SemaphoreType.DMA((1, 3)),
        ]
        + Reduce.scratch(rows, width, 1) * 2
        + Exchange.scratch()
        + Reduce.scratch(128, hidden, 1)
        + [pltpu.SemaphoreType.REGULAR],
        compiler_params=params(2, 64 << 20),
        name="feed_forward",
    )(second, grad_out, assigned, w_gate, w_up, w_down.reshape(width // 128, 128, hidden), out_weights, small, residual, own_grad, own_valid)


class Share:
    @staticmethod
    def scratch(width, split=1):
        own = width // split
        return (
            [pltpu.VMEM((CHIPS, 128, width), jnp.bfloat16), pltpu.VMEM((128, own), jnp.bfloat16)]
            + Exchange.scratch()
            + Reduce.scratch(128, width, 1)
            + [pltpu.SemaphoreType.DMA((Both.SEMAPHORES,))] * 2
            + [pltpu.SemaphoreType.DMA]
        )

    COUNT = 2 + 2 + 5 + 2 + 1

    def __init__(self, staged, out, scratch):
        parts, self.owned = scratch[0:2]
        self.exchange = Exchange(parts, staged, *scratch[2:4])
        self.reduce = Reduce(parts, parts, *scratch[4:9], axis="shard")
        if out.shape[-1] > 2 * AFTER:
            self.gather = Both(self.owned, out, *scratch[9:11], AFTER)
        else:
            self.gather = Gather(self.owned, out, *scratch[9:11])
        self.local = scratch[11]

    def near(self, side):
        return lambda: self.reduce.send_near(side)

    def side(self, side):
        return lambda: self.reduce.pass_side(side)

    def ring(self, column):
        return lambda: self.gather.pass_ring(column)

    def own(self):
        self.sum_into(self.owned)
        self.pass_own()

    def sum_into(self, ref):
        self.reduce.ready()

        def keep(there):
            ref[there, :] = self.reduce.total(there).astype(jnp.bfloat16)

        by_rows(128, keep)

    def pass_own(self):
        self.gather.begin()
        self._kept().start()

    def _kept(self):
        return pltpu.make_async_copy(
            self.owned, self.gather.out.at[self.gather.me], self.local
        )

    def end(self):
        self._kept().wait()
        self.gather.end()
        self.reduce.end()


def backward(own, grad_mixed, mixed, out_own, second, grad_gu, qkv, weights, first, cosines, sines, key_pos, query_pos, inputs, grad_residual, gain, second_gain_grad, logits_grad):
    rows, width = own.shape
    seq = rows * N_CTX
    hidden = out_own.shape[1]
    heads_width = width // N_CTX
    heads = heads_width // HEAD
    n_shard = width // 128
    f32, bf16 = jnp.float32, jnp.bfloat16
    scale = HEAD ** (-0.5)
    tile = 256
    half = width // 2
    columns_grad = 3 * heads_width

    def kernel(
        own, grad_mixed, mixed, out_own, second, grad_gu, qkv, weights, first,
        cosines, sines, key_pos, query_pos, inputs, grad_residual, gain, second_gain_grad, logits_grad,
        input_grad, small_out, out_share, gate_share, up_share, mixed_share, qkv_share,
        grad_held, parts, left_held, gu_held, w_held, turned, staged, key_sum, value_sum, gain_sum,
        small, small_in, small_kept, small_across, mixed_in,
        loads, left_loads, grad_sends, grad_arrivals, mixed_sends, mixed_arrivals,
        small_sends, small_arrivals, across_sends, across_arrivals, *scratch,
    ):
        reduce = Reduce(parts, parts, *scratch[0:5])
        shares = []
        for k, out in enumerate((gate_share, up_share, mixed_share, qkv_share)):
            start = 8 + Share.COUNT * k
            shares.append(Share(staged, out, scratch[start : start + Share.COUNT]))
        b, c, d, e = shares
        gather = Both(out_own, out_share, *scratch[5:7], AFTER)
        local = scratch[7]
        me = reduce.places[0][0]
        shard = lax.axis_index("shard")
        owners = [lax.rem(shard + k, n_shard) for k in range(1, n_shard)]
        places = [lax.rem(me + k, N_CTX) for k in range(1, N_CTX)]

        def load(k, source, target):
            return pltpu.make_async_copy(source, target, loads.at[k])

        def columns_of(place):
            return pl.ds(pl.multiple_of(heads_width * place, heads_width), heads_width)

        def left_copy(source, step):
            slot = lax.rem(step, 2)
            return pltpu.make_async_copy(
                source.at[:, :, b.exchange.columns_at(step)], left_held.at[slot], left_loads.at[slot]
            )

        def streamed(source):
            left_copy(source, 0).start()

            def left(step):
                @pl.when(step < CHIPS - 1)
                def _():
                    left_copy(source, step + 1).start()

                left_copy(source, step).wait()
                return left_held[lax.rem(step, 2)].reshape(seq, 256)

            return left

        early = [load(1, grad_gu, gu_held), load(3, grad_residual, input_grad)]
        for copy in early:
            copy.start()
        left = streamed(second)
        greet([{"ctx": p} for p in places] + [{"shard": s} for s in owners])
        to_heads = [
            remote(
                grad_mixed.at[:, columns_of(p)], grad_held.at[me], grad_sends, grad_arrivals, k, {"ctx": p}
            )
            for k, p in enumerate(places)
        ]
        for copy in to_heads:
            copy.start()
        grad_held[me] = grad_mixed[:, columns_of(me)]
        gather.begin()
        kept = pltpu.make_async_copy(out_own, out_share.at[me], local)
        kept.start()
        late = [
            load(
                2 * k,
                weights.at[pl.ds(half * k, half), pl.ds(0, columns_grad)],
                w_held.at[:, columns_grad * k : columns_grad * (k + 1)],
            )
            for k in range(2)
        ]
        for copy in late:
            copy.start()
        early[0].wait()
        b.exchange.run(
            left,
            lambda start, count: gu_held[:, start : start + count],
            turned,
            {
                3: [b.reduce.send_far],
                4: [gather.pass_other],
                5: [b.near(0)],
                7: [b.near(1)],
            },
        )
        c.exchange.run(
            streamed(second),
            lambda start, count: gu_held[:, hidden + start : hidden + start + count],
            turned,
            {
                0: [lambda: gather.pass_ring(0)],
                1: [b.side(0)],
                2: [b.side(1)],
                3: [c.reduce.send_far],
                4: [lambda: gather.pass_ring(1)],
                5: [c.near(0)],
                7: [c.near(1)],
            },
        )
        late.append(load(1, qkv, gu_held.at[:, 0:columns_grad]))
        late[-1].start()
        small[...] = jnp.zeros_like(small)
        for s in range(n_shard):
            there = slice(128 * s, 128 * (s + 1))
            small[s, 1:2, :] = second_gain_grad[:, there]
            small[s, 2 : 3 + EXPERTS, :] = logits_grad[: EXPERTS + 1, there]
        for k, p in enumerate(places):
            place = lax.rem(me + N_CTX - 1 - k, N_CTX)
            ref = grad_held.at[place]
            remote(ref, ref, grad_sends, grad_arrivals, k, {"ctx": p}).wait_recv()
        for copy in late:
            copy.wait()
        events = {
            1: [b.reduce.cross],
            3: [c.side(0)],
            4: [c.side(1)],
            5: [b.own],
        }

        def attend(n, carry):
            head, i = n // (seq // tile), lax.rem(n, seq // tile)
            there = pl.ds(pl.multiple_of(i * tile, tile), tile)

            def lanes_of(start):
                return pl.ds(pl.multiple_of(start + HEAD * head, HEAD), HEAD)

            query = gu_held[there, lanes_of(0)]
            key = gu_held[:, lanes_of(heads_width)]
            value = gu_held[:, lanes_of(2 * heads_width)]
            grad = grad_held[pl.ds(2 * i, 2), :, lanes_of(0)].reshape(tile, HEAD)
            scores = contract_last(key, query) * scale
            scores = jnp.where(key_pos[...] <= query_pos[:, there], scores, -1e30)
            raised = jnp.exp(scores - jnp.max(scores, axis=0, keepdims=True))
            probs = raised * (1.0 / jnp.sum(raised, axis=0, keepdims=True))
            grad_probs = contract_last(value, grad)
            centre = jnp.sum(probs * grad_probs, axis=0, keepdims=True)
            grad_scores = (probs * (grad_probs - centre)).astype(bf16)

            @pl.when(i == 0)
            def _():
                key_sum[...] = jnp.zeros_like(key_sum)
                value_sum[...] = jnp.zeros_like(value_sum)

            key_sum[...] += jnp.dot(grad_scores, query, preferred_element_type=f32)
            value_sum[...] += jnp.dot(probs.astype(bf16), grad, preferred_element_type=f32)
            grad_query = contract_first(grad_scores, key) * scale

            def turn_back(values, cosines, sines):
                return (values * cosines - pltpu.roll(values, HEAD // 2, 1) * sines).astype(bf16)

            gu_held[there, lanes_of(columns_grad)] = turn_back(
                grad_query, cosines[there, :], sines[there, :]
            )

            @pl.when(i == seq // tile - 1)
            def _():
                gu_held[:, lanes_of(columns_grad + heads_width)] = turn_back(
                    key_sum[...] * scale, cosines[...], sines[...]
                )
                gu_held[:, lanes_of(columns_grad + 2 * heads_width)] = value_sum[...].astype(bf16)

            for at, todo in events.items():

                @pl.when(n == at)
                def _(todo=todo):
                    for event in todo:
                        event()

            return carry

        lax.fori_loop(0, heads * (seq // tile), attend, 0)

        def start_of(k):
            ahead = 2 - k + 3 * (k // 2) - 2 * (k // 3)
            return lax.rem(me // 2 + ahead, N_CTX // 2) * 2

        def grad_first(k, carry):
            block = start_of(k)
            left = gu_held[
                pl.ds(pl.multiple_of(block * rows, tile), tile), columns_grad : 2 * columns_grad
            ]
            for t in range(4):
                low, start = 512 * (t % 2), columns_grad * (t // 2)
                made = contract_last(left, w_held[low : low + 512, start : start + columns_grad])
                parts[pl.ds(block, 2), :, 512 * t : 512 * (t + 1)] = made.astype(bf16).reshape(
                    2, rows, 512
                )
            pl.when(k == 0)(reduce.send_far)
            pl.when(k == 1)(lambda: reduce.send_near(0))
            pl.when(k == 2)(lambda: reduce.send_near(1))
            return carry

        lax.fori_loop(0, 4, grad_first, 0)
        e.exchange.run(
            streamed(first),
            lambda start, count: gu_held[:, columns_grad + start : columns_grad + start + count],
            turned,
            {
                0: [c.reduce.cross],
                2: [b.gather.pass_other],
                3: [e.reduce.send_far],
                5: [e.near(0), b.ring(0)],
                7: [e.near(1), c.own],
            },
        )
        d.exchange.run(
            lambda step: own[:, b.exchange.columns_at(step)],
            lambda start, count: mixed[:, start : start + count],
            turned,
            {
                0: [lambda: reduce.pass_side(0)],
                1: [lambda: reduce.pass_side(1)],
                3: [d.reduce.send_far],
                4: [b.ring(1)],
                5: [d.near(0)],
                6: [e.side(0), e.side(1)],
                7: [d.near(1), reduce.cross],
            },
        )
        mixed_sum = staged.at[0, 0]
        own_inputs = staged.at[1, 0]
        inputs_load = load(1, inputs, own_inputs)
        inputs_load.start()
        bias = jnp.sum(
            gu_held[:, columns_grad : 2 * columns_grad].astype(f32), axis=0, keepdims=True
        )
        per = heads_width // 128
        for i in range(3):
            for j in range(per):
                block = n_shard * i + per * me + j
                there = slice(heads_width * i + 128 * j, heads_width * i + 128 * (j + 1))
                small[block // 3, pl.ds(3 + EXPERTS + lax.rem(block, 3), 1), :] = bias[:, there]
        e.reduce.cross()
        reduce.ready()
        early[1].wait()
        inputs_load.wait()
        gain_sum[...] = jnp.zeros_like(gain_sum)

        def norm(there):
            normed, factor = normalize(own_inputs[there, :].astype(f32))
            grad = reduce.total(there)
            gain_sum[...] += grad * normed
            input_grad[there, :] += norm_back(grad, normed, factor, gain[...])

        by_rows(rows, norm)
        first_gain_grad = jnp.sum(gain_sum[...], axis=0, keepdims=True)
        for s in range(n_shard):
            small[s, 0:1, :] = first_gain_grad[:, 128 * s : 128 * (s + 1)]
        to_owners = [
            remote(small.at[s], small_in.at[k], small_sends, small_arrivals, k, {"shard": s})
            for k, s in enumerate(owners)
        ]
        for copy in to_owners:
            copy.start()
        d.side(0)()
        d.side(1)()
        c.gather.pass_other()
        e.own()
        c.ring(0)()
        d.reduce.cross()
        e.gather.pass_other()
        total = small[shard]
        for k, copy in enumerate(to_owners):
            copy.wait_recv()
            total = total + small_in[k]
        small_kept[...] = total
        to_places = [
            remote(small_kept, small_across.at[k], across_sends, across_arrivals, k, {"ctx": p})
            for k, p in enumerate(places)
        ]
        for copy in to_places:
            copy.start()
        c.ring(1)()
        e.ring(0)()
        d.sum_into(mixed_sum)
        to_columns = [
            remote(
                mixed_sum.at[:, columns_of(p)], mixed_in.at[k], mixed_sends, mixed_arrivals, k, {"ctx": p}
            )
            for k, p in enumerate(places)
        ]
        for copy in to_columns:
            copy.start()
        e.ring(1)()
        for k, copy in enumerate(to_columns):
            copy.wait_recv()
        part = mixed_sum[:, columns_of(me)].astype(f32)
        for k in range(N_CTX - 1):
            part = part + mixed_in[k].astype(f32)
        d.owned[...] = part.astype(bf16)
        d.pass_own()
        for k, copy in enumerate(to_places):
            copy.wait_recv()
            total = total + small_across[k]
        small_out[...] = total
        d.gather.pass_other()
        d.ring(0)()
        d.ring(1)()
        for copy in to_heads + to_owners + to_places + to_columns:
            copy.wait_send()
        reduce.end()
        kept.wait()
        gather.end()
        for share in (b, c, e, d):
            share.end()

    def shared(count):
        return jax.ShapeDtypeStruct((N_CTX, 128, count), bf16)

    return pl.pallas_call(
        kernel,
        out_shape=(
            jax.ShapeDtypeStruct((rows, width), f32),
            jax.ShapeDtypeStruct((16, 128), f32),
            shared(hidden),
            shared(hidden),
            shared(hidden),
            shared(heads_width),
            shared(3 * heads_width),
        ),
        in_specs=[VMEM] * 4 + [ANY] * 5 + [VMEM] * 4 + [ANY] * 2 + [VMEM] * 3,
        out_specs=(VMEM, VMEM) + (ANY,) * 5,
        scratch_shapes=[
            pltpu.VMEM((N_CTX, rows, heads_width), bf16),
            pltpu.VMEM((N_CTX, rows, width), bf16),
            pltpu.VMEM((2, N_CTX, rows, 256), bf16),
            pltpu.VMEM(grad_gu.shape, bf16),
            pltpu.VMEM((half, 2 * columns_grad), bf16),
            pltpu.VMEM((256, seq), bf16),
            pltpu.VMEM((3, 2, 128, width), bf16),
            pltpu.VMEM((seq, HEAD), f32),
            pltpu.VMEM((seq, HEAD), f32),
            pltpu.VMEM((16, width), f32),
            pltpu.VMEM((n_shard, 16, 128), f32),
            pltpu.VMEM((n_shard - 1, 16, 128), f32),
            pltpu.VMEM((16, 128), f32),
            pltpu.VMEM((N_CTX - 1, 16, 128), f32),
            pltpu.VMEM((N_CTX - 1, 128, heads_width), bf16),
            pltpu.SemaphoreType.DMA((4,)),
            pltpu.SemaphoreType.DMA((2,)),
        ]
        + [pltpu.SemaphoreType.DMA((N_CTX - 1,))] * 4
        + [pltpu.SemaphoreType.DMA((n_shard - 1,))] * 2
        + [pltpu.SemaphoreType.DMA((N_CTX - 1,))] * 2
        + Reduce.scratch(rows, width, 1)
        + [pltpu.SemaphoreType.DMA((Both.SEMAPHORES,))] * 2
        + [pltpu.SemaphoreType.DMA]
        + Share.scratch(hidden) * 2
        + Share.scratch(width, N_CTX)
        + Share.scratch(3 * heads_width),
        compiler_params=params(3, 64 << 20),
        name="backward",
    )(own, grad_mixed, mixed, out_own, second, grad_gu, qkv, weights, first, cosines, sines, key_pos, query_pos, inputs, grad_residual, gain, second_gain_grad, logits_grad)


def local(
    tokens,
    cotangent,
    lengths,
    routes,
    block_order,
    norm_gains,
    qkv_weight,
    qkv_bias,
    out_weight,
    router,
    shared_gate,
    ffn_in,
    ffn_out,
):
    bf16, f32 = jnp.bfloat16, jnp.float32
    n_ctx = lax.axis_size("ctx")
    n_shard = lax.axis_size("shard")
    rows_dev = tokens.shape[1]
    seq_len = rows_dev * n_ctx
    n_blocks = block_order.shape[0]
    block = seq_len // n_blocks
    place = lax.axis_index("ctx")

    every = jnp.arange(seq_len, dtype=jnp.int32)
    matches = (every // block)[:, None] == jnp.arange(n_blocks, dtype=jnp.int32)[None, :]
    pos = jnp.sum(jnp.where(matches, block_order[None, :], 0), axis=1) * block + every % block
    valid = pos < lengths[0]
    valid_rows = valid.astype(f32)[:, None]

    own_valid = lax.dynamic_slice_in_dim(valid_rows, place * rows_dev, rows_dev)
    picks = routes[0][:, :, None] == jnp.arange(LANE, dtype=jnp.int32)[None, None, :]
    own_assigned = jnp.sum(picks.astype(f32), axis=1).astype(bf16)
    small = jnp.concatenate(
        [
            norm_gains,
            router.T,
            shared_gate.reshape(1, LANE),
            qkv_bias.reshape(3, LANE),
            jnp.zeros((4, LANE), bf16),
        ]
    )
    cosines, sines = rope_tables(pos)
    key_pos = jnp.where(valid, pos, 2 * seq_len)[:, None]
    (
        residual,
        second_all,
        g_all,
        attn_weights,
        out_weights,
        small_all,
        first_all,
        w_gate,
        w_up,
        w_down,
        qkv,
        mixed,
        assigned,
    ) = front(
        jnp.concatenate([tokens[0], own_assigned], axis=1),
        cotangent[0],
        own_valid,
        qkv_weight,
        out_weight,
        ffn_in,
        ffn_out,
        small,
        cosines,
        sines,
        key_pos,
        pos[None],
    )

    (
        grad_residual,
        grad_low,
        grad_mixed,
        output,
        grad_second_gain,
        grad_both,
        _,
        grad_gu,
        out_own,
    ) = feed_forward(
        second_all,
        g_all,
        assigned,
        w_gate.reshape(D, -1),
        w_up.reshape(D, -1),
        w_down.reshape(D, -1),
        out_weights.reshape(D, D),
        small_all,
        residual,
        cotangent[0],
        own_valid,
    )
    first_gain = small_all[:, 0, :].reshape(1, D).astype(f32)
    input_grad, own_small, out_share, gate_share, up_share, mixed_share, qkv_share = backward(
        grad_low,
        grad_mixed,
        mixed,
        out_own,
        second_all,
        grad_gu,
        qkv,
        attn_weights.reshape(D, -1),
        first_all,
        cosines,
        sines,
        key_pos,
        pos[None],
        tokens[0],
        grad_residual,
        first_gain,
        grad_second_gain,
        grad_both,
    )
    own_small = own_small.reshape(-1)
    grad_gains = own_small[: 2 * LANE].reshape(2, LANE)
    grad_router = own_small[2 * LANE : 8 * LANE].reshape(EXPERTS, LANE).T
    grad_shared_gate = own_small[8 * LANE : 9 * LANE]
    grad_bias_out = own_small[9 * LANE : 12 * LANE]

    grad_ffn_out, grad_ffn_in, grad_out, grad_qkv = assemble(
        out_share, gate_share, up_share, mixed_share, qkv_share
    )
    return (
        output[None],
        input_grad[None],
        grad_gains,
        grad_qkv,
        grad_bias_out,
        grad_out,
        grad_router,
        grad_shared_gate,
        grad_ffn_in,
        grad_ffn_out,
    )


def solution(mesh):
    placed = (
        P("shard", "ctx", None),
        P("shard", "ctx", None),
        P("shard"),
        P("shard", "ctx", None),
        P(),
        P(None, "shard"),
        P("shard", None),
        P("shard"),
        P("shard", None),
        P("shard", None),
        P("shard"),
        P("shard", None),
        P("shard", None),
    )
    return jax.shard_map(
        local,
        mesh=mesh,
        in_specs=placed,
        out_specs=(
            P("shard", "ctx", None),
            P("shard", "ctx", None),
            P(None, "shard"),
            P("shard", None),
            P("shard"),
            P("shard", None),
            P("shard", None),
            P("shard"),
            P("shard", None),
            P("shard", None),
        ),
        check_vma=False,
    )
```
